256 devices in a mesh: pts: 32 (over x, y, core), row: 8 (over z).
Axes of the slice: x: 4, y: 4, z: 8, core: 2. Of those that a mesh axis runs over, the one named last changes fastest.
Arguments:
- g_jets: bfloat16 [96, 9, 8192], P(None, None, 'pts'), may hold values from -6 to 6
- layer_input_jets: bfloat16 [9, 128, 8192], P(None, None, 'pts'), may hold values from -5 to 5
- speed: bfloat16 [8192], P('pts'), may hold values from 0.5 to 2
- resid: bfloat16 [8192], P('pts'), may hold values from -6 to 6
- point_index: int32 [4096], P('pts'), may hold values from 0 to 255
- damping: float32 [12, 8, 128], P(None, 'row'), may hold values from 0.5 to 4
- panel: int32 [1], replicated, may hold values from 0 to 47
Outputs:
- factor: float32 [12, 8, 128, 3, 32, 128], P(None, 'row', None, None, 'pts')
- direction: float32 [12288], replicated
The draws below stay inside these ranges and needn't reach their ends.
All inputs are finite; a program needn't handle non-finite values.
Results may differ from the reference program's by a relative error of at most 0.0036.
Values may be sent and summed in bfloat16 or wider, within the bound.
No kernel may reach another device: no remote copies, remote signals or barrier semaphores. Data moves between devices by JAX's collectives and lax.ppermute only.
A program may use at most 192 MiB of HBM per device.

```python
import math
import jax
import jax.numpy as jnp
from jax import lax

A = 96
K = 128
C = 9
R_DEV = 128
POOL = 256
NPTS = 4096
NPOOL = 8192
LR = 12
LC = 3
N_PTS = 32
N_ROW = 8


def with_ends(result, rng, smallest, top_value):
    index_at = [jax.random.randint(jax.random.fold_in(rng, axis), (), 0, length) for axis, length in enumerate(result.shape)]
    main_axis = result.shape.index(max(result.shape))
    next_to = index_at[:main_axis] + [(index_at[main_axis] + 1) % result.shape[main_axis]] + index_at[main_axis + 1:]
    return result.at[tuple(index_at)].set(smallest).at[tuple(next_to)].set(top_value)


def block_levels(stream_key, shape, cuts, low, top_value):
    loudness = 1.0
    for axis_at, shards_of in cuts:
        heights = jax.random.uniform(jax.random.fold_in(jax.random.fold_in(stream_key, 6), axis_at), (shards_of,), jnp.float32, low / len(cuts), top_value / len(cuts))
        loudness = loudness * jnp.repeat(jnp.exp(heights), shape[axis_at] // shards_of).reshape((-1,) + (1,) * (len(shape) - 1 - axis_at))
    return loudness


def normal_values(rng, shape, scale, reach, pieces=(), held_as=jnp.bfloat16):
    loudness = block_levels(rng, shape, pieces, -0.22, 0.18) if pieces else 1.0
    result = jax.random.normal(rng, shape, jnp.float32) * scale * loudness
    return jnp.minimum(jnp.maximum(result, -reach), reach).astype(held_as)


def setup_inputs(seed: int = 0) -> dict:
    key_of = jax.random.split(jax.random.key(seed), 8)
    g_jets = normal_values(key_of[0], (A, C, NPOOL), 1.0, 6.0, ((2, 32),))
    layer_input_jets = normal_values(key_of[1], (C, K, NPOOL), 0.35, 5.0, ((2, 32),))
    speed = jnp.clip(jnp.exp(math.log(2.0) - 1.3862944 * jax.random.uniform(key_of[2], (NPOOL,), jnp.float32) ** block_levels(key_of[2], (NPOOL,), ((0, 32),), -0.2, 0.2)), 0.5, 2.0).astype(jnp.bfloat16)
    resid = normal_values(key_of[3], (NPOOL,), 1.0, 6.0, ((0, 32),))
    point_index = with_ends(jax.random.randint(key_of[4], (NPTS,), 0, POOL), jax.random.fold_in(key_of[4], 1), 0, POOL - 1).astype(jnp.int32)
    damping = jnp.clip(jnp.exp(math.log(4.0) - 2.0794415 * jax.random.uniform(key_of[5], (LR, N_ROW, K), jnp.float32) ** block_levels(key_of[5], (LR, N_ROW, K), ((1, 8),), -0.2, 0.2)), 0.5, 4.0)
    panel = jax.random.randint(key_of[6], (1,), 0, A // 2).astype(jnp.int32)
    return {"g_jets": g_jets, "layer_input_jets": layer_input_jets, "speed": speed, "resid": resid, "point_index": point_index, "damping": damping, "panel": panel}


def weights_of(vel):
    base = jnp.array([1.0, 2.0, 1.0], jnp.float32)
    ones = jnp.ones_like(vel)
    time_part = base[:, None] * ones[None, :]
    space_part = -base[:, None] * vel[None, :]
    return jnp.concatenate([time_part, space_part, space_part], 0)

def reference(g_jets, layer_input_jets, speed, resid, point_index, damping, panel):
    shard = (jnp.arange(NPTS) // R_DEV).astype(jnp.int32)
    chosen = (shard * POOL + point_index).astype(jnp.int32)
    gsel = jnp.take(g_jets, chosen, axis=2).astype(jnp.float32)
    hidden_selected = jnp.take(layer_input_jets, chosen, axis=2).astype(jnp.float32)
    vel = jnp.take(speed, chosen).astype(jnp.float32)
    res = jnp.take(resid, chosen)
    wts = weights_of(vel)
    mixed_derivative = gsel * wts[None]
    jacobian_matrix = jnp.einsum('fjz,jvz->zfv', mixed_derivative, hidden_selected, precision=lax.Precision.HIGHEST)
    jacobian_matrix = jacobian_matrix.reshape(NPTS, A * K).astype(jnp.bfloat16)
    gram = jnp.dot(jacobian_matrix.T.astype(jnp.float32), jacobian_matrix.astype(jnp.float32), preferred_element_type=jnp.float32) / NPTS
    gram = gram + jnp.diag(damping.reshape(-1))
    grad = jnp.dot(res.astype(jnp.float32), jacobian_matrix.astype(jnp.float32), preferred_element_type=jnp.float32) / NPTS
    at = panel[0]
    gram4 = gram.reshape(A, K, A, K)
    grad2 = grad.reshape(A, K)
    column = lax.dynamic_index_in_dim(gram4, at, 2, keepdims=False)
    dtile = lax.dynamic_index_in_dim(column, at, 0, keepdims=False)
    chol = jnp.linalg.cholesky(dtile)
    gk = lax.dynamic_index_in_dim(grad2, at, 0, keepdims=False)
    ysol = jax.scipy.linalg.solve_triangular(chol, gk, lower=True)
    lpan = jax.scipy.linalg.solve_triangular(chol, column.reshape(A * K, K).T, lower=True).T.reshape(A, K, K)
    blocks = jnp.arange(A)
    later = blocks > at
    same = blocks == at
    update = jnp.einsum('ibc,jdc->ibjd', lpan, lpan, precision=lax.Precision.HIGHEST)
    trail = (later[:, None] & later[None, :])[:, None, :, None]
    pcol = (later[:, None] & same[None, :])[:, None, :, None]
    pdiag = (same[:, None] & same[None, :])[:, None, :, None]
    factor = jnp.where(trail, gram4 - update, jnp.where(pcol, lpan[:, :, None, :], jnp.where(pdiag, chol[None, :, None, :], gram4)))
    factor = factor.reshape(LR, N_ROW, K, LC, N_PTS, K)
    proj = jnp.einsum('ibc,c->ib', lpan, ysol, precision=lax.Precision.HIGHEST)
    direction = jnp.where(later[:, None], grad2 - proj, jnp.where(same[:, None], ysol[None, :], grad2))
    return (factor, direction.reshape(-1))
```

```python
import jax
import jax.numpy as jnp
from jax import lax
from jax.experimental import pallas as pl
from jax.experimental.pallas import tpu as pltpu
from jax.sharding import Mesh, PartitionSpec as P

NX, NY, NC, NZ = 4, 4, 2, 8
A, K, C, POOL, M = 96, 128, 9, 256, 128
LR, LC = 12, 3
TOTAL = 4096
HR = C * K
BR = 1280
ROWG, KG, VR, RR = HR, HR + 108, HR + 117, HR + 118
GC = 64
RU, CU = LR * K, LC * K
JR = RU + 2 * CU + 2 * K
J_K, J_R = RU + 2 * CU, RU + 2 * CU + K
F32, BF16 = jnp.float32, jnp.bfloat16
AXES = ("x", "y", "core", "row")
HI = lax.Precision.HIGHEST
NT = (((1,), (1,)), ((), ()))
TN = (((0,), (0,)), ((), ()))
VMEM_LIMIT = 56 * 1024 * 1024
SMEM = pl.BlockSpec(memory_space=pltpu.SMEM)
VM = pl.BlockSpec(memory_space=pltpu.VMEM)


def params():
    return pltpu.CompilerParams(vmem_limit_bytes=VMEM_LIMIT)


def pack_kernel(s_ref, idx_ref, h_ref, g_ref, v_ref, r_ref, blk_ref, col_ref, gs, tail, cbuf):
    q, core, k = s_ref[0], s_ref[1], s_ref[2]
    pool = lax.broadcasted_iota(jnp.int32, (POOL, M), 0)
    sel = (pool == idx_ref[...]).astype(F32).astype(BF16)
    for c in range(C):
        blk_ref[c * K : (c + 1) * K, :] = jnp.dot(
            h_ref[c * K : (c + 1) * K, :], sel, preferred_element_type=F32
        ).astype(BF16)
    for c in range(C):
        gs[c * A : (c + 1) * A, :] = jnp.dot(
            g_ref[c * A : (c + 1) * A, :], sel, preferred_element_type=F32
        )
    tail[...] = jnp.zeros_like(tail)
    for c in range(C):
        tail[c * LR : (c + 1) * LR, :] = gs[pl.ds(c * A + q, LR, stride=NZ), :]
        tail[108 + c : 109 + c, :] = gs[pl.ds(c * A + k, 1), :]
    tail[117:118, :] = jnp.dot(v_ref[...], sel, preferred_element_type=F32)
    tail[118:119, :] = jnp.dot(r_ref[...], sel, preferred_element_type=F32)
    blk_ref[HR:BR, :] = tail[...].astype(BF16)
    cbuf[...] = jnp.zeros_like(cbuf)
    for d in range(NX * NY):
        for c in range(C):
            for o in range(2):
                cc = core if o == 0 else 1 - core
                for lc in range(LC):
                    cbuf[c * 6 + o * LC + lc : c * 6 + o * LC + lc + 1, :] = gs[
                        pl.ds(c * A + lc * 32 + 2 * d + cc, 1), :
                    ]
        col_ref[d] = cbuf[...].astype(BF16)


def pack(scal, idx, h, g, v, r):
    return pl.pallas_call(
        pack_kernel,
        out_shape=(
            jax.ShapeDtypeStruct((BR, M), BF16),
            jax.ShapeDtypeStruct((NX * NY, GC, M), BF16),
        ),
        in_specs=[SMEM, VM, VM, VM, VM, VM],
        out_specs=(VM, VM),
        scratch_shapes=[
            pltpu.VMEM((C * A, M), F32),
            pltpu.VMEM((128, M), F32),
            pltpu.VMEM((GC, M), F32),
        ],
        compiler_params=params(),
        name="pack",
    )(scal, idx, h, g, v, r)


def coefs(rows, per, v):
    row = lax.broadcasted_iota(jnp.int32, (rows, M), 0)
    c = jnp.zeros((rows, M), jnp.int32)
    for i in range(1, C):
        c = c + (row >= per * i).astype(jnp.int32)
    base = jnp.where((c == 1) | (c == 4) | (c == 7), 2.0, 1.0)
    return jnp.where(c < 3, base, -base * v)


def chunk_kernel(first, s_ref, a_ref, b_ref, gc_ref, *refs):
    if first:
        outs, (jac, wg) = refs[:5], refs[5:]
        ins = None
    else:
        ins, outs, (jac, wg) = refs[:5], refs[5:10], refs[10:]
    for blk in range(4):
        src = a_ref if blk < 2 else b_ref
        off = (blk % 2) * BR
        tail = src[off + HR : off + BR, :].astype(F32)
        v = tail[117:118, :]
        lanes = slice(blk * M, (blk + 1) * M)
        wg[blk, 0:108, :] = tail[0:108, :] * coefs(108, LR, v)
        wg[blk, 176:185, :] = tail[108:117, :] * coefs(C, 1, v)
        gc = gc_ref[s_ref[blk]].astype(F32)
        wg[blk, 112:176, :] = gc * coefs(GC, 6, v)
        jac[J_R:JR, lanes] = jnp.zeros((JR - J_R, M), BF16)
        first_row = lax.broadcasted_iota(jnp.int32, (16, M), 0) == 0
        jac[J_R : J_R + 16, lanes] = jnp.where(first_row, tail[118:119, :], 0.0).astype(BF16)

    for blk in range(4):
        src = a_ref if blk < 2 else b_ref
        off = (blk % 2) * BR
        lanes = slice(blk * M, (blk + 1) * M)

        def slab(t, carry, src=src, off=off, lanes=lanes, blk=blk):
            base = pl.multiple_of(t * 16, 16)
            h = [src[pl.ds(off + c * K + base, 16), :].astype(F32) for c in range(C)]

            def unit(rows, dst):
                acc = wg[blk, rows[0] : rows[0] + 1, :] * h[0]
                for c in range(1, C):
                    acc = acc + wg[blk, rows[c] : rows[c] + 1, :] * h[c]
                jac[pl.ds(dst + base, 16), lanes] = acc.astype(BF16)

            for u in range(LR):
                unit([c * LR + u for c in range(C)], u * K)
            for u in range(6):
                unit([112 + c * 6 + u for c in range(C)], RU + u * K)
            unit([176 + c for c in range(C)], J_K)
            return carry

        lax.fori_loop(0, K // 16, slab, 0)

    def acc(i, rows, cols, val):
        if ins is not None:
            val = val + ins[i][rows, cols]
        outs[i][rows, cols] = val

    pd = lax.dot_general(jac[RU : J_R + 16, :], jac[J_K:J_R, :], NT, preferred_element_type=F32)
    al = slice(None)
    acc(2, al, al, pd[0:CU])
    acc(3, al, al, pd[CU : 2 * CU])
    acc(4, al, al, pd[2 * CU :])
    tile = 512
    for n in range(4):
        for m in range(RU // tile):
            rows = slice(m * tile, (m + 1) * tile)
            val = lax.dot_general(
                jac[rows, :], jac[RU + n * 256 : RU + (n + 1) * 256, :], NT,
                preferred_element_type=F32,
            )
            if n == 0:
                acc(0, rows, slice(0, 256), val)
            elif n == 1:
                acc(0, rows, slice(256, 384), val[:, :128])
                acc(1, rows, slice(0, 128), val[:, 128:])
            else:
                acc(1, rows, slice(n * 256 - 384, n * 256 - 128), val)


def chunk(first, idx, a, b, gcol, accs):
    shapes = tuple(
        jax.ShapeDtypeStruct(s, F32)
        for s in ((RU, CU), (RU, CU + 2 * K), (CU, K), (CU, K), (K + 16, K))
    )
    return pl.pallas_call(
        lambda *r: chunk_kernel(first, *r),
        out_shape=shapes,
        in_specs=[SMEM, VM, VM, VM] + [VM] * len(accs),
        out_specs=(VM,) * 5,
        scratch_shapes=[pltpu.VMEM((JR, 4 * M), BF16), pltpu.VMEM((4, 192, M), F32)],
        input_output_aliases={} if first else {4 + i: i for i in range(5)},
        compiler_params=params(),
        name="chunk_first" if first else "chunk",
    )(idx, a, b, gcol, *accs)


def chol_kernel(a_ref, b_ref, d_ref, chol_ref, w_ref, yz_ref, m_ref, u_ref):
    row = lax.broadcasted_iota(jnp.int32, (K, K), 0)
    col = lax.broadcasted_iota(jnp.int32, (K, K), 1)
    eye = row == col
    gram = (a_ref[0:K, :] + b_ref[0:K, :]) * (1.0 / TOTAL)
    m_ref[:, :K] = gram + jnp.where(eye, d_ref[0:1, :], 0.0)
    m_ref[:, K:] = jnp.where(eye, 1.0, 0.0)
    sub = lax.broadcasted_iota(jnp.int32, (8, 2 * K), 0)
    for b in range(K // 8):
        p = m_ref[8 * b : 8 * b + 8, :]
        for r in range(8):
            j = 8 * b + r
            cb = p[:, j : j + 1]
            rs = lax.rsqrt(p[r : r + 1, j : j + 1])
            urow = p[r : r + 1, :] * rs
            p = jnp.where(sub > r, p - (cb * rs) * urow, jnp.where(sub == r, urow, p))
        u_ref[8 * b : 8 * b + 8, :] = p
        if b < K // 8 - 1:
            upd = lax.dot_general(p[:, :K], p, TN, precision=HI, preferred_element_type=F32)
            lo = 8 * (b + 1)
            m_ref[lo:, :] = m_ref[lo:, :] - upd[lo:, :]
    chol_ref[...] = jnp.where(col >= row, u_ref[:, :K], 0.0).T
    w = u_ref[:, K:]
    w_ref[...] = w
    g = (a_ref[K : K + 8, :] + b_ref[K : K + 8, :]) * (1.0 / TOTAL)
    y = lax.dot_general(g, w, NT, precision=HI, preferred_element_type=F32)
    z = lax.dot_general(y, w, (((1,), (0,)), ((), ())), precision=HI, preferred_element_type=F32)
    yz_ref[0:8, :] = y
    yz_ref[8:16, :] = z


def cholesky(dk, dk2, damp):
    return pl.pallas_call(
        chol_kernel,
        out_shape=(
            jax.ShapeDtypeStruct((K, K), F32),
            jax.ShapeDtypeStruct((K, K), F32),
            jax.ShapeDtypeStruct((16, K), F32),
        ),
        in_specs=[VM] * 3,
        out_specs=(VM,) * 3,
        scratch_shapes=[pltpu.VMEM((K, 2 * K), F32), pltpu.VMEM((K, 2 * K), F32)],
        compiler_params=params(),
        name="panel_factor",
    )(dk, dk2, damp)


def final_kernel(
    s_ref, g_ref, xp_ref, xr_ref, po_ref, pr_ref, chol_ref, w_ref, yz_ref, damp_ref,
    out_ref, dir_ref, lpc,
):
    q, s, k = s_ref[0], s_ref[1], s_ref[2]
    lr = pl.program_id(0)
    inv = 1.0 / TOTAL

    @pl.when(lr == 0)
    def _():
        pc = (po_ref[...] + pr_ref[...]) * inv
        lpc[...] = lax.dot_general(pc, w_ref[...], NT, precision=HI, preferred_element_type=F32)

    i = lr * NZ + q
    pe = (xp_ref[:, CU:] + xr_ref[:, CU:]) * inv
    lpan = lax.dot_general(pe[:, :K], w_ref[...], NT, precision=HI, preferred_element_type=F32)
    upd = lax.dot_general(lpan, lpc[...], NT, precision=HI, preferred_element_type=F32)
    gram = (g_ref[...] + xr_ref[:, :CU]) * inv
    row = lax.broadcasted_iota(jnp.int32, (K, K), 0)
    col = lax.broadcasted_iota(jnp.int32, (K, K), 1)
    eye = row == col
    damp = damp_ref[pl.ds(lr, 1), :]
    for lc in range(LC):
        j = lc * (NX * NY * NC) + s
        gt = gram[:, lc * K : (lc + 1) * K] + jnp.where(eye & (i == j), damp, 0.0)
        later_row = i > k
        val = jnp.where(
            later_row & (j > k),
            gt - upd[:, lc * K : (lc + 1) * K],
            jnp.where(
                later_row & (j == k),
                lpan,
                jnp.where((i == k) & (j == k), chol_ref[...], gt),
            ),
        )
        out_ref[pl.ds(lc, K, stride=LC), :] = val
    sub = lax.broadcasted_iota(jnp.int32, (8, 2 * K), 0)
    lane = lax.broadcasted_iota(jnp.int32, (8, 2 * K), 1)
    z = yz_ref[8:9, :]
    z2 = jnp.concatenate([z, jnp.zeros_like(z)], axis=1)
    lhs = jnp.where(lane == K, 1.0, jnp.where((sub == 0) & (i > k), -z2, 0.0))
    d = lax.dot_general(lhs, pe, NT, precision=HI, preferred_element_type=F32)
    dir_ref[pl.ds(lr, 1), :] = jnp.where(i == k, yz_ref[0:1, :], d[0:1, :])


def final(scal, gown, xown, xrecv, po, pr, chol, w, yz, damp):
    full = lambda shape: pl.BlockSpec(shape, lambda i: (0,) * len(shape))
    return pl.pallas_call(
        final_kernel,
        grid=(LR,),
        out_shape=(
            jax.ShapeDtypeStruct((RU * LC, K), F32),
            jax.ShapeDtypeStruct((LR, K), F32),
        ),
        in_specs=[
            SMEM,
            pl.BlockSpec((K, CU), lambda i: (i, 0)),
            pl.BlockSpec((K, CU + 2 * K), lambda i: (i, 0)),
            pl.BlockSpec((K, CU + 2 * K), lambda i: (i, 0)),
            full((CU, K)),
            full((CU, K)),
            full((K, K)),
            full((K, K)),
            full((16, K)),
            full((LR, K)),
        ],
        out_specs=(pl.BlockSpec((K * LC, K), lambda i: (i, 0)), full((LR, K))),
        scratch_shapes=[pltpu.VMEM((CU, K), F32)],
        compiler_params=params(),
        name="trailing_update",
    )(scal, gown, xown, xrecv, po, pr, chol, w, yz, damp)


def device(x, y, c, z):
    return ((x * NY + y) * NC + c) * NZ + z


def hops(along_x_core, d):
    pairs = []
    for x in range(NX):
        for y in range(NY):
            for c in range(NC):
                for z in range(NZ):
                    to = ((x + d) % NX, y) if c == along_x_core else (x, (y + d) % NY)
                    pairs.append((device(x, y, c, z), device(*to, c, z)))
    return pairs


def body(g_jets, layer_input_jets, speed, resid, point_index, damping, panel):
    x, y = lax.axis_index("x"), lax.axis_index("y")
    core, q = lax.axis_index("core"), lax.axis_index("row")
    k = panel[0]
    s = (x * NY + y) * NC + core
    one = lambda v, d: lax.ppermute(v, AXES, hops(0, d))
    two = lambda v, d: lax.ppermute(v, AXES, hops(1, d))
    swap = lambda v: lax.ppermute(v, "core", [(0, 1), (1, 0)])

    block, gcol = pack(
        jnp.stack([q, core, k]).astype(jnp.int32),
        point_index.reshape(1, M),
        layer_input_jets.reshape(HR, POOL),
        g_jets.transpose(1, 0, 2).reshape(C * A, POOL),
        speed.reshape(1, POOL),
        resid.reshape(1, POOL),
    )
    a1, a2 = one(block, 1), one(block, -1)
    gcol = lax.all_to_all(gcol, ("x", "y"), split_axis=0, concat_axis=0, tiled=True)
    half = BR // 2
    r1, r2 = one(a1[:half], 1), one(a2[half:], -1)
    ba = jnp.concatenate([block, a1])
    bb = jnp.concatenate([a2, r1, r2])
    ma, mb = two(ba, 1), two(bb, -1)
    ba, bb, ma, mb = lax.optimization_barrier((ba, bb, ma, mb))
    na, nb = two(bb, 1), two(ba, -1)
    ra, rb = two(ma, 1), two(mb, -1)

    def sources(first, second):
        out = []
        for d1, d2 in first + second:
            sx = jnp.where(core == 0, x + d1, x + d2) % NX
            sy = jnp.where(core == 0, y + d2, y + d1) % NY
            out.append(sx * NY + sy)
        return jnp.stack(out).astype(jnp.int32)

    low, high = (0, -1), (1, 2)
    pair = lambda ds, d2: [(d, d2) for d in ds]
    accs = chunk(True, sources(pair(low, 0), pair(high, 0)), ba, bb, gcol, ())
    accs = chunk(False, sources(pair(low, -1), pair(high, 1)), ma, mb, gcol, accs)
    accs = chunk(False, sources(pair(high, -1), pair(low, 1)), na, nb, gcol, accs)
    accs = chunk(False, sources(pair(low, 2), pair(high, 2)), ra, rb, gcol, accs)
    gown, xs, po, ps, dk = accs

    dsel = lax.dynamic_index_in_dim(damping[:, 0, :], k // NZ, 0, keepdims=True)
    dsel = jnp.broadcast_to(jnp.where(k % NZ == q, dsel, 0.0), (8, K))
    for bit in (1, 2, 4):
        dsel = dsel + lax.ppermute(dsel, "row", [(i, i ^ bit) for i in range(NZ)])

    dk2 = swap(dk)
    xr = swap(xs)
    pr = swap(ps)
    chol, w, yz = cholesky(dk, dk2, dsel)
    scal = jnp.stack([q, s, k]).astype(jnp.int32)
    fac, mine = final(scal, gown, xs, xr, po, pr, chol, w, yz, damping[:, 0, :])
    slot = lax.broadcasted_iota(jnp.int32, (1, NZ, 1), 1)
    full = jnp.where(slot == q, mine[:, None, :], 0.0)
    for bit in (1, 2, 4):
        full = full + lax.ppermute(full, "row", [(i, i ^ bit) for i in range(NZ)])
    return fac.reshape(LR, 1, K, LC, 1, K), full.reshape(-1)


def solution(mesh):
    grid = Mesh(mesh.devices.reshape(NX, NY, NC, NZ), AXES)
    pts = ("x", "y", "core")
    in_specs = (
        P(None, None, pts),
        P(None, None, pts),
        P(pts),
        P(pts),
        P(pts),
        P(None, "row", None),
        P(),
    )
    out_specs = (P(None, "row", None, None, pts, None), P())
    return jax.shard_map(body, mesh=grid, in_specs=in_specs, out_specs=out_specs, check_vma=False)
```

```python
import jax
import jax.numpy as jnp
from jax import lax
from jax.experimental import pallas as pl
from jax.experimental.pallas import tpu as pltpu
from jax.sharding import Mesh, PartitionSpec as P

NX, NY, NC, NZ = 4, 4, 2, 8
A, K, C, POOL, M = 96, 128, 9, 256, 128
LR, LC = 12, 3
TOTAL = 4096
HR = C * K
BR = 1280
ROWG, KG, VR, RR = HR, HR + 108, HR + 117, HR + 118
GC = 64
HB = BR // 2
PR = BR + 6 * GC
MR = 2 * BR + 3 * GC
RU, CU = LR * K, LC * K
JR = RU + 2 * CU + 2 * K
J_K, J_R = RU + 2 * CU, RU + 2 * CU + K
F32, BF16 = jnp.float32, jnp.bfloat16
AXES = ("x", "y", "core", "row")
HI = lax.Precision.HIGHEST
NT = (((1,), (1,)), ((), ()))
TN = (((0,), (0,)), ((), ()))
VMEM_LIMIT = 20 * 1024 * 1024
SMEM = pl.BlockSpec(memory_space=pltpu.SMEM)
VM = pl.BlockSpec(memory_space=pltpu.VMEM)
ANY = pl.BlockSpec(memory_space=pl.ANY)


def params():
    return pltpu.CompilerParams(vmem_limit_bytes=VMEM_LIMIT)


def pack_kernel(k_ref, idx_ref, h_ref, g_ref, vr_ref, plus_ref, minus_ref, own_ref, gs, tail, cbuf):
    x, y = lax.axis_index("x"), lax.axis_index("y")
    core, q = lax.axis_index("core"), lax.axis_index("row")
    k = k_ref[0]
    pool = lax.broadcasted_iota(jnp.int32, (POOL, M), 0)
    sel = (pool == idx_ref[...]).astype(F32).astype(BF16)
    for c in range(C):
        val = jnp.dot(h_ref[c * K : (c + 1) * K, :], sel, preferred_element_type=F32).astype(BF16)
        lo = c * K if c < 5 else c * K + 2 * GC
        plus_ref[lo : lo + K, :] = val
        lo = c * K + HB + 2 * GC if c < 5 else c * K - HB
        minus_ref[lo : lo + K, :] = val
    for c in range(C):
        gs[c * A : (c + 1) * A, :] = jnp.dot(
            g_ref[c * A : (c + 1) * A, :], sel, preferred_element_type=F32
        )
    tail[...] = jnp.zeros_like(tail)
    for c in range(C):
        tail[c * LR : (c + 1) * LR, :] = gs[pl.ds(c * A + q, LR, stride=NZ), :]
        tail[108 + c : 109 + c, :] = gs[pl.ds(c * A + k, 1), :]
    tail[117:119, :] = jnp.dot(vr_ref[...], sel, preferred_element_type=F32)
    val = tail[...].astype(BF16)
    plus_ref[HR + 2 * GC : BR + 2 * GC, :] = val
    minus_ref[HR - HB : HB, :] = val
    cbuf[...] = jnp.zeros_like(cbuf)
    for dp in range(4):
        for dt in range(4):
            px = lax.rem(jnp.where(core == 0, x + dp, x + dt), NX)
            py = lax.rem(jnp.where(core == 0, y + dt, y + dp), NY)
            d = px * NY + py
            for c in range(C):
                for o in range(2):
                    cc = core if o == 0 else 1 - core
                    for lc in range(LC):
                        row = c * 6 + o * LC + lc
                        cbuf[row : row + 1, :] = gs[pl.ds(c * A + lc * 32 + 2 * d + cc, 1), :]
            val = cbuf[...].astype(BF16)
            if dp == 0:
                own_ref[dt * GC : (dt + 1) * GC, :] = val
            elif dp == 1:
                plus_ref[BR + (2 + dt) * GC : BR + (3 + dt) * GC, :] = val
            elif dp == 3:
                minus_ref[BR + (2 + dt) * GC : BR + (3 + dt) * GC, :] = val
            elif dt < 2:
                plus_ref[HB + dt * GC : HB + (dt + 1) * GC, :] = val
            else:
                minus_ref[HB + (dt - 2) * GC : HB + (dt - 1) * GC, :] = val


def pack(k, idx, h, g, vr):
    return pl.pallas_call(
        pack_kernel,
        out_shape=(
            jax.ShapeDtypeStruct((PR, M), BF16),
            jax.ShapeDtypeStruct((PR, M), BF16),
            jax.ShapeDtypeStruct((4 * GC, M), BF16),
        ),
        in_specs=[SMEM, VM, VM, VM, VM],
        out_specs=(VM,) * 3,
        scratch_shapes=[
            pltpu.VMEM((C * A, M), F32),
            pltpu.VMEM((128, M), F32),
            pltpu.VMEM((GC, M), F32),
        ],
        compiler_params=params(),
        name="pack",
    )(k, idx, h, g, vr)


def block_from_plus(i, cols):
    return ([(i, 0, HB), (i, HB + 2 * GC, HB)], cols)


def block_from_minus(i, cols):
    return ([(i, HB + 2 * GC, HB), (i, 0, HB)], cols)


def after(i, lo):
    return [(i, lo + e * GC) for e in range(4)]


BLOCK0 = block_from_plus(0, after(1, 0))
BLOCK1 = block_from_plus(2, after(2, BR + 2 * GC))
BLOCK2 = block_from_minus(0, after(0, BR + 2 * GC))
BLOCK3 = (
    [(1, 0, HB), (2, 0, HB)],
    [(1, HB), (1, HB + GC), (2, HB), (2, HB + GC)],
)


def message(first, second, e):
    out, at = [], 0
    for i, lo, n in first[0]:
        out.append((i, lo, n, at))
        at += n
    out.append((*first[1][2], GC, at))
    at += GC
    for i, lo, n in second[0]:
        out.append((i, lo, n, at))
        at += n
    for blk in (first, second):
        out.append((*blk[1][e], GC, at))
        at += GC
    return out


def assemble_kernel(plans, n_in, *refs):
    ins, outs, sem = refs[:n_in], refs[n_in:-1], refs[-1]
    copies, i = [], 0
    for plan, out in zip(plans, outs):
        for src, lo, n, at in plan:
            copies.append(
                pltpu.make_async_copy(ins[src].at[lo : lo + n, :], out.at[at : at + n, :], sem.at[i])
            )
            i += 1
    for cp in copies:
        cp.start()
    for cp in copies:
        cp.wait()


def assemble(first, second, *ins):
    plans = (message(first, second, 1), message(second, first, 3))
    return pl.pallas_call(
        lambda *r: assemble_kernel(plans, len(ins), *r),
        out_shape=(jax.ShapeDtypeStruct((MR, M), BF16),) * 2,
        in_specs=[ANY] * len(ins),
        out_specs=(ANY,) * 2,
        scratch_shapes=[pltpu.SemaphoreType.DMA((sum(len(p) for p in plans),))],
        name="assemble",
    )(*ins)


def coefs(rows, per, v):
    row = lax.broadcasted_iota(jnp.int32, (rows, M), 0)
    c = jnp.zeros((rows, M), jnp.int32)
    for i in range(1, C):
        c = c + (row >= per * i).astype(jnp.int32)
    base = jnp.where((c == 1) | (c == 4) | (c == 7), 2.0, 1.0)
    return jnp.where(c < 3, base, -base * v)


ACCS = ((RU, CU), (RU, CU), (RU, 2 * K), (CU, K), (CU, K), (K + 16, K))


def chunk_kernel(blocks, n_in, n_acc, *refs):
    arrs, ins = refs[:n_in], refs[n_in : n_in + n_acc]
    outs, (jac, wg) = refs[n_in + n_acc : -2], refs[-2:]
    for blk, (hs, tl, cl) in enumerate(blocks):
        tail = arrs[tl[0]][tl[1] : tl[1] + 128, :].astype(F32)
        v = tail[117:118, :]
        lanes = slice(blk * M, (blk + 1) * M)
        wg[blk, 0:108, :] = tail[0:108, :] * coefs(108, LR, v)
        wg[blk, 176:185, :] = tail[108:117, :] * coefs(C, 1, v)
        gc = arrs[cl[0]][cl[1] : cl[1] + GC, :].astype(F32)
        wg[blk, 112:176, :] = gc * coefs(GC, 6, v)
        jac[J_R:JR, lanes] = jnp.zeros((JR - J_R, M), BF16)
        first_row = lax.broadcasted_iota(jnp.int32, (16, M), 0) == 0
        jac[J_R : J_R + 16, lanes] = jnp.where(first_row, tail[118:119, :], 0.0).astype(BF16)

    for blk, (hs, tl, cl) in enumerate(blocks):
        lanes = slice(blk * M, (blk + 1) * M)

        def slab(t, carry, hs=hs, lanes=lanes, blk=blk):
            base = pl.multiple_of(t * 16, 16)
            h = [arrs[i][pl.ds(lo + base, 16), :].astype(F32) for i, lo in hs]

            def unit(rows, dst):
                acc = wg[blk, rows[0] : rows[0] + 1, :] * h[0]
                for c in range(1, C):
                    acc = acc + wg[blk, rows[c] : rows[c] + 1, :] * h[c]
                jac[pl.ds(dst + base, 16), lanes] = acc.astype(BF16)

            for u in range(LR):
                unit([c * LR + u for c in range(C)], u * K)
            for u in range(6):
                unit([112 + c * 6 + u for c in range(C)], RU + u * K)
            unit([176 + c for c in range(C)], J_K)
            return carry

        lax.fori_loop(0, K // 16, slab, 0)

    def acc(i, rows, cols, val):
        if n_acc:
            val = val + ins[i][rows, cols]
        outs[i][rows, cols] = val

    al = slice(None)
    pd = lax.dot_general(jac[RU : J_R + 16, :], jac[J_K:J_R, :], NT, preferred_element_type=F32)
    acc(3, al, al, pd[0:CU])
    acc(4, al, al, pd[CU : 2 * CU])
    acc(5, al, al, pd[2 * CU :])
    tile = 512
    for n in (3, 0, 1, 2):
        for m in range(RU // tile):
            rows = slice(m * tile, (m + 1) * tile)
            val = lax.dot_general(
                jac[rows, :], jac[RU + n * 256 : RU + (n + 1) * 256, :], NT,
                preferred_element_type=F32,
            )
            if n == 0:
                acc(0, rows, slice(0, 256), val)
            elif n == 1:
                acc(0, rows, slice(256, 384), val[:, :128])
                acc(1, rows, slice(0, 128), val[:, 128:])
            elif n == 2:
                acc(1, rows, slice(128, 384), val)
            else:
                acc(2, rows, al, val)


def chunk(blocks, arrs, accs, name):
    n = len(blocks)
    return pl.pallas_call(
        lambda *r: chunk_kernel(blocks, len(arrs), len(accs), *r),
        out_shape=tuple(jax.ShapeDtypeStruct(s, F32) for s in ACCS),
        in_specs=[VM] * (len(arrs) + len(accs)),
        out_specs=(VM,) * len(ACCS),
        scratch_shapes=[pltpu.VMEM((JR, n * M), BF16), pltpu.VMEM((n, 192, M), F32)],
        compiler_params=params(),
        name=name,
    )(*arrs, *accs)


def place(block, e, shift):
    hs, rows = [], [(i, lo + r) for i, lo, n in block[0] for r in range(0, n, K)]
    rows = [(i + shift, lo) for i, lo in rows]
    i, lo = block[1][e]
    return rows[:C], rows[C], (i + shift, lo)


def received(i, col):
    two = []
    for b in range(2):
        lo = b * (BR + GC)
        two.append(([(i, lo + c * K) for c in range(C)], (i, lo + HR), (i, col + b * GC)))
    return two


def chol_kernel(a_ref, b_ref, d_ref, chol_ref, w_ref, yz_ref, m_ref, u_ref):
    row = lax.broadcasted_iota(jnp.int32, (K, K), 0)
    col = lax.broadcasted_iota(jnp.int32, (K, K), 1)
    eye = row == col
    gram = (a_ref[0:K, :] + b_ref[0:K, :]) * (1.0 / TOTAL)
    m_ref[:, :K] = gram + jnp.where(eye, d_ref[0:1, :], 0.0)
    m_ref[:, K:] = jnp.where(eye, 1.0, 0.0)
    sub = lax.broadcasted_iota(jnp.int32, (8, 2 * K), 0)
    for b in range(K // 8):
        p = m_ref[8 * b : 8 * b + 8, :]
        for r in range(8):
            j = 8 * b + r
            cb = p[:, j : j + 1]
            rs = lax.rsqrt(p[r : r + 1, j : j + 1])
            urow = p[r : r + 1, :] * rs
            p = jnp.where(sub > r, p - (cb * rs) * urow, jnp.where(sub == r, urow, p))
        u_ref[8 * b : 8 * b + 8, :] = p
        if b < K // 8 - 1:
            upd = lax.dot_general(p[:, :K], p, TN, precision=HI, preferred_element_type=F32)
            lo = 8 * (b + 1)
            m_ref[lo:, :] = m_ref[lo:, :] - upd[lo:, :]
    chol_ref[...] = jnp.where(col >= row, u_ref[:, :K], 0.0).T
    w = u_ref[:, K:]
    w_ref[...] = w
    g = (a_ref[K : K + 8, :] + b_ref[K : K + 8, :]) * (1.0 / TOTAL)
    y = lax.dot_general(g, w, NT, precision=HI, preferred_element_type=F32)
    z = lax.dot_general(y, w, (((1,), (0,)), ((), ())), precision=HI, preferred_element_type=F32)
    yz_ref[0:8, :] = y
    yz_ref[8:16, :] = z


def cholesky(dk, dk2, damp):
    return pl.pallas_call(
        chol_kernel,
        out_shape=(
            jax.ShapeDtypeStruct((K, K), F32),
            jax.ShapeDtypeStruct((K, K), F32),
            jax.ShapeDtypeStruct((16, K), F32),
        ),
        in_specs=[VM] * 3,
        out_specs=(VM,) * 3,
        scratch_shapes=[pltpu.VMEM((K, 2 * K), F32), pltpu.VMEM((K, 2 * K), F32)],
        compiler_params=params(),
        name="panel_factor",
    )(dk, dk2, damp)


def halves(v):
    hi = v.astype(BF16)
    return hi, (v - hi.astype(F32)).astype(BF16)


def panel_kernel(k_ref, p_ref, pr_ref, po_ref, por_ref, w_ref, yz_ref, dir_ref, lpan_ref, la_ref, lb_ref):
    q, k = lax.axis_index("row"), k_ref[0]
    inv = 1.0 / TOTAL
    w_hi, w_lo = halves(w_ref[...])
    wb = jnp.concatenate([w_hi, w_lo, w_hi], axis=1)
    sub = lax.broadcasted_iota(jnp.int32, (8, 2 * K), 0)
    lane = lax.broadcasted_iota(jnp.int32, (8, 2 * K), 1)
    z = yz_ref[8:9, :]
    z2 = jnp.concatenate([z, jnp.zeros_like(z)], axis=1)
    lhs = jnp.where(lane == K, 1.0, jnp.where(sub == 0, -z2, 0.0))

    def solve(p):
        hi, lo = halves(p)
        return lax.dot_general(
            jnp.concatenate([hi, hi, lo], axis=1), wb, NT, preferred_element_type=F32
        )

    for lr in range(LR):
        rows = slice(lr * K, (lr + 1) * K)
        pe = (p_ref[rows, :] + pr_ref[rows, :]) * inv
        d = lax.dot_general(lhs, pe, NT, precision=HI, preferred_element_type=F32)
        i = lr * NZ + q
        dir_ref[lr : lr + 1, :] = jnp.where(
            i == k, yz_ref[0:1, :], jnp.where(i > k, d[0:1, :], d[1:2, :])
        )
        lpan = solve(pe[:, :K])
        lpan_ref[rows, :] = lpan
        hi, lo = halves(lpan)
        la_ref[rows, :] = jnp.concatenate([hi, hi, lo], axis=1)
    hi, lo = halves(solve((po_ref[...] + por_ref[...]) * inv))
    lb_ref[...] = jnp.concatenate([hi, lo, hi], axis=1)


def panel_solve(k, p, pr, po, por, w, yz):
    return pl.pallas_call(
        panel_kernel,
        out_shape=(
            jax.ShapeDtypeStruct((LR, K), F32),
            jax.ShapeDtypeStruct((RU, K), F32),
            jax.ShapeDtypeStruct((RU, 3 * K), BF16),
            jax.ShapeDtypeStruct((CU, 3 * K), BF16),
        ),
        in_specs=[SMEM] + [VM] * 6,
        out_specs=(VM,) * 4,
        compiler_params=params(),
        name="panel_solve",
    )(k, p, pr, po, por, w, yz)


def final_kernel(k_ref, g_ref, gr_ref, la_ref, lb_ref, lpan_ref, chol_ref, damp_ref, out_ref):
    q, k = lax.axis_index("row"), k_ref[0]
    s = (lax.axis_index("x") * NY + lax.axis_index("y")) * NC + lax.axis_index("core")
    lr = pl.program_id(0)
    i = lr * NZ + q
    upd = lax.dot_general(la_ref[...], lb_ref[...], NT, preferred_element_type=F32)
    gram = (g_ref[...] + gr_ref[...]) * (1.0 / TOTAL)
    row = lax.broadcasted_iota(jnp.int32, (K, K), 0)
    col = lax.broadcasted_iota(jnp.int32, (K, K), 1)
    damp = damp_ref[pl.ds(lr, 1), :]
    for lc in range(LC):
        j = lc * (NX * NY * NC) + s
        gt = gram[:, lc * K : (lc + 1) * K] + jnp.where((row == col) & (i == j), damp, 0.0)
        val = jnp.where(
            (i > k) & (j > k),
            gt - upd[:, lc * K : (lc + 1) * K],
            jnp.where(
                (i > k) & (j == k),
                lpan_ref[...],
                jnp.where((i == k) & (j == k), chol_ref[...], gt),
            ),
        )
        out_ref[pl.ds(lc, K, stride=LC), :] = val


def final(k, gown, grecv, la, lb, lpan, chol, damp):
    full = lambda shape: pl.BlockSpec(shape, lambda i: (0,) * len(shape))
    rows = lambda width: pl.BlockSpec((K, width), lambda i: (i, 0))
    return pl.pallas_call(
        final_kernel,
        grid=(LR,),
        out_shape=jax.ShapeDtypeStruct((RU * LC, K), F32),
        in_specs=[
            SMEM, rows(CU), rows(CU), rows(3 * K), full((CU, 3 * K)), rows(K), full((K, K)),
            full((LR, K)),
        ],
        out_specs=pl.BlockSpec((K * LC, K), lambda i: (i, 0)),
        compiler_params=params(),
        name="trailing_update",
    )(k, gown, grecv, la, lb, lpan, chol, damp)


def device(x, y, c, z):
    return ((x * NY + y) * NC + c) * NZ + z


def hops(along_x_core, d):
    pairs = []
    for x in range(NX):
        for y in range(NY):
            for c in range(NC):
                for z in range(NZ):
                    to = ((x + d) % NX, y) if c == along_x_core else (x, (y + d) % NY)
                    pairs.append((device(x, y, c, z), device(*to, c, z)))
    return pairs


def body(g_jets, layer_input_jets, speed, resid, point_index, damping, panel):
    q = lax.axis_index("row")
    k = panel[0]
    one = lambda v, d: lax.ppermute(v, AXES, hops(0, d))
    two = lambda v, d: lax.ppermute(v, AXES, hops(1, d))
    swap = lambda v: lax.ppermute(v, "core", [(0, 1), (1, 0)])
    zbit = lambda v, bit: v + lax.ppermute(v, "row", [(i, i ^ bit) for i in range(NZ)])
    bar = lax.optimization_barrier

    plus, minus, own = pack(
        panel,
        point_index.reshape(1, M),
        layer_input_jets.reshape(HR, POOL),
        g_jets.transpose(1, 0, 2).reshape(C * A, POOL),
        jnp.stack([speed, resid]),
    )
    ap, am = one(plus, 1), one(minus, -1)
    m1 = assemble(BLOCK0, BLOCK1, plus, own, ap)
    relay = HB + 2 * GC
    rp, rm = one(ap[:relay], 1), one(am[:relay], -1)
    m1p, m1m = two(m1[0], 1), two(m1[1], -1)
    m2 = assemble(BLOCK2, BLOCK3, am, rp, rm)
    dsel = lax.dynamic_index_in_dim(damping[:, 0, :], k // NZ, 0, keepdims=True)
    dsel = jnp.broadcast_to(jnp.where(k % NZ == q, dsel, 0.0), (8, K))

    line = [place(BLOCK0, 0, 0), place(BLOCK1, 0, 0), place(BLOCK2, 0, 3), place(BLOCK3, 0, 3)]
    accs = chunk(line, (plus, own, ap, am, rp, rm), (), "chunk_line")
    dsel = zbit(dsel, 1)
    m2, m1p, m1m, dsel = bar((m2, m1p, m1m, dsel))
    n1 = BR + GC
    r1p, r1m = two(m1p[:n1], 1), two(m1m[:n1], -1)
    m2p, m2m = two(m2[0], 1), two(m2[1], -1)
    near = received(0, 2 * BR + GC) + received(1, 2 * BR + GC)
    accs = chunk(near, (m1p, m1m), accs, "chunk_near1")
    dsel = zbit(dsel, 2)
    accs, dsel = bar((accs, dsel))
    far = [received(0, BR)[0], received(1, BR)[0]]
    accs = chunk(far, (r1p, r1m), accs, "chunk_far1")
    dsel = zbit(dsel, 4)
    accs, dsel = bar((accs, dsel))
    r2p, r2m = two(m2p[:n1], 1), two(m2m[:n1], -1)
    accs = chunk(near, (m2p, m2m), accs, "chunk_near2")
    accs = chunk(far, (r2p, r2m), accs, "chunk_far2")
    gown, gsib, p, po, ps, dk = accs

    dk2 = swap(dk)
    pr, por = swap(p), swap(ps)
    gr = swap(gsib)
    chol, w, yz = cholesky(dk, dk2, dsel)
    mine, lpan, la, lb = panel_solve(panel, p, pr, po, por, w, yz)
    slot = lax.broadcasted_iota(jnp.int32, (1, NZ, 1), 1)
    full = jnp.where(slot == q, mine[:, None, :], 0.0)
    for bit in (1, 2, 4):
        full = zbit(full, bit)
    fac = final(panel, gown, gr, la, lb, lpan, chol, damping[:, 0, :])
    return fac.reshape(LR, 1, K, LC, 1, K), full.reshape(-1)


def solution(mesh):
    grid = Mesh(mesh.devices.reshape(NX, NY, NC, NZ), AXES)
    pts = ("x", "y", "core")
    in_specs = (
        P(None, None, pts),
        P(None, None, pts),
        P(pts),
        P(pts),
        P(pts),
        P(None, "row", None),
        P(),
    )
    out_specs = (P(None, "row", None, None, pts, None), P())
    return jax.shard_map(body, mesh=grid, in_specs=in_specs, out_specs=out_specs, check_vma=False)
```

```python
import jax
import jax.numpy as jnp
from jax import lax
from jax.experimental import pallas as pl
from jax.experimental.pallas import tpu as pltpu
from jax.sharding import Mesh, PartitionSpec as P

NX, NY, NC, NZ = 4, 4, 2, 8
A, K, C, POOL, M = 96, 128, 9, 256, 128
LR, LC = 12, 3
TOTAL = 4096
HR = C * K
BR = 1280
ROWG, KG, VR, RR = HR, HR + 108, HR + 117, HR + 118
GC = 64
HB = BR // 2
PR = BR + 6 * GC
MR = 2 * BR + 3 * GC
RU, CU = LR * K, LC * K
JR = RU + 2 * CU + 2 * K
J_K, J_R = RU + 2 * CU, RU + 2 * CU + K
F32, BF16 = jnp.float32, jnp.bfloat16
AXES = ("x", "y", "core", "row")
HI = lax.Precision.HIGHEST
NT = (((1,), (1,)), ((), ()))
TN = (((0,), (0,)), ((), ()))
VMEM_LIMIT = 20 * 1024 * 1024
SMEM = pl.BlockSpec(memory_space=pltpu.SMEM)
VM = pl.BlockSpec(memory_space=pltpu.VMEM)


def params():
    return pltpu.CompilerParams(vmem_limit_bytes=VMEM_LIMIT)


def pack_kernel(k_ref, idx_ref, h_ref, g_ref, vr_ref, plus_ref, minus_ref, own_ref, gs, tail, cbuf):
    x, y = lax.axis_index("x"), lax.axis_index("y")
    core, q = lax.axis_index("core"), lax.axis_index("row")
    k = k_ref[0]
    pool = lax.broadcasted_iota(jnp.int32, (POOL, M), 0)
    sel = (pool == idx_ref[...]).astype(F32).astype(BF16)
    for c in range(C):
        val = jnp.dot(h_ref[c * K : (c + 1) * K, :], sel, preferred_element_type=F32).astype(BF16)
        lo = c * K if c < 5 else c * K + 2 * GC
        plus_ref[lo : lo + K, :] = val
        lo = c * K + HB + 2 * GC if c < 5 else c * K - HB
        minus_ref[lo : lo + K, :] = val
    for c in range(C):
        gs[c * A : (c + 1) * A, :] = jnp.dot(
            g_ref[c * A : (c + 1) * A, :], sel, preferred_element_type=F32
        )
    tail[...] = jnp.zeros_like(tail)
    for c in range(C):
        tail[c * LR : (c + 1) * LR, :] = gs[pl.ds(c * A + q, LR, stride=NZ), :]
        tail[108 + c : 109 + c, :] = gs[pl.ds(c * A + k, 1), :]
    tail[117:119, :] = jnp.dot(vr_ref[...], sel, preferred_element_type=F32)
    val = tail[...].astype(BF16)
    plus_ref[HR + 2 * GC : BR + 2 * GC, :] = val
    minus_ref[HR - HB : HB, :] = val
    cbuf[...] = jnp.zeros_like(cbuf)
    for dp in range(4):
        for dt in range(4):
            px = lax.rem(jnp.where(core == 0, x + dp, x + dt), NX)
            py = lax.rem(jnp.where(core == 0, y + dt, y + dp), NY)
            d = px * NY + py
            for c in range(C):
                for o in range(2):
                    cc = core if o == 0 else 1 - core
                    for lc in range(LC):
                        row = c * 6 + o * LC + lc
                        cbuf[row : row + 1, :] = gs[pl.ds(c * A + lc * 32 + 2 * d + cc, 1), :]
            val = cbuf[...].astype(BF16)
            if dp == 0:
                own_ref[dt * GC : (dt + 1) * GC, :] = val
            elif dp == 1:
                plus_ref[BR + (2 + dt) * GC : BR + (3 + dt) * GC, :] = val
            elif dp == 3:
                minus_ref[BR + (2 + dt) * GC : BR + (3 + dt) * GC, :] = val
            elif dt < 2:
                plus_ref[HB + dt * GC : HB + (dt + 1) * GC, :] = val
            else:
                minus_ref[HB + (dt - 2) * GC : HB + (dt - 1) * GC, :] = val


def pack(k, idx, h, g, vr):
    return pl.pallas_call(
        pack_kernel,
        out_shape=(
            jax.ShapeDtypeStruct((PR, M), BF16),
            jax.ShapeDtypeStruct((PR, M), BF16),
            jax.ShapeDtypeStruct((4 * GC, M), BF16),
        ),
        in_specs=[SMEM, VM, VM, VM, VM],
        out_specs=(VM,) * 3,
        scratch_shapes=[
            pltpu.VMEM((C * A, M), F32),
            pltpu.VMEM((128, M), F32),
            pltpu.VMEM((GC, M), F32),
        ],
        compiler_params=params(),
        name="pack",
    )(k, idx, h, g, vr)


def block_from_plus(i, cols):
    return ([(i, 0, HB), (i, HB + 2 * GC, HB)], cols)


def block_from_minus(i, cols):
    return ([(i, HB + 2 * GC, HB), (i, 0, HB)], cols)


def after(i, lo):
    return [(i, lo + e * GC) for e in range(4)]


BLOCK0 = block_from_plus(0, after(1, 0))
BLOCK1 = block_from_plus(2, after(2, BR + 2 * GC))
BLOCK2 = block_from_minus(0, after(0, BR + 2 * GC))
BLOCK3 = (
    [(1, 0, HB), (2, 0, HB)],
    [(1, HB), (1, HB + GC), (2, HB), (2, HB + GC)],
)


def message(first, second, e):
    out, at = [], 0
    for i, lo, n in first[0]:
        out.append((i, lo, n, at))
        at += n
    out.append((*first[1][2], GC, at))
    at += GC
    for i, lo, n in second[0]:
        out.append((i, lo, n, at))
        at += n
    for blk in (first, second):
        out.append((*blk[1][e], GC, at))
        at += GC
    return out


def assemble_kernel(plans, n_in, *refs):
    ins, outs = refs[:n_in], refs[n_in:]
    for plan, out in zip(plans, outs):
        for src, lo, n, at in plan:
            out[at : at + n, :] = ins[src][lo : lo + n, :]


def assemble(first, second, *ins):
    plans = (message(first, second, 1), message(second, first, 3))
    return pl.pallas_call(
        lambda *r: assemble_kernel(plans, len(ins), *r),
        out_shape=(jax.ShapeDtypeStruct((MR, M), BF16),) * 2,
        in_specs=[VM] * len(ins),
        out_specs=(VM,) * 2,
        compiler_params=params(),
        name="assemble",
    )(*ins)


def coefs(rows, per, v):
    row = lax.broadcasted_iota(jnp.int32, (rows, M), 0)
    c = jnp.zeros((rows, M), jnp.int32)
    for i in range(1, C):
        c = c + (row >= per * i).astype(jnp.int32)
    base = jnp.where((c == 1) | (c == 4) | (c == 7), 2.0, 1.0)
    return jnp.where(c < 3, base, -base * v)


ACCS = ((RU, CU), (RU, CU), (RU, 2 * K), (CU, K), (CU, K), (K + 16, K))


def chunk_kernel(blocks, n_in, n_acc, *refs):
    arrs, ins = refs[:n_in], refs[n_in : n_in + n_acc]
    outs, (jac, wg) = refs[n_in + n_acc : -2], refs[-2:]
    for blk, (hs, tl, cl) in enumerate(blocks):
        tail = arrs[tl[0]][tl[1] : tl[1] + 128, :].astype(F32)
        v = tail[117:118, :]
        lanes = slice(blk * M, (blk + 1) * M)
        wg[blk, 0:108, :] = tail[0:108, :] * coefs(108, LR, v)
        wg[blk, 176:185, :] = tail[108:117, :] * coefs(C, 1, v)
        gc = arrs[cl[0]][cl[1] : cl[1] + GC, :].astype(F32)
        wg[blk, 112:176, :] = gc * coefs(GC, 6, v)
        jac[J_R:JR, lanes] = jnp.zeros((JR - J_R, M), BF16)
        first_row = lax.broadcasted_iota(jnp.int32, (16, M), 0) == 0
        jac[J_R : J_R + 16, lanes] = jnp.where(first_row, tail[118:119, :], 0.0).astype(BF16)

    for blk, (hs, tl, cl) in enumerate(blocks):
        lanes = slice(blk * M, (blk + 1) * M)

        def slab(t, carry, hs=hs, lanes=lanes, blk=blk):
            base = pl.multiple_of(t * 16, 16)
            h = [arrs[i][pl.ds(lo + base, 16), :].astype(F32) for i, lo in hs]

            def unit(rows, dst):
                acc = wg[blk, rows[0] : rows[0] + 1, :] * h[0]
                for c in range(1, C):
                    acc = acc + wg[blk, rows[c] : rows[c] + 1, :] * h[c]
                jac[pl.ds(dst + base, 16), lanes] = acc.astype(BF16)

            for u in range(LR):
                unit([c * LR + u for c in range(C)], u * K)
            for u in range(6):
                unit([112 + c * 6 + u for c in range(C)], RU + u * K)
            unit([176 + c for c in range(C)], J_K)
            return carry

        lax.fori_loop(0, K // 16, slab, 0)

    def acc(i, rows, cols, val):
        if n_acc:
            val = val + ins[i][rows, cols]
        outs[i][rows, cols] = val

    al = slice(None)
    pd = lax.dot_general(jac[RU : J_R + 16, :], jac[J_K:J_R, :], NT, preferred_element_type=F32)
    acc(3, al, al, pd[0:CU])
    acc(4, al, al, pd[CU : 2 * CU])
    acc(5, al, al, pd[2 * CU :])
    tile = 512
    for n in (3, 0, 1, 2):
        for m in range(RU // tile):
            rows = slice(m * tile, (m + 1) * tile)
            val = lax.dot_general(
                jac[rows, :], jac[RU + n * 256 : RU + (n + 1) * 256, :], NT,
                preferred_element_type=F32,
            )
            if n == 0:
                acc(0, rows, slice(0, 256), val)
            elif n == 1:
                acc(0, rows, slice(256, 384), val[:, :128])
                acc(1, rows, slice(0, 128), val[:, 128:])
            elif n == 2:
                acc(1, rows, slice(128, 384), val)
            else:
                acc(2, rows, al, val)


def chunk(blocks, arrs, accs, name):
    n = len(blocks)
    return pl.pallas_call(
        lambda *r: chunk_kernel(blocks, len(arrs), len(accs), *r),
        out_shape=tuple(jax.ShapeDtypeStruct(s, F32) for s in ACCS),
        in_specs=[VM] * (len(arrs) + len(accs)),
        out_specs=(VM,) * len(ACCS),
        scratch_shapes=[pltpu.VMEM((JR, n * M), BF16), pltpu.VMEM((n, 192, M), F32)],
        compiler_params=params(),
        name=name,
    )(*arrs, *accs)


def place(block, e, shift):
    hs, rows = [], [(i, lo + r) for i, lo, n in block[0] for r in range(0, n, K)]
    rows = [(i + shift, lo) for i, lo in rows]
    i, lo = block[1][e]
    return rows[:C], rows[C], (i + shift, lo)


def received(i, col):
    two = []
    for b in range(2):
        lo = b * (BR + GC)
        two.append(([(i, lo + c * K) for c in range(C)], (i, lo + HR), (i, col + b * GC)))
    return two


def chol_kernel(a_ref, b_ref, d_ref, chol_ref, w_ref, yz_ref, m_ref, u_ref):
    row = lax.broadcasted_iota(jnp.int32, (K, K), 0)
    col = lax.broadcasted_iota(jnp.int32, (K, K), 1)
    eye = row == col
    gram = (a_ref[0:K, :] + b_ref[0:K, :]) * (1.0 / TOTAL)
    m_ref[:, :K] = gram + jnp.where(eye, d_ref[0:1, :], 0.0)
    m_ref[:, K:] = jnp.where(eye, 1.0, 0.0)
    sub = lax.broadcasted_iota(jnp.int32, (8, 2 * K), 0)
    for b in range(K // 8):
        p = m_ref[8 * b : 8 * b + 8, :]
        for r in range(8):
            j = 8 * b + r
            cb = p[:, j : j + 1]
            rs = lax.rsqrt(p[r : r + 1, j : j + 1])
            urow = p[r : r + 1, :] * rs
            p = jnp.where(sub > r, p - (cb * rs) * urow, jnp.where(sub == r, urow, p))
        u_ref[8 * b : 8 * b + 8, :] = p
        if b < K // 8 - 1:
            upd = lax.dot_general(p[:, :K], p, TN, precision=HI, preferred_element_type=F32)
            lo = 8 * (b + 1)
            m_ref[lo:, :] = m_ref[lo:, :] - upd[lo:, :]
    chol_ref[...] = jnp.where(col >= row, u_ref[:, :K], 0.0).T
    w = u_ref[:, K:]
    w_ref[...] = w
    g = (a_ref[K : K + 8, :] + b_ref[K : K + 8, :]) * (1.0 / TOTAL)
    y = lax.dot_general(g, w, NT, precision=HI, preferred_element_type=F32)
    z = lax.dot_general(y, w, (((1,), (0,)), ((), ())), precision=HI, preferred_element_type=F32)
    yz_ref[0:8, :] = y
    yz_ref[8:16, :] = z


def cholesky(dk, dk2, damp):
    return pl.pallas_call(
        chol_kernel,
        out_shape=(
            jax.ShapeDtypeStruct((K, K), F32),
            jax.ShapeDtypeStruct((K, K), F32),
            jax.ShapeDtypeStruct((16, K), F32),
        ),
        in_specs=[VM] * 3,
        out_specs=(VM,) * 3,
        scratch_shapes=[pltpu.VMEM((K, 2 * K), F32), pltpu.VMEM((K, 2 * K), F32)],
        compiler_params=params(),
        name="panel_factor",
    )(dk, dk2, damp)


def halves(v):
    hi = v.astype(BF16)
    return hi, (v - hi.astype(F32)).astype(BF16)


def panel_kernel(k_ref, p_ref, pr_ref, po_ref, por_ref, w_ref, yz_ref, dir_ref, lpan_ref, la_ref, lb_ref):
    q, k = lax.axis_index("row"), k_ref[0]
    inv = 1.0 / TOTAL
    w_hi, w_lo = halves(w_ref[...])
    wb = jnp.concatenate([w_hi, w_lo, w_hi], axis=1)
    sub = lax.broadcasted_iota(jnp.int32, (8, 2 * K), 0)
    lane = lax.broadcasted_iota(jnp.int32, (8, 2 * K), 1)
    z = yz_ref[8:9, :]
    z2 = jnp.concatenate([z, jnp.zeros_like(z)], axis=1)
    lhs = jnp.where(lane == K, 1.0, jnp.where(sub == 0, -z2, 0.0))

    def solve(p):
        hi, lo = halves(p)
        return lax.dot_general(
            jnp.concatenate([hi, hi, lo], axis=1), wb, NT, preferred_element_type=F32
        )

    for lr in range(LR):
        rows = slice(lr * K, (lr + 1) * K)
        pe = (p_ref[rows, :] + pr_ref[rows, :]) * inv
        d = lax.dot_general(lhs, pe, NT, precision=HI, preferred_element_type=F32)
        i = lr * NZ + q
        dir_ref[lr : lr + 1, :] = jnp.where(
            i == k, yz_ref[0:1, :], jnp.where(i > k, d[0:1, :], d[1:2, :])
        )
        lpan = solve(pe[:, :K])
        lpan_ref[rows, :] = lpan
        hi, lo = halves(lpan)
        la_ref[rows, :] = jnp.concatenate([hi, hi, lo], axis=1)
    hi, lo = halves(solve((po_ref[...] + por_ref[...]) * inv))
    lb_ref[...] = jnp.concatenate([hi, lo, hi], axis=1)


def panel_solve(k, p, pr, po, por, w, yz):
    return pl.pallas_call(
        panel_kernel,
        out_shape=(
            jax.ShapeDtypeStruct((LR, K), F32),
            jax.ShapeDtypeStruct((RU, K), F32),
            jax.ShapeDtypeStruct((RU, 3 * K), BF16),
            jax.ShapeDtypeStruct((CU, 3 * K), BF16),
        ),
        in_specs=[SMEM] + [VM] * 6,
        out_specs=(VM,) * 4,
        compiler_params=params(),
        name="panel_solve",
    )(k, p, pr, po, por, w, yz)


def final_kernel(k_ref, g_ref, gr_ref, la_ref, lb_ref, lpan_ref, chol_ref, damp_ref, out_ref):
    q, k = lax.axis_index("row"), k_ref[0]
    s = (lax.axis_index("x") * NY + lax.axis_index("y")) * NC + lax.axis_index("core")
    lr = pl.program_id(0)
    i = lr * NZ + q
    upd = lax.dot_general(la_ref[...], lb_ref[...], NT, preferred_element_type=F32)
    gram = (g_ref[...] + gr_ref[...]) * (1.0 / TOTAL)
    row = lax.broadcasted_iota(jnp.int32, (K, K), 0)
    col = lax.broadcasted_iota(jnp.int32, (K, K), 1)
    damp = damp_ref[pl.ds(lr, 1), :]
    for lc in range(LC):
        j = lc * (NX * NY * NC) + s
        gt = gram[:, lc * K : (lc + 1) * K] + jnp.where((row == col) & (i == j), damp, 0.0)
        val = jnp.where(
            (i > k) & (j > k),
            gt - upd[:, lc * K : (lc + 1) * K],
            jnp.where(
                (i > k) & (j == k),
                lpan_ref[...],
                jnp.where((i == k) & (j == k), chol_ref[...], gt),
            ),
        )
        out_ref[pl.ds(lc, K, stride=LC), :] = val


def final(k, gown, grecv, la, lb, lpan, chol, damp):
    full = lambda shape: pl.BlockSpec(shape, lambda i: (0,) * len(shape))
    rows = lambda width: pl.BlockSpec((K, width), lambda i: (i, 0))
    return pl.pallas_call(
        final_kernel,
        grid=(LR,),
        out_shape=jax.ShapeDtypeStruct((RU * LC, K), F32),
        in_specs=[
            SMEM, rows(CU), rows(CU), rows(3 * K), full((CU, 3 * K)), rows(K), full((K, K)),
            full((LR, K)),
        ],
        out_specs=pl.BlockSpec((K * LC, K), lambda i: (i, 0)),
        compiler_params=params(),
        name="trailing_update",
    )(k, gown, grecv, la, lb, lpan, chol, damp)


def device(x, y, c, z):
    return ((x * NY + y) * NC + c) * NZ + z


def hops(along_x_core, d):
    pairs = []
    for x in range(NX):
        for y in range(NY):
            for c in range(NC):
                for z in range(NZ):
                    to = ((x + d) % NX, y) if c == along_x_core else (x, (y + d) % NY)
                    pairs.append((device(x, y, c, z), device(*to, c, z)))
    return pairs


def body(g_jets, layer_input_jets, speed, resid, point_index, damping, panel):
    q = lax.axis_index("row")
    k = panel[0]
    one = lambda v, d: lax.ppermute(v, AXES, hops(0, d))
    two = lambda v, d: lax.ppermute(v, AXES, hops(1, d))
    swap = lambda v: lax.ppermute(v, "core", [(0, 1), (1, 0)])
    zbit = lambda v, bit: v + lax.ppermute(v, "row", [(i, i ^ bit) for i in range(NZ)])
    bar = lax.optimization_barrier

    plus, minus, own = pack(
        panel,
        point_index.reshape(1, M),
        layer_input_jets.reshape(HR, POOL),
        g_jets.transpose(1, 0, 2).reshape(C * A, POOL),
        jnp.stack([speed, resid]),
    )
    ap, am = bar((one(plus, 1), one(minus, -1)))
    m1 = assemble(BLOCK0, BLOCK1, plus, own, ap)
    relay = HB + 2 * GC
    rp, rm = one(ap[:relay], 1), one(am[:relay], -1)
    m1p, m1m = two(m1[0], 1), two(m1[1], -1)
    m2 = assemble(BLOCK2, BLOCK3, am, rp, rm)
    dsel = lax.dynamic_index_in_dim(damping[:, 0, :], k // NZ, 0, keepdims=True)
    dsel = jnp.broadcast_to(jnp.where(k % NZ == q, dsel, 0.0), (8, K))

    line = [place(BLOCK0, 0, 0), place(BLOCK1, 0, 0), place(BLOCK2, 0, 3), place(BLOCK3, 0, 3)]
    accs = chunk(line, (plus, own, ap, am, rp, rm), (), "chunk_line")
    m2, m1p, m1m, accs, dsel = bar((m2, m1p, m1m, accs, zbit(dsel, 1)))
    n1 = BR + GC
    r1p, r1m = two(m1p[:n1], 1), two(m1m[:n1], -1)
    m2p, m2m = two(m2[0], 1), two(m2[1], -1)
    near = received(0, 2 * BR + GC) + received(1, 2 * BR + GC)
    accs = chunk(near, (m1p, m1m), accs, "chunk_near1")
    far = [received(0, BR)[0], received(1, BR)[0]]
    accs = chunk(far, (r1p, r1m), accs, "chunk_far1")
    m2p, m2m, accs, dsel = bar((m2p, m2m, accs, zbit(dsel, 2)))
    r2p, r2m = two(m2p[:n1], 1), two(m2m[:n1], -1)
    accs = chunk(near, (m2p, m2m), accs, "chunk_near2")
    r2p, r2m, accs, dsel = bar((r2p, r2m, accs, zbit(dsel, 4)))
    accs = chunk(far, (r2p, r2m), accs, "chunk_far2")
    gown, gsib, p, po, ps, dk = accs

    dk2, p, ps, gsib = bar((swap(dk), p, ps, gsib))
    pr, por = swap(p), swap(ps)
    gr = swap(gsib)
    chol, w, yz = cholesky(dk, dk2, dsel)
    mine, lpan, la, lb = panel_solve(panel, p, pr, po, por, w, yz)
    slot = lax.broadcasted_iota(jnp.int32, (1, NZ, 1), 1)
    full = jnp.where(slot == q, mine[:, None, :], 0.0)
    full, la = bar((zbit(full, 1), la))
    fac = final(panel, gown, gr, la, lb, lpan, chol, damping[:, 0, :])
    full, fac = bar((zbit(full, 2), fac))
    full = zbit(full, 4)
    return fac.reshape(LR, 1, K, LC, 1, K), full.reshape(-1)


def solution(mesh):
    grid = Mesh(mesh.devices.reshape(NX, NY, NC, NZ), AXES)
    pts = ("x", "y", "core")
    in_specs = (
        P(None, None, pts),
        P(None, None, pts),
        P(pts),
        P(pts),
        P(pts),
        P(None, "row", None),
        P(),
    )
    out_specs = (P(None, "row", None, None, pts, None), P())
    return jax.shard_map(body, mesh=grid, in_specs=in_specs, out_specs=out_specs, check_vma=False)
```

```python
import jax
import jax.numpy as jnp
from jax import lax
from jax.experimental import pallas as pl
from jax.experimental.pallas import tpu as pltpu
from jax.sharding import Mesh, PartitionSpec as P

NX, NY, NC, NZ = 4, 4, 2, 8
A, K, C, POOL, M = 96, 128, 9, 256, 128
LR, LC = 12, 3
TOTAL = 4096
HR = C * K
BR = 1280
ROWG, KG, VR, RR = HR, HR + 108, HR + 117, HR + 118
GC = 64
HB = BR // 2
PR = BR + 6 * GC
MR = 2 * BR + 3 * GC
RU, CU = LR * K, LC * K
JR = RU + 2 * CU + 2 * K
J_K, J_R = RU + 2 * CU, RU + 2 * CU + K
F32, BF16 = jnp.float32, jnp.bfloat16
AXES = ("x", "y", "core", "row")
HI = lax.Precision.HIGHEST
NT = (((1,), (1,)), ((), ()))
TN = (((0,), (0,)), ((), ()))
VMEM_LIMIT = 20 * 1024 * 1024
SMEM = pl.BlockSpec(memory_space=pltpu.SMEM)
VM = pl.BlockSpec(memory_space=pltpu.VMEM)


def params():
    return pltpu.CompilerParams(vmem_limit_bytes=VMEM_LIMIT)


def pack_kernel(k_ref, idx_ref, h_ref, g_ref, vr_ref, plus_ref, minus_ref, own_ref, gs, tail, cbuf):
    x, y = lax.axis_index("x"), lax.axis_index("y")
    core, q = lax.axis_index("core"), lax.axis_index("row")
    k = k_ref[0]
    pool = lax.broadcasted_iota(jnp.int32, (POOL, M), 0)
    sel = (pool == idx_ref[...]).astype(F32).astype(BF16)
    for c in range(C):
        val = jnp.dot(h_ref[c * K : (c + 1) * K, :], sel, preferred_element_type=F32).astype(BF16)
        lo = c * K if c < 5 else c * K + 2 * GC
        plus_ref[lo : lo + K, :] = val
        lo = c * K + HB + 2 * GC if c < 5 else c * K - HB
        minus_ref[lo : lo + K, :] = val
    for c in range(C):
        gs[c * A : (c + 1) * A, :] = jnp.dot(
            g_ref[c * A : (c + 1) * A, :], sel, preferred_element_type=F32
        )
    tail[...] = jnp.zeros_like(tail)
    for c in range(C):
        tail[c * LR : (c + 1) * LR, :] = gs[pl.ds(c * A + q, LR, stride=NZ), :]
        tail[108 + c : 109 + c, :] = gs[pl.ds(c * A + k, 1), :]
    tail[117:119, :] = jnp.dot(vr_ref[...], sel, preferred_element_type=F32)
    val = tail[...].astype(BF16)
    plus_ref[HR + 2 * GC : BR + 2 * GC, :] = val
    minus_ref[HR - HB : HB, :] = val
    cbuf[...] = jnp.zeros_like(cbuf)
    for dp in range(4):
        for dt in range(4):
            px = lax.rem(jnp.where(core == 0, x + dp, x + dt), NX)
            py = lax.rem(jnp.where(core == 0, y + dt, y + dp), NY)
            d = px * NY + py
            for c in range(C):
                for o in range(2):
                    cc = core if o == 0 else 1 - core
                    for lc in range(LC):
                        row = c * 6 + o * LC + lc
                        cbuf[row : row + 1, :] = gs[pl.ds(c * A + lc * 32 + 2 * d + cc, 1), :]
            val = cbuf[...].astype(BF16)
            if dp == 0:
                own_ref[dt * GC : (dt + 1) * GC, :] = val
            elif dp == 1:
                plus_ref[BR + (2 + dt) * GC : BR + (3 + dt) * GC, :] = val
            elif dp == 3:
                minus_ref[BR + (2 + dt) * GC : BR + (3 + dt) * GC, :] = val
            elif dt < 2:
                plus_ref[HB + dt * GC : HB + (dt + 1) * GC, :] = val
            else:
                minus_ref[HB + (dt - 2) * GC : HB + (dt - 1) * GC, :] = val


def pack(k, idx, h, g, vr):
    return pl.pallas_call(
        pack_kernel,
        out_shape=(
            jax.ShapeDtypeStruct((PR, M), BF16),
            jax.ShapeDtypeStruct((PR, M), BF16),
            jax.ShapeDtypeStruct((4 * GC, M), BF16),
        ),
        in_specs=[SMEM, VM, VM, VM, VM],
        out_specs=(VM,) * 3,
        scratch_shapes=[
            pltpu.VMEM((C * A, M), F32),
            pltpu.VMEM((128, M), F32),
            pltpu.VMEM((GC, M), F32),
        ],
        compiler_params=params(),
        name="pack",
    )(k, idx, h, g, vr)


def block_from_plus(i, cols):
    return ([(i, 0, HB), (i, HB + 2 * GC, HB)], cols)


def block_from_minus(i, cols):
    return ([(i, HB + 2 * GC, HB), (i, 0, HB)], cols)


def after(i, lo):
    return [(i, lo + e * GC) for e in range(4)]


BLOCK0 = block_from_plus(0, after(1, 0))
BLOCK1 = block_from_plus(2, after(2, BR + 2 * GC))
BLOCK2 = block_from_minus(0, after(0, BR + 2 * GC))
BLOCK3 = (
    [(1, 0, HB), (2, 0, HB)],
    [(1, HB), (1, HB + GC), (2, HB), (2, HB + GC)],
)


def message(first, second, e):
    out, at = [], 0
    for i, lo, n in first[0]:
        out.append((i, lo, n, at))
        at += n
    out.append((*first[1][2], GC, at))
    at += GC
    for i, lo, n in second[0]:
        out.append((i, lo, n, at))
        at += n
    for blk in (first, second):
        out.append((*blk[1][e], GC, at))
        at += GC
    return out


def assemble_kernel(plans, n_in, *refs):
    ins, outs = refs[:n_in], refs[n_in:]
    for plan, out in zip(plans, outs):
        for src, lo, n, at in plan:
            out[at : at + n, :] = ins[src][lo : lo + n, :]


def assemble(first, second, *ins):
    plans = (message(first, second, 1), message(second, first, 3))
    return pl.pallas_call(
        lambda *r: assemble_kernel(plans, len(ins), *r),
        out_shape=(jax.ShapeDtypeStruct((MR, M), BF16),) * 2,
        in_specs=[VM] * len(ins),
        out_specs=(VM,) * 2,
        compiler_params=params(),
        name="assemble",
    )(*ins)


def coefs(rows, per, v):
    row = lax.broadcasted_iota(jnp.int32, (rows, M), 0)
    c = jnp.zeros((rows, M), jnp.int32)
    for i in range(1, C):
        c = c + (row >= per * i).astype(jnp.int32)
    base = jnp.where((c == 1) | (c == 4) | (c == 7), 2.0, 1.0)
    return jnp.where(c < 3, base, -base * v)


ACCS = ((RU, CU), (RU, CU), (RU, 2 * K), (CU, K), (CU, K), (K + 16, K))


def chunk_kernel(blocks, n_in, n_acc, *refs):
    arrs, ins = refs[:n_in], refs[n_in : n_in + n_acc]
    outs, (jac, wg) = refs[n_in + n_acc : -2], refs[-2:]
    for blk, (hs, tl, cl) in enumerate(blocks):
        tail = arrs[tl[0]][tl[1] : tl[1] + 128, :].astype(F32)
        v = tail[117:118, :]
        lanes = slice(blk * M, (blk + 1) * M)
        wg[blk, 0:108, :] = tail[0:108, :] * coefs(108, LR, v)
        wg[blk, 176:185, :] = tail[108:117, :] * coefs(C, 1, v)
        gc = arrs[cl[0]][cl[1] : cl[1] + GC, :].astype(F32)
        wg[blk, 112:176, :] = gc * coefs(GC, 6, v)
        jac[J_R:JR, lanes] = jnp.zeros((JR - J_R, M), BF16)
        first_row = lax.broadcasted_iota(jnp.int32, (16, M), 0) == 0
        jac[J_R : J_R + 16, lanes] = jnp.where(first_row, tail[118:119, :], 0.0).astype(BF16)

    for blk, (hs, tl, cl) in enumerate(blocks):
        lanes = slice(blk * M, (blk + 1) * M)

        def slab(t, carry, hs=hs, lanes=lanes, blk=blk):
            base = pl.multiple_of(t * 16, 16)
            h = [arrs[i][pl.ds(lo + base, 16), :].astype(F32) for i, lo in hs]

            def unit(rows, dst):
                acc = wg[blk, rows[0] : rows[0] + 1, :] * h[0]
                for c in range(1, C):
                    acc = acc + wg[blk, rows[c] : rows[c] + 1, :] * h[c]
                jac[pl.ds(dst + base, 16), lanes] = acc.astype(BF16)

            for u in range(LR):
                unit([c * LR + u for c in range(C)], u * K)
            for u in range(6):
                unit([112 + c * 6 + u for c in range(C)], RU + u * K)
            unit([176 + c for c in range(C)], J_K)
            return carry

        lax.fori_loop(0, K // 16, slab, 0)

    def acc(i, rows, cols, val):
        if n_acc:
            val = val + ins[i][rows, cols]
        outs[i][rows, cols] = val

    al = slice(None)
    pd = lax.dot_general(jac[RU : J_R + 16, :], jac[J_K:J_R, :], NT, preferred_element_type=F32)
    acc(3, al, al, pd[0:CU])
    acc(4, al, al, pd[CU : 2 * CU])
    acc(5, al, al, pd[2 * CU :])
    tile = 512
    for n in (3, 0, 1, 2):
        for m in range(RU // tile):
            rows = slice(m * tile, (m + 1) * tile)
            val = lax.dot_general(
                jac[rows, :], jac[RU + n * 256 : RU + (n + 1) * 256, :], NT,
                preferred_element_type=F32,
            )
            if n == 0:
                acc(0, rows, slice(0, 256), val)
            elif n == 1:
                acc(0, rows, slice(256, 384), val[:, :128])
                acc(1, rows, slice(0, 128), val[:, 128:])
            elif n == 2:
                acc(1, rows, slice(128, 384), val)
            else:
                acc(2, rows, al, val)


def chunk(blocks, arrs, accs, name):
    n = len(blocks)
    return pl.pallas_call(
        lambda *r: chunk_kernel(blocks, len(arrs), len(accs), *r),
        out_shape=tuple(jax.ShapeDtypeStruct(s, F32) for s in ACCS),
        in_specs=[VM] * (len(arrs) + len(accs)),
        out_specs=(VM,) * len(ACCS),
        scratch_shapes=[pltpu.VMEM((JR, n * M), BF16), pltpu.VMEM((n, 192, M), F32)],
        compiler_params=params(),
        cost_estimate=pl.CostEstimate(
            flops=n * 2 * JR * K * (RU + C), bytes_accessed=n * 4_000_000, transcendentals=0
        ),
        name=name,
    )(*arrs, *accs)


def place(block, e, shift):
    hs, rows = [], [(i, lo + r) for i, lo, n in block[0] for r in range(0, n, K)]
    rows = [(i + shift, lo) for i, lo in rows]
    i, lo = block[1][e]
    return rows[:C], rows[C], (i + shift, lo)


def received(i, col):
    two = []
    for b in range(2):
        lo = b * (BR + GC)
        two.append(([(i, lo + c * K) for c in range(C)], (i, lo + HR), (i, col + b * GC)))
    return two


def chol_kernel(a_ref, b_ref, d_ref, chol_ref, w_ref, yz_ref, m_ref, u_ref):
    row = lax.broadcasted_iota(jnp.int32, (K, K), 0)
    col = lax.broadcasted_iota(jnp.int32, (K, K), 1)
    eye = row == col
    gram = (a_ref[0:K, :] + b_ref[0:K, :]) * (1.0 / TOTAL)
    m_ref[:, :K] = gram + jnp.where(eye, d_ref[0:1, :], 0.0)
    m_ref[:, K:] = jnp.where(eye, 1.0, 0.0)
    sub = lax.broadcasted_iota(jnp.int32, (8, K), 0)
    pick = lambda v, r: jnp.broadcast_to(v[r : r + 1, :], (8, v.shape[1]))
    for b in range(K // 8):
        lo = 8 * b
        p = m_ref[lo : lo + 8, :]
        left, right = p[:, :K], p[:, K:]
        cols = [jnp.broadcast_to(p[:, lo + c : lo + c + 1], (8, K)) for c in range(8)]
        scale = jnp.ones((8, K), F32)
        for r in range(8):
            rs = lax.rsqrt(pick(cols[r], r))
            mult = jnp.where(sub > r, cols[r] * (rs * rs), 0.0)
            for c in range(r + 1, 8):
                cols[c] = cols[c] - mult * pick(cols[c], r)
            scale = jnp.where(sub == r, rs, scale)
            left = left - mult * pick(left, r)
            right = right - mult * pick(right, r)
        p = jnp.concatenate([left * scale, right * scale], axis=1)
        u_ref[lo : lo + 8, :] = p
        if b < K // 8 - 1:
            ut = p[:, :K].T
            rows = [pick(p, r) for r in range(8)]
            for t in range(b + 1, K // 8):
                at = slice(8 * t, 8 * t + 8)
                acc = m_ref[at, :]
                for r in range(8):
                    acc = acc - jnp.broadcast_to(ut[at, r : r + 1], (8, 2 * K)) * rows[r]
                m_ref[at, :] = acc
    chol_ref[...] = jnp.where(col >= row, u_ref[:, :K], 0.0).T
    w = u_ref[:, K:]
    w_ref[...] = w
    g = (a_ref[K : K + 8, :] + b_ref[K : K + 8, :]) * (1.0 / TOTAL)
    y = lax.dot_general(g, w, NT, precision=HI, preferred_element_type=F32)
    z = lax.dot_general(y, w, (((1,), (0,)), ((), ())), precision=HI, preferred_element_type=F32)
    yz_ref[0:8, :] = y
    yz_ref[8:16, :] = z


def cholesky(dk, dk2, damp):
    return pl.pallas_call(
        chol_kernel,
        out_shape=(
            jax.ShapeDtypeStruct((K, K), F32),
            jax.ShapeDtypeStruct((K, K), F32),
            jax.ShapeDtypeStruct((16, K), F32),
        ),
        in_specs=[VM] * 3,
        out_specs=(VM,) * 3,
        scratch_shapes=[pltpu.VMEM((K, 2 * K), F32), pltpu.VMEM((K, 2 * K), F32)],
        compiler_params=params(),
        name="panel_factor",
    )(dk, dk2, damp)


def halves(v):
    hi = v.astype(BF16)
    return hi, (v - hi.astype(F32)).astype(BF16)


def panel_kernel(k_ref, p_ref, pr_ref, po_ref, por_ref, w_ref, yz_ref, dir_ref, lpan_ref, la_ref, lb_ref):
    q, k = lax.axis_index("row"), k_ref[0]
    inv = 1.0 / TOTAL
    w_hi, w_lo = halves(w_ref[...])
    wb = jnp.concatenate([w_hi, w_lo, w_hi], axis=1)
    sub = lax.broadcasted_iota(jnp.int32, (8, 2 * K), 0)
    lane = lax.broadcasted_iota(jnp.int32, (8, 2 * K), 1)
    z = yz_ref[8:9, :]
    z2 = jnp.concatenate([z, jnp.zeros_like(z)], axis=1)
    lhs = jnp.where(lane == K, 1.0, jnp.where(sub == 0, -z2, 0.0))

    def solve(p):
        hi, lo = halves(p)
        return lax.dot_general(
            jnp.concatenate([hi, hi, lo], axis=1), wb, NT, preferred_element_type=F32
        )

    for lr in range(LR):
        rows = slice(lr * K, (lr + 1) * K)
        pe = (p_ref[rows, :] + pr_ref[rows, :]) * inv
        d = lax.dot_general(lhs, pe, NT, precision=HI, preferred_element_type=F32)
        i = lr * NZ + q
        dir_ref[lr : lr + 1, :] = jnp.where(
            i == k, yz_ref[0:1, :], jnp.where(i > k, d[0:1, :], d[1:2, :])
        )
        lpan = solve(pe[:, :K])
        lpan_ref[rows, :] = lpan
        hi, lo = halves(lpan)
        la_ref[rows, :] = jnp.concatenate([hi, hi, lo], axis=1)
    hi, lo = halves(solve((po_ref[...] + por_ref[...]) * inv))
    lb_ref[...] = jnp.concatenate([hi, lo, hi], axis=1)


def panel_solve(k, p, pr, po, por, w, yz):
    return pl.pallas_call(
        panel_kernel,
        out_shape=(
            jax.ShapeDtypeStruct((LR, K), F32),
            jax.ShapeDtypeStruct((RU, K), F32),
            jax.ShapeDtypeStruct((RU, 3 * K), BF16),
            jax.ShapeDtypeStruct((CU, 3 * K), BF16),
        ),
        in_specs=[SMEM] + [VM] * 6,
        out_specs=(VM,) * 4,
        compiler_params=params(),
        name="panel_solve",
    )(k, p, pr, po, por, w, yz)


def final_kernel(start, k_ref, g_ref, gr_ref, la_ref, lb_ref, lpan_ref, chol_ref, damp_ref, *refs):
    out_ref = refs[-1]
    q, k = lax.axis_index("row"), k_ref[0]
    s = (lax.axis_index("x") * NY + lax.axis_index("y")) * NC + lax.axis_index("core")
    lr = start + pl.program_id(0)
    i = lr * NZ + q
    upd = lax.dot_general(la_ref[...], lb_ref[...], NT, preferred_element_type=F32)
    gram = (g_ref[...] + gr_ref[...]) * (1.0 / TOTAL)
    row = lax.broadcasted_iota(jnp.int32, (K, K), 0)
    col = lax.broadcasted_iota(jnp.int32, (K, K), 1)
    damp = damp_ref[pl.ds(lr, 1), :]
    for lc in range(LC):
        j = lc * (NX * NY * NC) + s
        gt = gram[:, lc * K : (lc + 1) * K] + jnp.where((row == col) & (i == j), damp, 0.0)
        val = jnp.where(
            (i > k) & (j > k),
            gt - upd[:, lc * K : (lc + 1) * K],
            jnp.where(
                (i > k) & (j == k),
                lpan_ref[...],
                jnp.where((i == k) & (j == k), chol_ref[...], gt),
            ),
        )
        out_ref[pl.ds(lc, K, stride=LC), :] = val


def final(start, count, k, gown, grecv, la, lb, lpan, chol, damp, *prev):
    full = lambda shape: pl.BlockSpec(shape, lambda i: (0,) * len(shape))
    rows = lambda width: pl.BlockSpec((K, width), lambda i: (i + start, 0))
    return pl.pallas_call(
        lambda *r: final_kernel(start, *r),
        grid=(count,),
        out_shape=jax.ShapeDtypeStruct((RU * LC, K), F32),
        in_specs=[
            SMEM, rows(CU), rows(CU), rows(3 * K), full((CU, 3 * K)), rows(K), full((K, K)),
            full((LR, K)),
        ] + [pl.BlockSpec(memory_space=pl.ANY)] * len(prev),
        out_specs=pl.BlockSpec((K * LC, K), lambda i: (i + start, 0)),
        input_output_aliases={8: 0} if prev else {},
        compiler_params=params(),
        cost_estimate=pl.CostEstimate(
            flops=count * 6 * K * CU * K, bytes_accessed=count * 1_500_000, transcendentals=0
        ),
        name="trailing_update",
    )(k, gown, grecv, la, lb, lpan, chol, damp, *prev)


def device(x, y, c, z):
    return ((x * NY + y) * NC + c) * NZ + z


def hops(along_x_core, d):
    pairs = []
    for x in range(NX):
        for y in range(NY):
            for c in range(NC):
                for z in range(NZ):
                    to = ((x + d) % NX, y) if c == along_x_core else (x, (y + d) % NY)
                    pairs.append((device(x, y, c, z), device(*to, c, z)))
    return pairs


def body(g_jets, layer_input_jets, speed, resid, point_index, damping, panel):
    q = lax.axis_index("row")
    k = panel[0]
    one = lambda v, d: lax.ppermute(v, AXES, hops(0, d))
    two = lambda v, d: lax.ppermute(v, AXES, hops(1, d))
    swap = lambda v: lax.ppermute(v, "core", [(0, 1), (1, 0)])
    zbit = lambda v, bit: v + lax.ppermute(v, "row", [(i, i ^ bit) for i in range(NZ)])
    bar = lax.optimization_barrier

    plus, minus, own = pack(
        panel,
        point_index.reshape(1, M),
        layer_input_jets.reshape(HR, POOL),
        g_jets.transpose(1, 0, 2).reshape(C * A, POOL),
        jnp.stack([speed, resid]),
    )
    dsel = lax.dynamic_index_in_dim(damping[:, 0, :], k // NZ, 0, keepdims=True)
    dsel = jnp.broadcast_to(jnp.where(k % NZ == q, dsel, 0.0), (8, K))
    ap, am, dsel = bar((one(plus, 1), one(minus, -1), zbit(dsel, 1)))
    m1 = assemble(BLOCK0, BLOCK1, plus, own, ap)
    relay = HB + 2 * GC
    rp, rm = one(ap[:relay], 1), one(am[:relay], -1)
    m1p, m1m = two(m1[0], 1), two(m1[1], -1)
    accs = chunk([place(BLOCK0, 0, 0), place(BLOCK1, 0, 0)], (plus, own, ap), (), "chunk_line1")
    rp, rm, accs, dsel = bar((rp, rm, accs, zbit(dsel, 2)))
    m2 = assemble(BLOCK2, BLOCK3, am, rp, rm)
    m2p, m2m = two(m2[0], 1), two(m2[1], -1)
    n1 = BR + GC
    r1p, r1m = two(m1p[:n1], 1), two(m1m[:n1], -1)
    e1 = 2 * BR + GC
    blocks = received(0, e1) + received(1, e1) + [place(BLOCK2, 0, 2), place(BLOCK3, 0, 2)]
    accs = chunk(blocks, (m1p, m1m, am, rp, rm), accs, "chunk_line2")
    r1p, r1m, m2p, m2m, accs, dsel = bar((r1p, r1m, m2p, m2m, accs, zbit(dsel, 4)))
    r2p, r2m = two(m2p[:n1], 1), two(m2m[:n1], -1)
    blocks = [received(0, BR)[0], received(1, BR)[0]] + received(2, e1) + received(3, e1)
    accs = chunk(blocks, (r1p, r1m, m2p, m2m), accs, "chunk_far1")
    far = [received(0, BR)[0], received(1, BR)[0]]
    accs = chunk(far, (r2p, r2m), accs, "chunk_far2")
    gown, gsib, p, po, ps, dk = accs

    dk2, p, ps, gsib = bar((swap(dk), p, ps, gsib))
    pr, por = swap(p), swap(ps)
    gr = swap(gsib)
    chol, w, yz = cholesky(dk, dk2, dsel)
    mine, lpan, la, lb = panel_solve(panel, p, pr, po, por, w, yz)
    slot = lax.broadcasted_iota(jnp.int32, (1, NZ, 1), 1)
    full = jnp.where(slot == q, mine[:, None, :], 0.0)
    full, la = bar((zbit(full, 1), la))
    rest = (panel, gown, gr, la, lb, lpan, chol, damping[:, 0, :])
    fac = final(0, 9, *rest)
    fac = final(9, 3, *rest, fac)
    full, fac = bar((zbit(full, 2), fac))
    full = zbit(full, 4)
    return fac.reshape(LR, 1, K, LC, 1, K), full.reshape(-1)


def solution(mesh):
    grid = Mesh(mesh.devices.reshape(NX, NY, NC, NZ), AXES)
    pts = ("x", "y", "core")
    in_specs = (
        P(None, None, pts),
        P(None, None, pts),
        P(pts),
        P(pts),
        P(pts),
        P(None, "row", None),
        P(),
    )
    out_specs = (P(None, "row", None, None, pts, None), P())
    return jax.shard_map(body, mesh=grid, in_specs=in_specs, out_specs=out_specs, check_vma=False)
```

```python
import jax
import jax.numpy as jnp
from jax import lax
from jax.experimental import pallas as pl
from jax.experimental.pallas import tpu as pltpu
from jax.sharding import Mesh, PartitionSpec as P

NX, NY, NC, NZ = 4, 4, 2, 8
A, K, C, POOL, M = 96, 128, 9, 256, 128
LR, LC = 12, 3
TOTAL = 4096
HR = C * K
BR = 1280
ROWG, KG, VR, RR = HR, HR + 108, HR + 117, HR + 118
GC = 64
HB = BR // 2
PR = BR + 6 * GC
MR = 2 * BR + 3 * GC
RU, CU = LR * K, LC * K
JR = RU + 2 * CU + 2 * K
J_K, J_R = RU + 2 * CU, RU + 2 * CU + K
F32, BF16 = jnp.float32, jnp.bfloat16
AXES = ("x", "y", "core", "row")
HI = lax.Precision.HIGHEST
NT = (((1,), (1,)), ((), ()))
TN = (((0,), (0,)), ((), ()))
VMEM_LIMIT = 20 * 1024 * 1024
SMEM = pl.BlockSpec(memory_space=pltpu.SMEM)
VM = pl.BlockSpec(memory_space=pltpu.VMEM)
HBM = pl.BlockSpec(memory_space=pltpu.HBM)


def params():
    return pltpu.CompilerParams(vmem_limit_bytes=VMEM_LIMIT)


def pack_kernel(
    k_ref, idx_hbm, h_hbm, g_hbm, v_hbm, r_hbm, plus_ref, minus_ref, own_ref,
    gs, tail, cbuf, idx_ref, h_ref, g_ref, v_ref, r_ref, sem,
):
    copies = [
        pltpu.make_async_copy(src, dst, sem.at[i])
        for i, (src, dst) in enumerate(
            (
                (idx_hbm, idx_ref), (v_hbm, v_ref), (r_hbm, r_ref), (g_hbm, g_ref), (h_hbm, h_ref),
            )
        )
    ]
    for cp in copies:
        cp.start()
    x, y = lax.axis_index("x"), lax.axis_index("y")
    core, q = lax.axis_index("core"), lax.axis_index("row")
    k = k_ref[0]
    pool = lax.broadcasted_iota(jnp.int32, (POOL, M), 0)
    copies[0].wait()
    sel = (pool == idx_ref[...]).astype(F32).astype(BF16)
    for cp in copies[1:]:
        cp.wait()
    for c in range(C):
        val = jnp.dot(h_ref[c * K : (c + 1) * K, :], sel, preferred_element_type=F32).astype(BF16)
        lo = c * K if c < 5 else c * K + 2 * GC
        plus_ref[lo : lo + K, :] = val
        lo = c * K + HB + 2 * GC if c < 5 else c * K - HB
        minus_ref[lo : lo + K, :] = val
    for c in range(C):
        gs[c * A : (c + 1) * A, :] = jnp.dot(
            g_ref[c * A : (c + 1) * A, :], sel, preferred_element_type=F32
        )
    tail[...] = jnp.zeros_like(tail)
    for c in range(C):
        tail[c * LR : (c + 1) * LR, :] = gs[pl.ds(c * A + q, LR, stride=NZ), :]
        tail[108 + c : 109 + c, :] = gs[pl.ds(c * A + k, 1), :]
    for i, ref in enumerate((v_ref, r_ref)):
        low = jnp.dot(ref[...], sel[:M], preferred_element_type=F32)
        high = jnp.dot(ref[...], sel[M:], preferred_element_type=F32)
        tail[117 + i : 118 + i, :] = low[0:1] + high[1:2]
    val = tail[...].astype(BF16)
    plus_ref[HR + 2 * GC : BR + 2 * GC, :] = val
    minus_ref[HR - HB : HB, :] = val
    cbuf[...] = jnp.zeros_like(cbuf)
    for dp in range(4):
        for dt in range(4):
            px = lax.rem(jnp.where(core == 0, x + dp, x + dt), NX)
            py = lax.rem(jnp.where(core == 0, y + dt, y + dp), NY)
            d = px * NY + py
            for c in range(C):
                for o in range(2):
                    cc = core if o == 0 else 1 - core
                    for lc in range(LC):
                        row = c * 6 + o * LC + lc
                        cbuf[row : row + 1, :] = gs[pl.ds(c * A + lc * 32 + 2 * d + cc, 1), :]
            val = cbuf[...].astype(BF16)
            if dp == 0:
                own_ref[dt * GC : (dt + 1) * GC, :] = val
            elif dp == 1:
                plus_ref[BR + (2 + dt) * GC : BR + (3 + dt) * GC, :] = val
            elif dp == 3:
                minus_ref[BR + (2 + dt) * GC : BR + (3 + dt) * GC, :] = val
            elif dt < 2:
                plus_ref[HB + dt * GC : HB + (dt + 1) * GC, :] = val
            else:
                minus_ref[HB + (dt - 2) * GC : HB + (dt - 1) * GC, :] = val


def pack(k, idx, h, g, v, r):
    return pl.pallas_call(
        pack_kernel,
        out_shape=(
            jax.ShapeDtypeStruct((PR, M), BF16),
            jax.ShapeDtypeStruct((PR, M), BF16),
            jax.ShapeDtypeStruct((4 * GC, M), BF16),
        ),
        in_specs=[SMEM] + [HBM] * 5,
        out_specs=(VM,) * 3,
        scratch_shapes=[
            pltpu.VMEM((C * A, M), F32),
            pltpu.VMEM((128, M), F32),
            pltpu.VMEM((GC, M), F32),
            pltpu.VMEM((1, M), jnp.int32),
            pltpu.VMEM((HR, POOL), BF16),
            pltpu.VMEM((C * A, POOL), BF16),
            pltpu.VMEM((2, M), BF16),
            pltpu.VMEM((2, M), BF16),
            pltpu.SemaphoreType.DMA((5,)),
        ],
        compiler_params=pltpu.CompilerParams(vmem_limit_bytes=60 * 1024 * 1024),
        name="pack",
    )(k, idx, h, g, v, r)


def block_from_plus(i, cols):
    return ([(i, 0, HB), (i, HB + 2 * GC, HB)], cols)


def block_from_minus(i, cols):
    return ([(i, HB + 2 * GC, HB), (i, 0, HB)], cols)


def after(i, lo):
    return [(i, lo + e * GC) for e in range(4)]


BLOCK0 = block_from_plus(0, after(1, 0))
BLOCK1 = block_from_plus(2, after(2, BR + 2 * GC))
BLOCK2 = block_from_minus(0, after(0, BR + 2 * GC))
BLOCK3 = (
    [(1, 0, HB), (2, 0, HB)],
    [(1, HB), (1, HB + GC), (2, HB), (2, HB + GC)],
)


def message(first, second, e):
    out, at = [], 0
    for i, lo, n in first[0]:
        out.append((i, lo, n, at))
        at += n
    out.append((*first[1][2], GC, at))
    at += GC
    for i, lo, n in second[0]:
        out.append((i, lo, n, at))
        at += n
    for blk in (first, second):
        out.append((*blk[1][e], GC, at))
        at += GC
    return out


def assemble_kernel(plans, n_in, *refs):
    ins, outs = refs[:n_in], refs[n_in:]
    for plan, out in zip(plans, outs):
        for src, lo, n, at in plan:
            out[at : at + n, :] = ins[src][lo : lo + n, :]


def assemble(first, second, *ins):
    plans = (message(first, second, 1), message(second, first, 3))
    return pl.pallas_call(
        lambda *r: assemble_kernel(plans, len(ins), *r),
        out_shape=(jax.ShapeDtypeStruct((MR, M), BF16),) * 2,
        in_specs=[VM] * len(ins),
        out_specs=(VM,) * 2,
        compiler_params=params(),
        name="assemble",
    )(*ins)


def coefs(rows, per, v):
    row = lax.broadcasted_iota(jnp.int32, (rows, M), 0)
    c = jnp.zeros((rows, M), jnp.int32)
    for i in range(1, C):
        c = c + (row >= per * i).astype(jnp.int32)
    base = jnp.where((c == 1) | (c == 4) | (c == 7), 2.0, 1.0)
    return jnp.where(c < 3, base, -base * v)


ACCS = ((RU, CU), (RU, CU), (RU, 2 * K), (CU, K), (CU, K), (K + 16, K))


def chunk_kernel(blocks, n_in, n_acc, *refs):
    arrs, ins = refs[:n_in], refs[n_in : n_in + n_acc]
    outs, (jac, wg) = refs[n_in + n_acc : -2], refs[-2:]
    for blk, (hs, tl, cl) in enumerate(blocks):
        tail = arrs[tl[0]][tl[1] : tl[1] + 128, :].astype(F32)
        v = tail[117:118, :]
        lanes = slice(blk * M, (blk + 1) * M)
        wg[blk, 0:108, :] = tail[0:108, :] * coefs(108, LR, v)
        wg[blk, 176:185, :] = tail[108:117, :] * coefs(C, 1, v)
        gc = arrs[cl[0]][cl[1] : cl[1] + GC, :].astype(F32)
        wg[blk, 112:176, :] = gc * coefs(GC, 6, v)
        jac[J_R:JR, lanes] = jnp.zeros((JR - J_R, M), BF16)
        first_row = lax.broadcasted_iota(jnp.int32, (16, M), 0) == 0
        jac[J_R : J_R + 16, lanes] = jnp.where(first_row, tail[118:119, :], 0.0).astype(BF16)

    for blk, (hs, tl, cl) in enumerate(blocks):
        lanes = slice(blk * M, (blk + 1) * M)

        def slab(t, carry, hs=hs, lanes=lanes, blk=blk):
            base = pl.multiple_of(t * 16, 16)
            h = [arrs[i][pl.ds(lo + base, 16), :].astype(F32) for i, lo in hs]

            def unit(rows, dst):
                acc = wg[blk, rows[0] : rows[0] + 1, :] * h[0]
                for c in range(1, C):
                    acc = acc + wg[blk, rows[c] : rows[c] + 1, :] * h[c]
                jac[pl.ds(dst + base, 16), lanes] = acc.astype(BF16)

            for u in range(LR):
                unit([c * LR + u for c in range(C)], u * K)
            for u in range(6):
                unit([112 + c * 6 + u for c in range(C)], RU + u * K)
            unit([176 + c for c in range(C)], J_K)
            return carry

        lax.fori_loop(0, K // 16, slab, 0)

    def acc(i, rows, cols, val):
        if n_acc:
            val = val + ins[i][rows, cols]
        outs[i][rows, cols] = val

    al = slice(None)
    pd = lax.dot_general(jac[RU : J_R + 16, :], jac[J_K:J_R, :], NT, preferred_element_type=F32)
    acc(3, al, al, pd[0:CU])
    acc(4, al, al, pd[CU : 2 * CU])
    acc(5, al, al, pd[2 * CU :])
    tile = 512
    for n in (3, 0, 1, 2):
        for m in range(RU // tile):
            rows = slice(m * tile, (m + 1) * tile)
            val = lax.dot_general(
                jac[rows, :], jac[RU + n * 256 : RU + (n + 1) * 256, :], NT,
                preferred_element_type=F32,
            )
            if n == 0:
                acc(0, rows, slice(0, 256), val)
            elif n == 1:
                acc(0, rows, slice(256, 384), val[:, :128])
                acc(1, rows, slice(0, 128), val[:, 128:])
            elif n == 2:
                acc(1, rows, slice(128, 384), val)
            else:
                acc(2, rows, al, val)


def chunk(blocks, arrs, accs, name):
    n = len(blocks)
    return pl.pallas_call(
        lambda *r: chunk_kernel(blocks, len(arrs), len(accs), *r),
        out_shape=tuple(jax.ShapeDtypeStruct(s, F32) for s in ACCS),
        in_specs=[VM] * (len(arrs) + len(accs)),
        out_specs=(VM,) * len(ACCS),
        scratch_shapes=[pltpu.VMEM((JR, n * M), BF16), pltpu.VMEM((n, 192, M), F32)],
        compiler_params=params(),
        cost_estimate=pl.CostEstimate(
            flops=n * 2 * JR * K * (RU + C), bytes_accessed=n * 4_000_000, transcendentals=0
        ),
        name=name,
    )(*arrs, *accs)


def place(block, e, shift):
    hs, rows = [], [(i, lo + r) for i, lo, n in block[0] for r in range(0, n, K)]
    rows = [(i + shift, lo) for i, lo in rows]
    i, lo = block[1][e]
    return rows[:C], rows[C], (i + shift, lo)


def received(i, col):
    two = []
    for b in range(2):
        lo = b * (BR + GC)
        two.append(([(i, lo + c * K) for c in range(C)], (i, lo + HR), (i, col + b * GC)))
    return two


def chol_kernel(a_ref, b_ref, d_ref, chol_ref, w_ref, yz_ref, m_ref, u_ref):
    row = lax.broadcasted_iota(jnp.int32, (K, K), 0)
    col = lax.broadcasted_iota(jnp.int32, (K, K), 1)
    eye = row == col
    gram = (a_ref[0:K, :] + b_ref[0:K, :]) * (1.0 / TOTAL)
    m_ref[:, :K] = gram + jnp.where(eye, d_ref[0:1, :], 0.0)
    m_ref[:, K:] = jnp.where(eye, 1.0, 0.0)
    sub = lax.broadcasted_iota(jnp.int32, (8, K), 0)
    pick = lambda v, r: jnp.broadcast_to(v[r : r + 1, :], (8, v.shape[1]))
    for b in range(K // 8):
        lo = 8 * b
        p = m_ref[lo : lo + 8, :]
        left, right = p[:, :K], p[:, K:]
        cols = [jnp.broadcast_to(p[:, lo + c : lo + c + 1], (8, K)) for c in range(8)]
        scale = jnp.ones((8, K), F32)
        for r in range(8):
            rs = lax.rsqrt(pick(cols[r], r))
            mult = jnp.where(sub > r, cols[r] * (rs * rs), 0.0)
            for c in range(r + 1, 8):
                cols[c] = cols[c] - mult * pick(cols[c], r)
            scale = jnp.where(sub == r, rs, scale)
            left = left - mult * pick(left, r)
            right = right - mult * pick(right, r)
        p = jnp.concatenate([left * scale, right * scale], axis=1)
        u_ref[lo : lo + 8, :] = p
        if b < K // 8 - 1:
            ut = p[:, :K].T
            rows = [pick(p, r) for r in range(8)]
            for t in range(b + 1, K // 8):
                at = slice(8 * t, 8 * t + 8)
                acc = m_ref[at, :]
                for r in range(8):
                    acc = acc - jnp.broadcast_to(ut[at, r : r + 1], (8, 2 * K)) * rows[r]
                m_ref[at, :] = acc
    chol_ref[...] = jnp.where(col >= row, u_ref[:, :K], 0.0).T
    w = u_ref[:, K:]
    w_ref[...] = w
    g = (a_ref[K : K + 8, :] + b_ref[K : K + 8, :]) * (1.0 / TOTAL)
    y = lax.dot_general(g, w, NT, precision=HI, preferred_element_type=F32)
    z = lax.dot_general(y, w, (((1,), (0,)), ((), ())), precision=HI, preferred_element_type=F32)
    yz_ref[0:8, :] = y
    yz_ref[8:16, :] = z


def cholesky(dk, dk2, damp):
    return pl.pallas_call(
        chol_kernel,
        out_shape=(
            jax.ShapeDtypeStruct((K, K), F32),
            jax.ShapeDtypeStruct((K, K), F32),
            jax.ShapeDtypeStruct((16, K), F32),
        ),
        in_specs=[VM] * 3,
        out_specs=(VM,) * 3,
        scratch_shapes=[pltpu.VMEM((K, 2 * K), F32), pltpu.VMEM((K, 2 * K), F32)],
        compiler_params=params(),
        name="panel_factor",
    )(dk, dk2, damp)


def halves(v):
    hi = v.astype(BF16)
    return hi, (v - hi.astype(F32)).astype(BF16)


def panel_kernel(k_ref, p_ref, pr_ref, po_ref, por_ref, w_ref, yz_ref, dir_ref, lpan_ref, la_ref, lb_ref):
    q, k = lax.axis_index("row"), k_ref[0]
    inv = 1.0 / TOTAL
    w_hi, w_lo = halves(w_ref[...])
    wb = jnp.concatenate([w_hi, w_lo, w_hi], axis=1)
    sub = lax.broadcasted_iota(jnp.int32, (8, 2 * K), 0)
    lane = lax.broadcasted_iota(jnp.int32, (8, 2 * K), 1)
    z = yz_ref[8:9, :]
    z2 = jnp.concatenate([z, jnp.zeros_like(z)], axis=1)
    lhs = jnp.where(lane == K, 1.0, jnp.where(sub == 0, -z2, 0.0))

    def solve(p):
        hi, lo = halves(p)
        return lax.dot_general(
            jnp.concatenate([hi, hi, lo], axis=1), wb, NT, preferred_element_type=F32
        )

    for lr in range(LR):
        rows = slice(lr * K, (lr + 1) * K)
        pe = (p_ref[rows, :] + pr_ref[rows, :]) * inv
        d = lax.dot_general(lhs, pe, NT, precision=HI, preferred_element_type=F32)
        i = lr * NZ + q
        dir_ref[lr : lr + 1, :] = jnp.where(
            i == k, yz_ref[0:1, :], jnp.where(i > k, d[0:1, :], d[1:2, :])
        )
        lpan = solve(pe[:, :K])
        lpan_ref[rows, :] = lpan
        hi, lo = halves(lpan)
        la_ref[rows, :] = jnp.concatenate([hi, hi, lo], axis=1)
    hi, lo = halves(solve((po_ref[...] + por_ref[...]) * inv))
    lb_ref[...] = jnp.concatenate([hi, lo, hi], axis=1)


def panel_solve(k, p, pr, po, por, w, yz):
    return pl.pallas_call(
        panel_kernel,
        out_shape=(
            jax.ShapeDtypeStruct((LR, K), F32),
            jax.ShapeDtypeStruct((RU, K), F32),
            jax.ShapeDtypeStruct((RU, 3 * K), BF16),
            jax.ShapeDtypeStruct((CU, 3 * K), BF16),
        ),
        in_specs=[SMEM] + [VM] * 6,
        out_specs=(VM,) * 4,
        compiler_params=params(),
        name="panel_solve",
    )(k, p, pr, po, por, w, yz)


def final_kernel(start, k_ref, g_ref, gr_ref, la_ref, lb_ref, lpan_ref, chol_ref, damp_ref, *refs):
    out_ref = refs[-1]
    q, k = lax.axis_index("row"), k_ref[0]
    s = (lax.axis_index("x") * NY + lax.axis_index("y")) * NC + lax.axis_index("core")
    lr = start + pl.program_id(0)
    i = lr * NZ + q
    upd = lax.dot_general(la_ref[...], lb_ref[...], NT, preferred_element_type=F32)
    gram = (g_ref[...] + gr_ref[...]) * (1.0 / TOTAL)
    row = lax.broadcasted_iota(jnp.int32, (K, K), 0)
    col = lax.broadcasted_iota(jnp.int32, (K, K), 1)
    damp = damp_ref[pl.ds(lr, 1), :]
    for lc in range(LC):
        j = lc * (NX * NY * NC) + s
        gt = gram[:, lc * K : (lc + 1) * K] + jnp.where((row == col) & (i == j), damp, 0.0)
        val = jnp.where(
            (i > k) & (j > k),
            gt - upd[:, lc * K : (lc + 1) * K],
            jnp.where(
                (i > k) & (j == k),
                lpan_ref[...],
                jnp.where((i == k) & (j == k), chol_ref[...], gt),
            ),
        )
        out_ref[pl.ds(lc, K, stride=LC), :] = val


def final(start, count, k, gown, grecv, la, lb, lpan, chol, damp, *prev):
    full = lambda shape: pl.BlockSpec(shape, lambda i: (0,) * len(shape))
    rows = lambda width: pl.BlockSpec((K, width), lambda i: (i + start, 0))
    return pl.pallas_call(
        lambda *r: final_kernel(start, *r),
        grid=(count,),
        out_shape=jax.ShapeDtypeStruct((RU * LC, K), F32),
        in_specs=[
            SMEM, rows(CU), rows(CU), rows(3 * K), full((CU, 3 * K)), rows(K), full((K, K)),
            full((LR, K)),
        ] + [pl.BlockSpec(memory_space=pl.ANY)] * len(prev),
        out_specs=pl.BlockSpec((K * LC, K), lambda i: (i + start, 0)),
        input_output_aliases={8: 0} if prev else {},
        compiler_params=params(),
        cost_estimate=pl.CostEstimate(
            flops=1, bytes_accessed=6000000, transcendentals=0
        ),
        name="trailing_update",
    )(k, gown, grecv, la, lb, lpan, chol, damp, *prev)


def device(x, y, c, z):
    return ((x * NY + y) * NC + c) * NZ + z


def hops(along_x_core, d):
    pairs = []
    for x in range(NX):
        for y in range(NY):
            for c in range(NC):
                for z in range(NZ):
                    to = ((x + d) % NX, y) if c == along_x_core else (x, (y + d) % NY)
                    pairs.append((device(x, y, c, z), device(*to, c, z)))
    return pairs


def body(g_jets, layer_input_jets, speed, resid, point_index, damping, panel):
    q = lax.axis_index("row")
    k = panel[0]
    one = lambda v, d: lax.ppermute(v, AXES, hops(0, d))
    two = lambda v, d: lax.ppermute(v, AXES, hops(1, d))
    swap = lambda v: lax.ppermute(v, "core", [(0, 1), (1, 0)])
    zbit = lambda v, bit: v + lax.ppermute(v, "row", [(i, i ^ bit) for i in range(NZ)])
    bar = lax.optimization_barrier

    plus, minus, own = pack(
        panel,
        point_index.reshape(1, M),
        layer_input_jets.reshape(HR, POOL),
        g_jets.transpose(1, 0, 2).reshape(C * A, POOL),
        speed.reshape(2, M),
        resid.reshape(2, M),
    )
    dsel = lax.dynamic_index_in_dim(damping[:, 0, :], k // NZ, 0, keepdims=True)
    dsel = jnp.broadcast_to(jnp.where(k % NZ == q, dsel, 0.0), (8, K))
    parts = [dsel]
    for bits in (1, 2, 3):
        parts.append(lax.ppermute(dsel, "row", [(i, i ^ bits) for i in range(NZ)]))
    dsel = parts[0] + parts[1] + parts[2] + parts[3]
    accs = chunk([place(BLOCK0, 0, 0)], (plus, own), (), "chunk_own")
    ap, am, accs, dsel = bar((one(plus, 1), one(minus, -1), accs, dsel))
    m1 = assemble(BLOCK0, BLOCK1, plus, own, ap)
    relay = HB + 2 * GC
    rp, rm = one(ap[:relay], 1), one(am[:relay], -1)
    m1p, m1m = two(m1[0], 1), two(m1[1], -1)
    accs = chunk([place(BLOCK1, 0, -2), place(BLOCK2, 0, 1)], (ap, am), accs, "chunk_line1")
    rp, rm, accs, dsel = bar((rp, rm, accs, zbit(dsel, 4)))
    m2 = assemble(BLOCK2, BLOCK3, am, rp, rm)
    m2p, m2m = two(m2[0], 1), two(m2[1], -1)
    n1 = BR + GC
    r1p, r1m = two(m1p[:n1], 1), two(m1m[:n1], -1)
    e1 = 2 * BR + GC
    blocks = received(0, e1) + received(1, e1) + [place(BLOCK3, 0, 1)]
    accs = chunk(blocks, (m1p, m1m, rp, rm), accs, "chunk_line2")
    r1p, r1m, m2p, m2m, accs = bar((r1p, r1m, m2p, m2m, accs))
    r2p, r2m = two(m2p[:n1], 1), two(m2m[:n1], -1)
    blocks = [received(0, BR)[0], received(1, BR)[0]] + received(2, e1) + received(3, e1)
    accs = chunk(blocks, (r1p, r1m, m2p, m2m), accs, "chunk_far1")
    far = [received(0, BR)[0], received(1, BR)[0]]
    accs = chunk(far, (r2p, r2m), accs, "chunk_far2")
    gown, gsib, p, po, ps, dk = accs

    dk2, p, ps, gsib = bar((swap(dk), p, ps, gsib))
    chol, w, yz = cholesky(dk, dk2, dsel)
    pr, por, gr, w = bar((swap(p), swap(ps), swap(gsib), w))
    mine, lpan, la, lb = panel_solve(panel, p, pr, po, por, w, yz)
    slot = lax.broadcasted_iota(jnp.int32, (1, NZ, 1), 1)
    full = jnp.where(slot == q, mine[:, None, :], 0.0)
    for bits in (1, 2, 3):
        other = lax.ppermute(mine, "row", [(i, i ^ bits) for i in range(NZ)])
        full = jnp.where(slot == q ^ bits, other[:, None, :], full)
    rest = (panel, gown, gr, la, lb, lpan, chol, damping[:, 0, :])
    fac = final(0, 8, *rest)
    full, fac = bar((full, fac))
    fac = final(8, 4, *rest, fac)
    full = zbit(full, 4)
    return fac.reshape(LR, 1, K, LC, 1, K), full.reshape(-1)


def solution(mesh):
    grid = Mesh(mesh.devices.reshape(NX, NY, NC, NZ), AXES)
    pts = ("x", "y", "core")
    in_specs = (
        P(None, None, pts),
        P(None, None, pts),
        P(pts),
        P(pts),
        P(pts),
        P(None, "row", None),
        P(),
    )
    out_specs = (P(None, "row", None, None, pts, None), P())
    return jax.shard_map(body, mesh=grid, in_specs=in_specs, out_specs=out_specs, check_vma=False)
```

```python
import jax
import jax.numpy as jnp
from jax import lax
from jax.experimental import pallas as pl
from jax.experimental.pallas import tpu as pltpu
from jax.sharding import Mesh, PartitionSpec as P

NX, NY, NC, NZ = 4, 4, 2, 8
A, K, C, POOL, M = 96, 128, 9, 256, 128
LR, LC = 12, 3
TOTAL = 4096
HR = C * K
BR = 1280
ROWG, KG, VR, RR = HR, HR + 108, HR + 117, HR + 118
GC = 64
HB = BR // 2
PR = BR + 6 * GC
MR = 2 * BR + 3 * GC
RU, CU = LR * K, LC * K
JR = RU + 2 * CU + 2 * K
J_K, J_R = RU + 2 * CU, RU + 2 * CU + K
F32, BF16 = jnp.float32, jnp.bfloat16
AXES = ("x", "y", "core", "row")
HI = lax.Precision.HIGHEST
NT = (((1,), (1,)), ((), ()))
TN = (((0,), (0,)), ((), ()))
VMEM_LIMIT = 20 * 1024 * 1024
SMEM = pl.BlockSpec(memory_space=pltpu.SMEM)
VM = pl.BlockSpec(memory_space=pltpu.VMEM)
HBM = pl.BlockSpec(memory_space=pltpu.HBM)


def params():
    return pltpu.CompilerParams(vmem_limit_bytes=VMEM_LIMIT)


def pack_kernel(
    k_ref, idx_hbm, h_hbm, g_hbm, v_hbm, r_hbm, plus_ref, minus_ref, own_ref,
    gs, tail, cbuf, idx_ref, h_ref, g_ref, v_ref, r_ref, sem,
):
    copies = [
        pltpu.make_async_copy(src, dst, sem.at[i])
        for i, (src, dst) in enumerate(
            (
                (idx_hbm, idx_ref), (v_hbm, v_ref), (r_hbm, r_ref), (g_hbm, g_ref), (h_hbm, h_ref),
            )
        )
    ]
    for cp in copies:
        cp.start()
    x, y = lax.axis_index("x"), lax.axis_index("y")
    core, q = lax.axis_index("core"), lax.axis_index("row")
    k = k_ref[0]
    pool = lax.broadcasted_iota(jnp.int32, (POOL, M), 0)
    copies[0].wait()
    sel = (pool == idx_ref[...]).astype(F32).astype(BF16)
    for cp in copies[1:]:
        cp.wait()
    for c in range(C):
        val = jnp.dot(h_ref[c * K : (c + 1) * K, :], sel, preferred_element_type=F32).astype(BF16)
        lo = c * K if c < 5 else c * K + 2 * GC
        plus_ref[lo : lo + K, :] = val
        lo = c * K + HB + 2 * GC if c < 5 else c * K - HB
        minus_ref[lo : lo + K, :] = val
    for c in range(C):
        gs[c * A : (c + 1) * A, :] = jnp.dot(
            g_ref[c * A : (c + 1) * A, :], sel, preferred_element_type=F32
        )
    tail[...] = jnp.zeros_like(tail)
    for c in range(C):
        tail[c * LR : (c + 1) * LR, :] = gs[pl.ds(c * A + q, LR, stride=NZ), :]
        tail[108 + c : 109 + c, :] = gs[pl.ds(c * A + k, 1), :]
    for i, ref in enumerate((v_ref, r_ref)):
        low = jnp.dot(ref[...], sel[:M], preferred_element_type=F32)
        high = jnp.dot(ref[...], sel[M:], preferred_element_type=F32)
        tail[117 + i : 118 + i, :] = low[0:1] + high[1:2]
    val = tail[...].astype(BF16)
    plus_ref[HR + 2 * GC : BR + 2 * GC, :] = val
    minus_ref[HR - HB : HB, :] = val
    cbuf[...] = jnp.zeros_like(cbuf)
    for dp in range(4):
        for dt in range(4):
            px = lax.rem(jnp.where(core == 0, x + dp, x + dt), NX)
            py = lax.rem(jnp.where(core == 0, y + dt, y + dp), NY)
            d = px * NY + py
            for c in range(C):
                for o in range(2):
                    cc = core if o == 0 else 1 - core
                    for lc in range(LC):
                        row = c * 6 + o * LC + lc
                        cbuf[row : row + 1, :] = gs[pl.ds(c * A + lc * 32 + 2 * d + cc, 1), :]
            val = cbuf[...].astype(BF16)
            if dp == 0:
                own_ref[dt * GC : (dt + 1) * GC, :] = val
            elif dp == 1:
                plus_ref[BR + (2 + dt) * GC : BR + (3 + dt) * GC, :] = val
            elif dp == 3:
                minus_ref[BR + (2 + dt) * GC : BR + (3 + dt) * GC, :] = val
            elif dt < 2:
                plus_ref[HB + dt * GC : HB + (dt + 1) * GC, :] = val
            else:
                minus_ref[HB + (dt - 2) * GC : HB + (dt - 1) * GC, :] = val


def pack(k, idx, h, g, v, r):
    return pl.pallas_call(
        pack_kernel,
        out_shape=(
            jax.ShapeDtypeStruct((PR, M), BF16),
            jax.ShapeDtypeStruct((PR, M), BF16),
            jax.ShapeDtypeStruct((4 * GC, M), BF16),
        ),
        in_specs=[SMEM] + [HBM] * 5,
        out_specs=(VM,) * 3,
        scratch_shapes=[
            pltpu.VMEM((C * A, M), F32),
            pltpu.VMEM((128, M), F32),
            pltpu.VMEM((GC, M), F32),
            pltpu.VMEM((1, M), jnp.int32),
            pltpu.VMEM((HR, POOL), BF16),
            pltpu.VMEM((C * A, POOL), BF16),
            pltpu.VMEM((2, M), BF16),
            pltpu.VMEM((2, M), BF16),
            pltpu.SemaphoreType.DMA((5,)),
        ],
        compiler_params=pltpu.CompilerParams(vmem_limit_bytes=60 * 1024 * 1024),
        name="pack",
    )(k, idx, h, g, v, r)


def block_from_plus(i, cols):
    return ([(i, 0, HB), (i, HB + 2 * GC, HB)], cols)


def block_from_minus(i, cols):
    return ([(i, HB + 2 * GC, HB), (i, 0, HB)], cols)


def after(i, lo):
    return [(i, lo + e * GC) for e in range(4)]


BLOCK0 = block_from_plus(0, after(1, 0))
BLOCK1 = block_from_plus(2, after(2, BR + 2 * GC))
BLOCK2 = block_from_minus(0, after(0, BR + 2 * GC))
BLOCK3 = (
    [(1, 0, HB), (2, 0, HB)],
    [(1, HB), (1, HB + GC), (2, HB), (2, HB + GC)],
)


def message(first, second, e):
    out, at = [], 0
    for i, lo, n in first[0]:
        out.append((i, lo, n, at))
        at += n
    out.append((*first[1][2], GC, at))
    at += GC
    for i, lo, n in second[0]:
        out.append((i, lo, n, at))
        at += n
    for blk in (first, second):
        out.append((*blk[1][e], GC, at))
        at += GC
    return out


def assemble_kernel(plans, n_in, *refs):
    ins, outs = refs[:n_in], refs[n_in:]
    for plan, out in zip(plans, outs):
        for src, lo, n, at in plan:
            out[at : at + n, :] = ins[src][lo : lo + n, :]


def assemble(first, second, *ins):
    plans = (message(first, second, 1), message(second, first, 3))
    return pl.pallas_call(
        lambda *r: assemble_kernel(plans, len(ins), *r),
        out_shape=(jax.ShapeDtypeStruct((MR, M), BF16),) * 2,
        in_specs=[VM] * len(ins),
        out_specs=(VM,) * 2,
        compiler_params=params(),
        name="assemble",
    )(*ins)


def coefs(rows, per, v):
    row = lax.broadcasted_iota(jnp.int32, (rows, M), 0)
    c = jnp.zeros((rows, M), jnp.int32)
    for i in range(1, C):
        c = c + (row >= per * i).astype(jnp.int32)
    base = jnp.where((c == 1) | (c == 4) | (c == 7), 2.0, 1.0)
    return jnp.where(c < 3, base, -base * v)


ACCS = ((RU, CU), (RU, CU), (RU, 2 * K), (CU, K), (CU, K), (K + 16, K))


def chunk_kernel(blocks, n_in, n_acc, *refs):
    arrs, ins = refs[:n_in], refs[n_in : n_in + n_acc]
    outs, (jac, wg) = refs[n_in + n_acc : -2], refs[-2:]
    for blk, (hs, tl, cl) in enumerate(blocks):
        tail = arrs[tl[0]][tl[1] : tl[1] + 128, :].astype(F32)
        v = tail[117:118, :]
        lanes = slice(blk * M, (blk + 1) * M)
        wg[blk, 0:108, :] = tail[0:108, :] * coefs(108, LR, v)
        wg[blk, 176:185, :] = tail[108:117, :] * coefs(C, 1, v)
        gc = arrs[cl[0]][cl[1] : cl[1] + GC, :].astype(F32)
        wg[blk, 112:176, :] = gc * coefs(GC, 6, v)
        jac[J_R:JR, lanes] = jnp.zeros((JR - J_R, M), BF16)
        first_row = lax.broadcasted_iota(jnp.int32, (16, M), 0) == 0
        jac[J_R : J_R + 16, lanes] = jnp.where(first_row, tail[118:119, :], 0.0).astype(BF16)

    for blk, (hs, tl, cl) in enumerate(blocks):
        lanes = slice(blk * M, (blk + 1) * M)

        def slab(t, carry, hs=hs, lanes=lanes, blk=blk):
            base = pl.multiple_of(t * 16, 16)
            h = [arrs[i][pl.ds(lo + base, 16), :].astype(F32) for i, lo in hs]

            def unit(rows, dst):
                acc = wg[blk, rows[0] : rows[0] + 1, :] * h[0]
                for c in range(1, C):
                    acc = acc + wg[blk, rows[c] : rows[c] + 1, :] * h[c]
                jac[pl.ds(dst + base, 16), lanes] = acc.astype(BF16)

            for u in range(LR):
                unit([c * LR + u for c in range(C)], u * K)
            for u in range(6):
                unit([112 + c * 6 + u for c in range(C)], RU + u * K)
            unit([176 + c for c in range(C)], J_K)
            return carry

        lax.fori_loop(0, K // 16, slab, 0)

    def acc(i, rows, cols, val):
        if n_acc:
            val = val + ins[i][rows, cols]
        outs[i][rows, cols] = val

    al = slice(None)
    pd = lax.dot_general(jac[RU : J_R + 16, :], jac[J_K:J_R, :], NT, preferred_element_type=F32)
    acc(3, al, al, pd[0:CU])
    acc(4, al, al, pd[CU : 2 * CU])
    acc(5, al, al, pd[2 * CU :])
    tile = 512
    for n in (3, 0, 1, 2):
        for m in range(RU // tile):
            rows = slice(m * tile, (m + 1) * tile)
            val = lax.dot_general(
                jac[rows, :], jac[RU + n * 256 : RU + (n + 1) * 256, :], NT,
                preferred_element_type=F32,
            )
            if n == 0:
                acc(0, rows, slice(0, 256), val)
            elif n == 1:
                acc(0, rows, slice(256, 384), val[:, :128])
                acc(1, rows, slice(0, 128), val[:, 128:])
            elif n == 2:
                acc(1, rows, slice(128, 384), val)
            else:
                acc(2, rows, al, val)


def chunk(blocks, arrs, accs, name):
    n = len(blocks)
    return pl.pallas_call(
        lambda *r: chunk_kernel(blocks, len(arrs), len(accs), *r),
        out_shape=tuple(jax.ShapeDtypeStruct(s, F32) for s in ACCS),
        in_specs=[VM] * (len(arrs) + len(accs)),
        out_specs=(VM,) * len(ACCS),
        scratch_shapes=[pltpu.VMEM((JR, n * M), BF16), pltpu.VMEM((n, 192, M), F32)],
        compiler_params=params(),
        cost_estimate=pl.CostEstimate(
            flops=n * 2 * JR * K * (RU + C), bytes_accessed=n * 4_000_000, transcendentals=0
        ),
        name=name,
    )(*arrs, *accs)


def place(block, e, shift):
    hs, rows = [], [(i, lo + r) for i, lo, n in block[0] for r in range(0, n, K)]
    rows = [(i + shift, lo) for i, lo in rows]
    i, lo = block[1][e]
    return rows[:C], rows[C], (i + shift, lo)


def received(i, col):
    two = []
    for b in range(2):
        lo = b * (BR + GC)
        two.append(([(i, lo + c * K) for c in range(C)], (i, lo + HR), (i, col + b * GC)))
    return two


def chol_kernel(a_ref, b_ref, d_ref, chol_ref, w_ref, yz_ref, m_ref, u_ref):
    row = lax.broadcasted_iota(jnp.int32, (K, K), 0)
    col = lax.broadcasted_iota(jnp.int32, (K, K), 1)
    eye = row == col
    gram = (a_ref[0:K, :] + b_ref[0:K, :]) * (1.0 / TOTAL)
    m_ref[:, :K] = gram + jnp.where(eye, d_ref[0:1, :], 0.0)
    m_ref[:, K:] = jnp.where(eye, 1.0, 0.0)
    sub = lax.broadcasted_iota(jnp.int32, (8, K), 0)
    pick = lambda v, r: jnp.broadcast_to(v[r : r + 1, :], (8, v.shape[1]))
    for b in range(K // 8):
        lo = 8 * b
        p = m_ref[lo : lo + 8, :]
        left, right = p[:, :K], p[:, K:]
        cols = [jnp.broadcast_to(p[:, lo + c : lo + c + 1], (8, K)) for c in range(8)]
        scale = jnp.ones((8, K), F32)
        for r in range(8):
            rs = lax.rsqrt(pick(cols[r], r))
            mult = jnp.where(sub > r, cols[r] * (rs * rs), 0.0)
            for c in range(r + 1, 8):
                cols[c] = cols[c] - mult * pick(cols[c], r)
            scale = jnp.where(sub == r, rs, scale)
            left = left - mult * pick(left, r)
            right = right - mult * pick(right, r)
        p = jnp.concatenate([left * scale, right * scale], axis=1)
        u_ref[lo : lo + 8, :] = p
        if b < K // 8 - 1:
            ut = p[:, :K].T
            rows = [pick(p, r) for r in range(8)]
            for t in range(b + 1, K // 8):
                at = slice(8 * t, 8 * t + 8)
                acc = m_ref[at, :]
                for r in range(8):
                    acc = acc - jnp.broadcast_to(ut[at, r : r + 1], (8, 2 * K)) * rows[r]
                m_ref[at, :] = acc
    chol_ref[...] = jnp.where(col >= row, u_ref[:, :K], 0.0).T
    w = u_ref[:, K:]
    w_ref[...] = w
    g = (a_ref[K : K + 8, :] + b_ref[K : K + 8, :]) * (1.0 / TOTAL)
    y = lax.dot_general(g, w, NT, precision=HI, preferred_element_type=F32)
    z = lax.dot_general(y, w, (((1,), (0,)), ((), ())), precision=HI, preferred_element_type=F32)
    yz_ref[0:8, :] = y
    yz_ref[8:16, :] = z


def cholesky(dk, dk2, damp):
    return pl.pallas_call(
        chol_kernel,
        out_shape=(
            jax.ShapeDtypeStruct((K, K), F32),
            jax.ShapeDtypeStruct((K, K), F32),
            jax.ShapeDtypeStruct((16, K), F32),
        ),
        in_specs=[VM] * 3,
        out_specs=(VM,) * 3,
        scratch_shapes=[pltpu.VMEM((K, 2 * K), F32), pltpu.VMEM((K, 2 * K), F32)],
        compiler_params=params(),
        name="panel_factor",
    )(dk, dk2, damp)


def halves(v):
    hi = v.astype(BF16)
    return hi, (v - hi.astype(F32)).astype(BF16)


def panel_kernel(k_ref, p_ref, pr_ref, po_ref, por_ref, w_ref, yz_ref, dir_ref, lpan_ref, la_ref, lb_ref):
    q, k = lax.axis_index("row"), k_ref[0]
    inv = 1.0 / TOTAL
    w_hi, w_lo = halves(w_ref[...])
    wb = jnp.concatenate([w_hi, w_lo, w_hi], axis=1)
    sub = lax.broadcasted_iota(jnp.int32, (8, 2 * K), 0)
    lane = lax.broadcasted_iota(jnp.int32, (8, 2 * K), 1)
    z = yz_ref[8:9, :]
    z2 = jnp.concatenate([z, jnp.zeros_like(z)], axis=1)
    lhs = jnp.where(lane == K, 1.0, jnp.where(sub == 0, -z2, 0.0))

    def solve(p):
        hi, lo = halves(p)
        return lax.dot_general(
            jnp.concatenate([hi, hi, lo], axis=1), wb, NT, preferred_element_type=F32
        )

    for lr in range(LR):
        rows = slice(lr * K, (lr + 1) * K)
        pe = (p_ref[rows, :] + pr_ref[rows, :]) * inv
        d = lax.dot_general(lhs, pe, NT, precision=HI, preferred_element_type=F32)
        i = lr * NZ + q
        dir_ref[lr : lr + 1, :] = jnp.where(
            i == k, yz_ref[0:1, :], jnp.where(i > k, d[0:1, :], d[1:2, :])
        )
        lpan = solve(pe[:, :K])
        lpan_ref[rows, :] = lpan
        hi, lo = halves(lpan)
        la_ref[rows, :] = jnp.concatenate([hi, hi, lo], axis=1)
    hi, lo = halves(solve((po_ref[...] + por_ref[...]) * inv))
    lb_ref[...] = jnp.concatenate([hi, lo, hi], axis=1)


def panel_solve(k, p, pr, po, por, w, yz):
    return pl.pallas_call(
        panel_kernel,
        out_shape=(
            jax.ShapeDtypeStruct((LR, K), F32),
            jax.ShapeDtypeStruct((RU, K), F32),
            jax.ShapeDtypeStruct((RU, 3 * K), BF16),
            jax.ShapeDtypeStruct((CU, 3 * K), BF16),
        ),
        in_specs=[SMEM] + [VM] * 6,
        out_specs=(VM,) * 4,
        compiler_params=params(),
        name="panel_solve",
    )(k, p, pr, po, por, w, yz)


def final_kernel(start, k_ref, g_ref, gr_ref, la_ref, lb_ref, lpan_ref, chol_ref, damp_ref, *refs):
    out_ref = refs[-1]
    q, k = lax.axis_index("row"), k_ref[0]
    s = (lax.axis_index("x") * NY + lax.axis_index("y")) * NC + lax.axis_index("core")
    lr = start + pl.program_id(0)
    i = lr * NZ + q
    upd = lax.dot_general(la_ref[...], lb_ref[...], NT, preferred_element_type=F32)
    gram = (g_ref[...] + gr_ref[...]) * (1.0 / TOTAL)
    row = lax.broadcasted_iota(jnp.int32, (K, K), 0)
    col = lax.broadcasted_iota(jnp.int32, (K, K), 1)
    damp = damp_ref[pl.ds(lr, 1), :]
    for lc in range(LC):
        j = lc * (NX * NY * NC) + s
        gt = gram[:, lc * K : (lc + 1) * K] + jnp.where((row == col) & (i == j), damp, 0.0)
        val = jnp.where(
            (i > k) & (j > k),
            gt - upd[:, lc * K : (lc + 1) * K],
            jnp.where(
                (i > k) & (j == k),
                lpan_ref[...],
                jnp.where((i == k) & (j == k), chol_ref[...], gt),
            ),
        )
        out_ref[pl.ds(lc, K, stride=LC), :] = val


def final(start, count, k, gown, grecv, la, lb, lpan, chol, damp, *prev):
    full = lambda shape: pl.BlockSpec(shape, lambda i: (0,) * len(shape))
    rows = lambda width: pl.BlockSpec((K, width), lambda i: (i + start, 0))
    return pl.pallas_call(
        lambda *r: final_kernel(start, *r),
        grid=(count,),
        out_shape=jax.ShapeDtypeStruct((RU * LC, K), F32),
        in_specs=[
            SMEM, rows(CU), rows(CU), rows(3 * K), full((CU, 3 * K)), rows(K), full((K, K)),
            full((LR, K)),
        ] + [pl.BlockSpec(memory_space=pl.ANY)] * len(prev),
        out_specs=pl.BlockSpec((K * LC, K), lambda i: (i + start, 0)),
        input_output_aliases={8: 0} if prev else {},
        compiler_params=params(),
        cost_estimate=pl.CostEstimate(
            flops=1, bytes_accessed=6000000, transcendentals=0
        ),
        name="trailing_update",
    )(k, gown, grecv, la, lb, lpan, chol, damp, *prev)


def device(x, y, c, z):
    return ((x * NY + y) * NC + c) * NZ + z


def hops(along_x_core, d):
    pairs = []
    for x in range(NX):
        for y in range(NY):
            for c in range(NC):
                for z in range(NZ):
                    to = ((x + d) % NX, y) if c == along_x_core else (x, (y + d) % NY)
                    pairs.append((device(x, y, c, z), device(*to, c, z)))
    return pairs


def body(g_jets, layer_input_jets, speed, resid, point_index, damping, panel):
    q = lax.axis_index("row")
    k = panel[0]
    one = lambda v, d: lax.ppermute(v, AXES, hops(0, d))
    two = lambda v, d: lax.ppermute(v, AXES, hops(1, d))
    swap = lambda v: lax.ppermute(v, "core", [(0, 1), (1, 0)])
    zbit = lambda v, bit: v + lax.ppermute(v, "row", [(i, i ^ bit) for i in range(NZ)])
    bar = lax.optimization_barrier

    plus, minus, own = pack(
        panel,
        point_index.reshape(1, M),
        layer_input_jets.reshape(HR, POOL),
        g_jets.transpose(1, 0, 2).reshape(C * A, POOL),
        speed.reshape(2, M),
        resid.reshape(2, M),
    )
    dsel = lax.dynamic_index_in_dim(damping[:, 0, :], k // NZ, 0, keepdims=True)
    dsel = jnp.broadcast_to(jnp.where(k % NZ == q, dsel, 0.0), (8, K))
    parts = [dsel]
    for bits in (1, 2, 3):
        parts.append(lax.ppermute(dsel, "row", [(i, i ^ bits) for i in range(NZ)]))
    dsel = parts[0] + parts[1] + parts[2] + parts[3]
    accs = chunk([place(BLOCK0, 0, 0)], (plus, own), (), "chunk_own")
    ap, am, accs, dsel = bar((one(plus, 1), one(minus, -1), accs, dsel))
    m1 = assemble(BLOCK0, BLOCK1, plus, own, ap)
    relay = HB + 2 * GC
    rp, rm = one(ap[:relay], 1), one(am[:relay], -1)
    m1p, m1m = two(m1[0], 1), two(m1[1], -1)
    accs = chunk([place(BLOCK1, 0, -2), place(BLOCK2, 0, 1)], (ap, am), accs, "chunk_line1")
    rp, rm, accs, dsel = bar((rp, rm, accs, zbit(dsel, 4)))
    m2 = assemble(BLOCK2, BLOCK3, am, rp, rm)
    m2p, m2m = two(m2[0], 1), two(m2[1], -1)
    n1 = BR + GC
    r1p, r1m = two(m1p[:n1], 1), two(m1m[:n1], -1)
    e1 = 2 * BR + GC
    blocks = received(0, e1) + received(1, e1) + [place(BLOCK3, 0, 1)]
    accs = chunk(blocks, (m1p, m1m, rp, rm), accs, "chunk_line2")
    r1p, r1m, m2p, m2m, accs = bar((r1p, r1m, m2p, m2m, accs))
    r2p, r2m = two(m2p[:n1], 1), two(m2m[:n1], -1)
    blocks = [received(0, BR)[0], received(1, BR)[0]] + received(2, e1) + received(3, e1)
    accs = chunk(blocks, (r1p, r1m, m2p, m2m), accs, "chunk_far1")
    far = [received(0, BR)[0], received(1, BR)[0]]
    accs = chunk(far, (r2p, r2m), accs, "chunk_far2")
    gown, gsib, p, po, ps, dk = accs

    dk2, p, ps, gsib = bar((swap(dk), p, ps, gsib))
    chol, w, yz = cholesky(dk, dk2, dsel)
    pr, por, gr, w = bar((swap(p), swap(ps), swap(gsib), w))
    mine, lpan, la, lb = panel_solve(panel, p, pr, po, por, w, yz)
    slot = lax.broadcasted_iota(jnp.int32, (1, NZ, 1), 1)
    full = jnp.where(slot == q, mine[:, None, :], 0.0)
    parts = [full]
    for bits in (1, 2, 3):
        parts.append(lax.ppermute(parts[0], "row", [(i, i ^ bits) for i in range(NZ)]))
    full = parts[0] + parts[1] + parts[2] + parts[3]
    rest = (panel, gown, gr, la, lb, lpan, chol, damping[:, 0, :])
    fac = final(0, 8, *rest)
    full, fac = bar((full, fac))
    fac = final(8, 4, *rest, fac)
    full = zbit(full, 4)
    return fac.reshape(LR, 1, K, LC, 1, K), full.reshape(-1)


def solution(mesh):
    grid = Mesh(mesh.devices.reshape(NX, NY, NC, NZ), AXES)
    pts = ("x", "y", "core")
    in_specs = (
        P(None, None, pts),
        P(None, None, pts),
        P(pts),
        P(pts),
        P(pts),
        P(None, "row", None),
        P(),
    )
    out_specs = (P(None, "row", None, None, pts, None), P())
    return jax.shard_map(body, mesh=grid, in_specs=in_specs, out_specs=out_specs, check_vma=False)
```

```python
import jax
import jax.numpy as jnp
from jax import lax
from jax.experimental import pallas as pl
from jax.experimental.pallas import tpu as pltpu
from jax.sharding import Mesh, PartitionSpec as P

NX, NY, NC, NZ = 4, 4, 2, 8
A, K, C, POOL, M = 96, 128, 9, 256, 128
LR, LC = 12, 3
TOTAL = 4096
HR = C * K
BR = 1280
ROWG, KG, VR, RR = HR, HR + 108, HR + 117, HR + 118
GC = 64
HB = BR // 2
PR = BR + 4 * GC
FR = HB + 2 * GC
MR = 2 * BR + 3 * GC
RU, CU = LR * K, LC * K
JR = RU + 2 * CU + 2 * K
J_K, J_R = RU + 2 * CU, RU + 2 * CU + K
F32, BF16 = jnp.float32, jnp.bfloat16
AXES = ("x", "y", "core", "row")
HI = lax.Precision.HIGHEST
NT = (((1,), (1,)), ((), ()))
TN = (((0,), (0,)), ((), ()))
VMEM_LIMIT = 20 * 1024 * 1024
SMEM = pl.BlockSpec(memory_space=pltpu.SMEM)
VM = pl.BlockSpec(memory_space=pltpu.VMEM)
HBM = pl.BlockSpec(memory_space=pltpu.HBM)


def params():
    return pltpu.CompilerParams(vmem_limit_bytes=VMEM_LIMIT)


def pack_kernel(
    k_ref, idx_hbm, h_hbm, g_hbm, v_hbm, r_hbm, plus_ref, minus_ref, low_ref, high_ref, own_ref,
    gs, tail, cbuf, idx_ref, h_ref, g_ref, v_ref, r_ref, sem,
):
    copies = [
        pltpu.make_async_copy(src, dst, sem.at[i])
        for i, (src, dst) in enumerate(
            (
                (idx_hbm, idx_ref), (v_hbm, v_ref), (r_hbm, r_ref), (g_hbm, g_ref), (h_hbm, h_ref),
            )
        )
    ]
    for cp in copies:
        cp.start()
    x, y = lax.axis_index("x"), lax.axis_index("y")
    core, q = lax.axis_index("core"), lax.axis_index("row")
    k = k_ref[0]
    pool = lax.broadcasted_iota(jnp.int32, (POOL, M), 0)
    copies[0].wait()
    sel = (pool == idx_ref[...]).astype(F32).astype(BF16)
    for cp in copies[1:]:
        cp.wait()
    for c in range(C):
        val = jnp.dot(h_ref[c * K : (c + 1) * K, :], sel, preferred_element_type=F32).astype(BF16)
        plus_ref[c * K : (c + 1) * K, :] = val
        minus_ref[c * K : (c + 1) * K, :] = val
        if c < 5:
            low_ref[c * K : (c + 1) * K, :] = val
        else:
            high_ref[c * K - HB : (c + 1) * K - HB, :] = val
    for c in range(C):
        gs[c * A : (c + 1) * A, :] = jnp.dot(
            g_ref[c * A : (c + 1) * A, :], sel, preferred_element_type=F32
        )
    tail[...] = jnp.zeros_like(tail)
    for c in range(C):
        tail[c * LR : (c + 1) * LR, :] = gs[pl.ds(c * A + q, LR, stride=NZ), :]
        tail[108 + c : 109 + c, :] = gs[pl.ds(c * A + k, 1), :]
    for i, ref in enumerate((v_ref, r_ref)):
        low = jnp.dot(ref[...], sel[:M], preferred_element_type=F32)
        high = jnp.dot(ref[...], sel[M:], preferred_element_type=F32)
        tail[117 + i : 118 + i, :] = low[0:1] + high[1:2]
    val = tail[...].astype(BF16)
    plus_ref[HR:BR, :] = val
    minus_ref[HR:BR, :] = val
    high_ref[HR - HB : HB, :] = val
    cbuf[...] = jnp.zeros_like(cbuf)
    for dp in range(4):
        for dt in range(4):
            px = lax.rem(jnp.where(core == 0, x + dp, x + dt), NX)
            py = lax.rem(jnp.where(core == 0, y + dt, y + dp), NY)
            d = px * NY + py
            for c in range(C):
                for o in range(2):
                    cc = core if o == 0 else 1 - core
                    for lc in range(LC):
                        row = c * 6 + o * LC + lc
                        cbuf[row : row + 1, :] = gs[pl.ds(c * A + lc * 32 + 2 * d + cc, 1), :]
            val = cbuf[...].astype(BF16)
            if dp == 0:
                own_ref[dt * GC : (dt + 1) * GC, :] = val
            elif dp == 1:
                plus_ref[BR + dt * GC : BR + (1 + dt) * GC, :] = val
            elif dp == 3:
                minus_ref[BR + dt * GC : BR + (1 + dt) * GC, :] = val
            elif dt < 2:
                low_ref[HB + dt * GC : HB + (dt + 1) * GC, :] = val
            else:
                high_ref[HB + (dt - 2) * GC : HB + (dt - 1) * GC, :] = val


def pack(k, idx, h, g, v, r):
    return pl.pallas_call(
        pack_kernel,
        out_shape=(
            jax.ShapeDtypeStruct((PR, M), BF16),
            jax.ShapeDtypeStruct((PR, M), BF16),
            jax.ShapeDtypeStruct((FR, M), BF16),
            jax.ShapeDtypeStruct((FR, M), BF16),
            jax.ShapeDtypeStruct((4 * GC, M), BF16),
        ),
        in_specs=[SMEM] + [HBM] * 5,
        out_specs=(VM,) * 5,
        scratch_shapes=[
            pltpu.VMEM((C * A, M), F32),
            pltpu.VMEM((128, M), F32),
            pltpu.VMEM((GC, M), F32),
            pltpu.VMEM((1, M), jnp.int32),
            pltpu.VMEM((HR, POOL), BF16),
            pltpu.VMEM((C * A, POOL), BF16),
            pltpu.VMEM((2, M), BF16),
            pltpu.VMEM((2, M), BF16),
            pltpu.SemaphoreType.DMA((5,)),
        ],
        compiler_params=pltpu.CompilerParams(vmem_limit_bytes=60 * 1024 * 1024),
        name="pack",
    )(k, idx, h, g, v, r)


def block(i, cols):
    return ([(i, 0, HB), (i, HB, HB)], cols)


def after(i, lo):
    return [(i, lo + e * GC) for e in range(4)]


BLOCK0 = block(0, after(1, 0))
BLOCK1 = block(2, after(2, BR))
BLOCK2 = block(0, after(0, BR))
BLOCK3 = (
    [(1, 0, HB), (2, 0, HB)],
    [(1, HB), (1, HB + GC), (2, HB), (2, HB + GC)],
)


def message(first, second, e):
    out, at = [], 0
    for i, lo, n in first[0]:
        out.append((i, lo, n, at))
        at += n
    out.append((*first[1][2], GC, at))
    at += GC
    for i, lo, n in second[0]:
        out.append((i, lo, n, at))
        at += n
    for blk in (first, second):
        out.append((*blk[1][e], GC, at))
        at += GC
    return out


def assemble_kernel(plans, n_in, *refs):
    ins, outs = refs[:n_in], refs[n_in:]
    for plan, out in zip(plans, outs):
        for src, lo, n, at in plan:
            out[at : at + n, :] = ins[src][lo : lo + n, :]


def assemble(first, second, *ins):
    plans = (message(first, second, 1), message(second, first, 3))
    return pl.pallas_call(
        lambda *r: assemble_kernel(plans, len(ins), *r),
        out_shape=(jax.ShapeDtypeStruct((MR, M), BF16),) * 2,
        in_specs=[VM] * len(ins),
        out_specs=(VM,) * 2,
        compiler_params=params(),
        name="assemble",
    )(*ins)


def coefs(rows, per, v):
    row = lax.broadcasted_iota(jnp.int32, (rows, M), 0)
    c = jnp.zeros((rows, M), jnp.int32)
    for i in range(1, C):
        c = c + (row >= per * i).astype(jnp.int32)
    base = jnp.where((c == 1) | (c == 4) | (c == 7), 2.0, 1.0)
    return jnp.where(c < 3, base, -base * v)


ACCS = ((RU, CU), (RU, CU), (RU, 2 * K), (CU, K), (CU, K), (K + 16, K))


def chunk_kernel(blocks, n_in, n_acc, *refs):
    arrs, ins = refs[:n_in], refs[n_in : n_in + n_acc]
    outs, (jac, wg) = refs[n_in + n_acc : -2], refs[-2:]
    for blk, (hs, tl, cl) in enumerate(blocks):
        tail = arrs[tl[0]][tl[1] : tl[1] + 128, :].astype(F32)
        v = tail[117:118, :]
        lanes = slice(blk * M, (blk + 1) * M)
        wg[blk, 0:108, :] = tail[0:108, :] * coefs(108, LR, v)
        wg[blk, 176:185, :] = tail[108:117, :] * coefs(C, 1, v)
        gc = arrs[cl[0]][cl[1] : cl[1] + GC, :].astype(F32)
        wg[blk, 112:176, :] = gc * coefs(GC, 6, v)
        jac[J_R:JR, lanes] = jnp.zeros((JR - J_R, M), BF16)
        first_row = lax.broadcasted_iota(jnp.int32, (16, M), 0) == 0
        jac[J_R : J_R + 16, lanes] = jnp.where(first_row, tail[118:119, :], 0.0).astype(BF16)

    for blk, (hs, tl, cl) in enumerate(blocks):
        lanes = slice(blk * M, (blk + 1) * M)

        def slab(t, carry, hs=hs, lanes=lanes, blk=blk):
            base = pl.multiple_of(t * 16, 16)
            h = [arrs[i][pl.ds(lo + base, 16), :].astype(F32) for i, lo in hs]

            def unit(rows, dst):
                acc = wg[blk, rows[0] : rows[0] + 1, :] * h[0]
                for c in range(1, C):
                    acc = acc + wg[blk, rows[c] : rows[c] + 1, :] * h[c]
                jac[pl.ds(dst + base, 16), lanes] = acc.astype(BF16)

            for u in range(LR):
                unit([c * LR + u for c in range(C)], u * K)
            for u in range(6):
                unit([112 + c * 6 + u for c in range(C)], RU + u * K)
            unit([176 + c for c in range(C)], J_K)
            return carry

        lax.fori_loop(0, K // 16, slab, 0)

    def acc(i, rows, cols, val):
        if n_acc:
            val = val + ins[i][rows, cols]
        outs[i][rows, cols] = val

    al = slice(None)
    pd = lax.dot_general(jac[RU : J_R + 16, :], jac[J_K:J_R, :], NT, preferred_element_type=F32)
    acc(3, al, al, pd[0:CU])
    acc(4, al, al, pd[CU : 2 * CU])
    acc(5, al, al, pd[2 * CU :])
    tile = 512
    for n in (3, 0, 1, 2):
        for m in range(RU // tile):
            rows = slice(m * tile, (m + 1) * tile)
            val = lax.dot_general(
                jac[rows, :], jac[RU + n * 256 : RU + (n + 1) * 256, :], NT,
                preferred_element_type=F32,
            )
            if n == 0:
                acc(0, rows, slice(0, 256), val)
            elif n == 1:
                acc(0, rows, slice(256, 384), val[:, :128])
                acc(1, rows, slice(0, 128), val[:, 128:])
            elif n == 2:
                acc(1, rows, slice(128, 384), val)
            else:
                acc(2, rows, al, val)


def chunk(blocks, arrs, accs, name):
    n = len(blocks)
    return pl.pallas_call(
        lambda *r: chunk_kernel(blocks, len(arrs), len(accs), *r),
        out_shape=tuple(jax.ShapeDtypeStruct(s, F32) for s in ACCS),
        in_specs=[VM] * (len(arrs) + len(accs)),
        out_specs=(VM,) * len(ACCS),
        scratch_shapes=[pltpu.VMEM((JR, n * M), BF16), pltpu.VMEM((n, 192, M), F32)],
        compiler_params=params(),
        cost_estimate=pl.CostEstimate(
            flops=n * 2 * JR * K * (RU + C), bytes_accessed=n * 4_000_000, transcendentals=0
        ),
        name=name,
    )(*arrs, *accs)


def place(blk, e, shift):
    hs, rows = [], [(i, lo + r) for i, lo, n in blk[0] for r in range(0, n, K)]
    rows = [(i + shift, lo) for i, lo in rows]
    i, lo = blk[1][e]
    return rows[:C], rows[C], (i + shift, lo)


def received(i, col):
    two = []
    for b in range(2):
        lo = b * (BR + GC)
        two.append(([(i, lo + c * K) for c in range(C)], (i, lo + HR), (i, col + b * GC)))
    return two


def chol_kernel(a_ref, b_ref, d_ref, chol_ref, w_ref, yz_ref, m_ref, u_ref):
    row = lax.broadcasted_iota(jnp.int32, (K, K), 0)
    col = lax.broadcasted_iota(jnp.int32, (K, K), 1)
    eye = row == col
    gram = (a_ref[0:K, :] + b_ref[0:K, :]) * (1.0 / TOTAL)
    m_ref[:, :K] = gram + jnp.where(eye, d_ref[0:1, :], 0.0)
    m_ref[:, K:] = jnp.where(eye, 1.0, 0.0)
    sub = lax.broadcasted_iota(jnp.int32, (8, K), 0)
    pick = lambda v, r: jnp.broadcast_to(v[r : r + 1, :], (8, v.shape[1]))
    for b in range(K // 8):
        lo = 8 * b
        p = m_ref[lo : lo + 8, :]
        left, right = p[:, :K], p[:, K:]
        cols = [jnp.broadcast_to(p[:, lo + c : lo + c + 1], (8, K)) for c in range(8)]
        scale = jnp.ones((8, K), F32)
        for r in range(8):
            rs = lax.rsqrt(pick(cols[r], r))
            mult = jnp.where(sub > r, cols[r] * (rs * rs), 0.0)
            for c in range(r + 1, 8):
                cols[c] = cols[c] - mult * pick(cols[c], r)
            scale = jnp.where(sub == r, rs, scale)
            left = left - mult * pick(left, r)
            right = right - mult * pick(right, r)
        p = jnp.concatenate([left * scale, right * scale], axis=1)
        u_ref[lo : lo + 8, :] = p
        if b < K // 8 - 1:
            ut = p[:, :K].T
            rows = [pick(p, r) for r in range(8)]
            for t in range(b + 1, K // 8):
                at = slice(8 * t, 8 * t + 8)
                acc = m_ref[at, :]
                for r in range(8):
                    acc = acc - jnp.broadcast_to(ut[at, r : r + 1], (8, 2 * K)) * rows[r]
                m_ref[at, :] = acc
    chol_ref[...] = jnp.where(col >= row, u_ref[:, :K], 0.0).T
    w = u_ref[:, K:]
    w_ref[...] = w
    g = (a_ref[K : K + 8, :] + b_ref[K : K + 8, :]) * (1.0 / TOTAL)
    y = lax.dot_general(g, w, NT, precision=HI, preferred_element_type=F32)
    z = lax.dot_general(y, w, (((1,), (0,)), ((), ())), precision=HI, preferred_element_type=F32)
    yz_ref[0:8, :] = y
    yz_ref[8:16, :] = z


def cholesky(dk, dk2, damp):
    return pl.pallas_call(
        chol_kernel,
        out_shape=(
            jax.ShapeDtypeStruct((K, K), F32),
            jax.ShapeDtypeStruct((K, K), F32),
            jax.ShapeDtypeStruct((16, K), F32),
        ),
        in_specs=[VM] * 3,
        out_specs=(VM,) * 3,
        scratch_shapes=[pltpu.VMEM((K, 2 * K), F32), pltpu.VMEM((K, 2 * K), F32)],
        compiler_params=params(),
        name="panel_factor",
    )(dk, dk2, damp)


def halves(v):
    hi = v.astype(BF16)
    return hi, (v - hi.astype(F32)).astype(BF16)


def panel_kernel(k_ref, p_ref, pr_ref, po_ref, por_ref, w_ref, yz_ref, dir_ref, lpan_ref, la_ref, lb_ref):
    q, k = lax.axis_index("row"), k_ref[0]
    inv = 1.0 / TOTAL
    w_hi, w_lo = halves(w_ref[...])
    wb = jnp.concatenate([w_hi, w_lo, w_hi], axis=1)
    sub = lax.broadcasted_iota(jnp.int32, (8, 2 * K), 0)
    lane = lax.broadcasted_iota(jnp.int32, (8, 2 * K), 1)
    z = yz_ref[8:9, :]
    z2 = jnp.concatenate([z, jnp.zeros_like(z)], axis=1)
    lhs = jnp.where(lane == K, 1.0, jnp.where(sub == 0, -z2, 0.0))

    def solve(p):
        hi, lo = halves(p)
        return lax.dot_general(
            jnp.concatenate([hi, hi, lo], axis=1), wb, NT, preferred_element_type=F32
        )

    for lr in range(LR):
        rows = slice(lr * K, (lr + 1) * K)
        pe = (p_ref[rows, :] + pr_ref[rows, :]) * inv
        d = lax.dot_general(lhs, pe, NT, precision=HI, preferred_element_type=F32)
        i = lr * NZ + q
        dir_ref[lr : lr + 1, :] = jnp.where(
            i == k, yz_ref[0:1, :], jnp.where(i > k, d[0:1, :], d[1:2, :])
        )
        lpan = solve(pe[:, :K])
        lpan_ref[rows, :] = lpan
        hi, lo = halves(lpan)
        la_ref[rows, :] = jnp.concatenate([hi, hi, lo], axis=1)
    hi, lo = halves(solve((po_ref[...] + por_ref[...]) * inv))
    lb_ref[...] = jnp.concatenate([hi, lo, hi], axis=1)


def panel_solve(k, p, pr, po, por, w, yz):
    return pl.pallas_call(
        panel_kernel,
        out_shape=(
            jax.ShapeDtypeStruct((LR, K), F32),
            jax.ShapeDtypeStruct((RU, K), F32),
            jax.ShapeDtypeStruct((RU, 3 * K), BF16),
            jax.ShapeDtypeStruct((CU, 3 * K), BF16),
        ),
        in_specs=[SMEM] + [VM] * 6,
        out_specs=(VM,) * 4,
        compiler_params=params(),
        name="panel_solve",
    )(k, p, pr, po, por, w, yz)


def final_kernel(start, k_ref, g_ref, gr_ref, la_ref, lb_ref, lpan_ref, chol_ref, damp_ref, *refs):
    out_ref = refs[-1]
    q, k = lax.axis_index("row"), k_ref[0]
    s = (lax.axis_index("x") * NY + lax.axis_index("y")) * NC + lax.axis_index("core")
    lr = start + pl.program_id(0)
    i = lr * NZ + q
    upd = lax.dot_general(la_ref[...], lb_ref[...], NT, preferred_element_type=F32)
    gram = (g_ref[...] + gr_ref[...]) * (1.0 / TOTAL)
    row = lax.broadcasted_iota(jnp.int32, (K, K), 0)
    col = lax.broadcasted_iota(jnp.int32, (K, K), 1)
    damp = damp_ref[pl.ds(lr, 1), :]
    for lc in range(LC):
        j = lc * (NX * NY * NC) + s
        gt = gram[:, lc * K : (lc + 1) * K] + jnp.where((row == col) & (i == j), damp, 0.0)
        val = jnp.where(
            (i > k) & (j > k),
            gt - upd[:, lc * K : (lc + 1) * K],
            jnp.where(
                (i > k) & (j == k),
                lpan_ref[...],
                jnp.where((i == k) & (j == k), chol_ref[...], gt),
            ),
        )
        out_ref[pl.ds(lc, K, stride=LC), :] = val


def final(start, count, k, gown, grecv, la, lb, lpan, chol, damp, *prev):
    full = lambda shape: pl.BlockSpec(shape, lambda i: (0,) * len(shape))
    rows = lambda width: pl.BlockSpec((K, width), lambda i: (i + start, 0))
    return pl.pallas_call(
        lambda *r: final_kernel(start, *r),
        grid=(count,),
        out_shape=jax.ShapeDtypeStruct((RU * LC, K), F32),
        in_specs=[
            SMEM, rows(CU), rows(CU), rows(3 * K), full((CU, 3 * K)), rows(K), full((K, K)),
            full((LR, K)),
        ] + [pl.BlockSpec(memory_space=pl.ANY)] * len(prev),
        out_specs=pl.BlockSpec((K * LC, K), lambda i: (i + start, 0)),
        input_output_aliases={8: 0} if prev else {},
        compiler_params=params(),
        cost_estimate=pl.CostEstimate(
            flops=1, bytes_accessed=6000000, transcendentals=0
        ),
        name="trailing_update",
    )(k, gown, grecv, la, lb, lpan, chol, damp, *prev)


def device(x, y, c, z):
    return ((x * NY + y) * NC + c) * NZ + z


def hops(along_x_core, d):
    pairs = []
    for x in range(NX):
        for y in range(NY):
            for c in range(NC):
                for z in range(NZ):
                    to = ((x + d) % NX, y) if c == along_x_core else (x, (y + d) % NY)
                    pairs.append((device(x, y, c, z), device(*to, c, z)))
    return pairs


def body(g_jets, layer_input_jets, speed, resid, point_index, damping, panel):
    q = lax.axis_index("row")
    k = panel[0]
    one = lambda v, d: lax.ppermute(v, AXES, hops(0, d))
    two = lambda v, d: lax.ppermute(v, AXES, hops(1, d))
    swap = lambda v: lax.ppermute(v, "core", [(0, 1), (1, 0)])
    zbit = lambda v, bit: v + lax.ppermute(v, "row", [(i, i ^ bit) for i in range(NZ)])
    bar = lax.optimization_barrier

    plus, minus, low, high, own = pack(
        panel,
        point_index.reshape(1, M),
        layer_input_jets.reshape(HR, POOL),
        g_jets.transpose(1, 0, 2).reshape(C * A, POOL),
        speed.reshape(2, M),
        resid.reshape(2, M),
    )
    dsel = lax.dynamic_index_in_dim(damping[:, 0, :], k // NZ, 0, keepdims=True)
    dsel = jnp.broadcast_to(jnp.where(k % NZ == q, dsel, 0.0), (8, K))
    accs = chunk([place(BLOCK0, 0, 0)], (plus, own), (), "chunk_own")
    ap, am, rp, rm = one(plus, 1), one(minus, -1), one(low, 2), one(high, 2)
    ap, am, rp, rm, accs, dsel = bar((ap, am, rp, rm, accs, zbit(zbit(dsel, 1), 2)))
    m1 = assemble(BLOCK0, BLOCK1, plus, own, ap)
    m2 = assemble(BLOCK2, BLOCK3, am, rp, rm)
    m1p, m1m, m2p, m2m = two(m1[0], 1), two(m1[1], -1), two(m2[0], 1), two(m2[1], -1)
    line = [place(BLOCK1, 0, -2), place(BLOCK2, 0, 1), place(BLOCK3, 0, 1)]
    accs = chunk(line, (ap, am, rp, rm), accs, "chunk_line")
    m1p, m1m, accs, dsel = bar((m1p, m1m, accs, zbit(dsel, 4)))
    n1 = BR + GC
    r1p, r1m = two(m1p[:n1], 1), two(m1m[:n1], -1)
    e1 = 2 * BR + GC
    near = received(0, e1) + received(1, e1)
    accs = chunk(near, (m1p, m1m), accs, "chunk_near1")
    m2p, m2m, accs = bar((m2p, m2m, accs))
    r2p, r2m = two(m2p[:n1], 1), two(m2m[:n1], -1)
    far = [received(0, BR)[0], received(1, BR)[0]]
    accs = chunk(far + received(2, e1) + received(3, e1), (r1p, r1m, m2p, m2m), accs, "chunk_far1")
    accs = chunk(far, (r2p, r2m), accs, "chunk_far2")
    gown, gsib, p, po, ps, dk = accs

    dk2, p, ps, gsib = bar((swap(dk), p, ps, gsib))
    chol, w, yz = cholesky(dk, dk2, dsel)
    pr, por, gr, w = bar((swap(p), swap(ps), swap(gsib), w))
    mine, lpan, la, lb = panel_solve(panel, p, pr, po, por, w, yz)
    slot = lax.broadcasted_iota(jnp.int32, (1, NZ, 1), 1)
    full = jnp.where(slot == q, mine[:, None, :], 0.0)
    parts = [full]
    for bits in (1, 2, 3):
        parts.append(lax.ppermute(parts[0], "row", [(i, i ^ bits) for i in range(NZ)]))
    full = parts[0] + parts[1] + parts[2] + parts[3]
    rest = (panel, gown, gr, la, lb, lpan, chol, damping[:, 0, :])
    fac = final(0, 8, *rest)
    full, fac = bar((full, fac))
    fac = final(8, 4, *rest, fac)
    full = zbit(full, 4)
    return fac.reshape(LR, 1, K, LC, 1, K), full.reshape(-1)


def solution(mesh):
    grid = Mesh(mesh.devices.reshape(NX, NY, NC, NZ), AXES)
    pts = ("x", "y", "core")
    in_specs = (
        P(None, None, pts),
        P(None, None, pts),
        P(pts),
        P(pts),
        P(pts),
        P(None, "row", None),
        P(),
    )
    out_specs = (P(None, "row", None, None, pts, None), P())
    return jax.shard_map(body, mesh=grid, in_specs=in_specs, out_specs=out_specs, check_vma=False)
```

```python
import jax
import jax.numpy as jnp
from jax import lax
from jax.experimental import pallas as pl
from jax.experimental.pallas import tpu as pltpu
from jax.sharding import Mesh, PartitionSpec as P

NX, NY, NC, NZ = 4, 4, 2, 8
A, K, C, POOL, M = 96, 128, 9, 256, 128
LR, LC = 12, 3
TOTAL = 4096
HR = C * K
BR = 1280
ROWG, KG, VR, RR = HR, HR + 108, HR + 117, HR + 118
GC = 64
HB = BR // 2
PR = BR + 4 * GC
FR = HB + 2 * GC
MR = 2 * BR + 3 * GC
RU, CU = LR * K, LC * K
JR = RU + 2 * CU + 2 * K
J_K, J_R = RU + 2 * CU, RU + 2 * CU + K
F32, BF16 = jnp.float32, jnp.bfloat16
AXES = ("x", "y", "core", "row")
HI = lax.Precision.HIGHEST
NT = (((1,), (1,)), ((), ()))
TN = (((0,), (0,)), ((), ()))
VMEM_LIMIT = 20 * 1024 * 1024
SMEM = pl.BlockSpec(memory_space=pltpu.SMEM)
VM = pl.BlockSpec(memory_space=pltpu.VMEM)
HBM = pl.BlockSpec(memory_space=pltpu.HBM)


def params():
    return pltpu.CompilerParams(vmem_limit_bytes=VMEM_LIMIT)


def pack_kernel(
    k_ref, idx_hbm, h_hbm, g_hbm, v_hbm, r_hbm, plus_ref, minus_ref, low_ref, high_ref, own_ref,
    gs, tail, cbuf, idx_ref, h_ref, g_ref, v_ref, r_ref, sem,
):
    copies = [
        pltpu.make_async_copy(src, dst, sem.at[i])
        for i, (src, dst) in enumerate(
            (
                (idx_hbm, idx_ref), (v_hbm, v_ref), (r_hbm, r_ref), (g_hbm, g_ref), (h_hbm, h_ref),
            )
        )
    ]
    for cp in copies:
        cp.start()
    x, y = lax.axis_index("x"), lax.axis_index("y")
    core, q = lax.axis_index("core"), lax.axis_index("row")
    k = k_ref[0]
    pool = lax.broadcasted_iota(jnp.int32, (POOL, M), 0)
    copies[0].wait()
    sel = (pool == idx_ref[...]).astype(F32).astype(BF16)
    for cp in copies[1:]:
        cp.wait()
    for c in range(C):
        val = jnp.dot(h_ref[c * K : (c + 1) * K, :], sel, preferred_element_type=F32).astype(BF16)
        plus_ref[c * K : (c + 1) * K, :] = val
        minus_ref[c * K : (c + 1) * K, :] = val
        if c < 5:
            low_ref[c * K : (c + 1) * K, :] = val
        else:
            high_ref[c * K - HB : (c + 1) * K - HB, :] = val
    for c in range(C):
        gs[c * A : (c + 1) * A, :] = jnp.dot(
            g_ref[c * A : (c + 1) * A, :], sel, preferred_element_type=F32
        )
    tail[...] = jnp.zeros_like(tail)
    for c in range(C):
        tail[c * LR : (c + 1) * LR, :] = gs[pl.ds(c * A + q, LR, stride=NZ), :]
        tail[108 + c : 109 + c, :] = gs[pl.ds(c * A + k, 1), :]
    for i, ref in enumerate((v_ref, r_ref)):
        low = jnp.dot(ref[...], sel[:M], preferred_element_type=F32)
        high = jnp.dot(ref[...], sel[M:], preferred_element_type=F32)
        tail[117 + i : 118 + i, :] = low[0:1] + high[1:2]
    val = tail[...].astype(BF16)
    plus_ref[HR:BR, :] = val
    minus_ref[HR:BR, :] = val
    high_ref[HR - HB : HB, :] = val
    cbuf[...] = jnp.zeros_like(cbuf)
    for dp in range(4):
        for dt in range(4):
            px = lax.rem(jnp.where(core == 0, x + dp, x + dt), NX)
            py = lax.rem(jnp.where(core == 0, y + dt, y + dp), NY)
            d = px * NY + py
            for c in range(C):
                for o in range(2):
                    cc = core if o == 0 else 1 - core
                    for lc in range(LC):
                        row = c * 6 + o * LC + lc
                        cbuf[row : row + 1, :] = gs[pl.ds(c * A + lc * 32 + 2 * d + cc, 1), :]
            val = cbuf[...].astype(BF16)
            if dp == 0:
                own_ref[dt * GC : (dt + 1) * GC, :] = val
            elif dp == 1:
                plus_ref[BR + dt * GC : BR + (1 + dt) * GC, :] = val
            elif dp == 3:
                minus_ref[BR + dt * GC : BR + (1 + dt) * GC, :] = val
            elif dt < 2:
                low_ref[HB + dt * GC : HB + (dt + 1) * GC, :] = val
            else:
                high_ref[HB + (dt - 2) * GC : HB + (dt - 1) * GC, :] = val


def pack(k, idx, h, g, v, r):
    return pl.pallas_call(
        pack_kernel,
        out_shape=(
            jax.ShapeDtypeStruct((PR, M), BF16),
            jax.ShapeDtypeStruct((PR, M), BF16),
            jax.ShapeDtypeStruct((FR, M), BF16),
            jax.ShapeDtypeStruct((FR, M), BF16),
            jax.ShapeDtypeStruct((4 * GC, M), BF16),
        ),
        in_specs=[SMEM] + [HBM] * 5,
        out_specs=(VM,) * 5,
        scratch_shapes=[
            pltpu.VMEM((C * A, M), F32),
            pltpu.VMEM((128, M), F32),
            pltpu.VMEM((GC, M), F32),
            pltpu.VMEM((1, M), jnp.int32),
            pltpu.VMEM((HR, POOL), BF16),
            pltpu.VMEM((C * A, POOL), BF16),
            pltpu.VMEM((2, M), BF16),
            pltpu.VMEM((2, M), BF16),
            pltpu.SemaphoreType.DMA((5,)),
        ],
        compiler_params=pltpu.CompilerParams(vmem_limit_bytes=60 * 1024 * 1024),
        name="pack",
    )(k, idx, h, g, v, r)


def block(i, cols):
    return ([(i, 0, HB), (i, HB, HB)], cols)


def after(i, lo):
    return [(i, lo + e * GC) for e in range(4)]


BLOCK0 = block(0, after(1, 0))
BLOCK1 = block(2, after(2, BR))
BLOCK2 = block(0, after(0, BR))
BLOCK3 = (
    [(1, 0, HB), (2, 0, HB)],
    [(1, HB), (1, HB + GC), (2, HB), (2, HB + GC)],
)


def message(first, second, e):
    out, at = [], 0
    for i, lo, n in first[0]:
        out.append((i, lo, n, at))
        at += n
    out.append((*first[1][2], GC, at))
    at += GC
    for i, lo, n in second[0]:
        out.append((i, lo, n, at))
        at += n
    for blk in (first, second):
        out.append((*blk[1][e], GC, at))
        at += GC
    return out


def assemble_kernel(plans, n_in, *refs):
    ins, outs = refs[:n_in], refs[n_in:]
    for plan, out in zip(plans, outs):
        for src, lo, n, at in plan:
            out[at : at + n, :] = ins[src][lo : lo + n, :]


def assemble(first, second, *ins):
    plans = (message(first, second, 1), message(second, first, 3))
    return pl.pallas_call(
        lambda *r: assemble_kernel(plans, len(ins), *r),
        out_shape=(jax.ShapeDtypeStruct((MR, M), BF16),) * 2,
        in_specs=[VM] * len(ins),
        out_specs=(VM,) * 2,
        compiler_params=params(),
        name="assemble",
    )(*ins)


def coefs(rows, per, v):
    row = lax.broadcasted_iota(jnp.int32, (rows, M), 0)
    c = jnp.zeros((rows, M), jnp.int32)
    for i in range(1, C):
        c = c + (row >= per * i).astype(jnp.int32)
    base = jnp.where((c == 1) | (c == 4) | (c == 7), 2.0, 1.0)
    return jnp.where(c < 3, base, -base * v)


ACCS = ((RU, CU), (RU, CU), (RU, 2 * K), (CU, K), (CU, K), (K + 16, K))


def chunk_kernel(blocks, n_in, n_acc, *refs):
    arrs, ins = refs[:n_in], refs[n_in : n_in + n_acc]
    outs, (jac, wg) = refs[n_in + n_acc : -2], refs[-2:]
    for blk, (hs, tl, cl) in enumerate(blocks):
        tail = arrs[tl[0]][tl[1] : tl[1] + 128, :].astype(F32)
        v = tail[117:118, :]
        lanes = slice(blk * M, (blk + 1) * M)
        wg[blk, 0:108, :] = tail[0:108, :] * coefs(108, LR, v)
        wg[blk, 176:185, :] = tail[108:117, :] * coefs(C, 1, v)
        gc = arrs[cl[0]][cl[1] : cl[1] + GC, :].astype(F32)
        wg[blk, 112:176, :] = gc * coefs(GC, 6, v)
        jac[J_R:JR, lanes] = jnp.zeros((JR - J_R, M), BF16)
        first_row = lax.broadcasted_iota(jnp.int32, (16, M), 0) == 0
        jac[J_R : J_R + 16, lanes] = jnp.where(first_row, tail[118:119, :], 0.0).astype(BF16)

    for blk, (hs, tl, cl) in enumerate(blocks):
        lanes = slice(blk * M, (blk + 1) * M)

        def slab(t, carry, hs=hs, lanes=lanes, blk=blk):
            base = pl.multiple_of(t * 16, 16)
            h = [arrs[i][pl.ds(lo + base, 16), :].astype(F32) for i, lo in hs]

            def unit(rows, dst):
                acc = wg[blk, rows[0] : rows[0] + 1, :] * h[0]
                for c in range(1, C):
                    acc = acc + wg[blk, rows[c] : rows[c] + 1, :] * h[c]
                jac[pl.ds(dst + base, 16), lanes] = acc.astype(BF16)

            for u in range(LR):
                unit([c * LR + u for c in range(C)], u * K)
            for u in range(6):
                unit([112 + c * 6 + u for c in range(C)], RU + u * K)
            unit([176 + c for c in range(C)], J_K)
            return carry

        lax.fori_loop(0, K // 16, slab, 0)

    def acc(i, rows, cols, val):
        if n_acc:
            val = val + ins[i][rows, cols]
        outs[i][rows, cols] = val

    al = slice(None)
    pd = lax.dot_general(jac[RU : J_R + 16, :], jac[J_K:J_R, :], NT, preferred_element_type=F32)
    acc(3, al, al, pd[0:CU])
    acc(4, al, al, pd[CU : 2 * CU])
    acc(5, al, al, pd[2 * CU :])
    tile = 512
    for n in (3, 0, 1, 2):
        for m in range(RU // tile):
            rows = slice(m * tile, (m + 1) * tile)
            val = lax.dot_general(
                jac[rows, :], jac[RU + n * 256 : RU + (n + 1) * 256, :], NT,
                preferred_element_type=F32,
            )
            if n == 0:
                acc(0, rows, slice(0, 256), val)
            elif n == 1:
                acc(0, rows, slice(256, 384), val[:, :128])
                acc(1, rows, slice(0, 128), val[:, 128:])
            elif n == 2:
                acc(1, rows, slice(128, 384), val)
            else:
                acc(2, rows, al, val)


def chunk(blocks, arrs, accs, name):
    n = len(blocks)
    return pl.pallas_call(
        lambda *r: chunk_kernel(blocks, len(arrs), len(accs), *r),
        out_shape=tuple(jax.ShapeDtypeStruct(s, F32) for s in ACCS),
        in_specs=[VM] * (len(arrs) + len(accs)),
        out_specs=(VM,) * len(ACCS),
        scratch_shapes=[pltpu.VMEM((JR, n * M), BF16), pltpu.VMEM((n, 192, M), F32)],
        compiler_params=params(),
        cost_estimate=pl.CostEstimate(
            flops=n * 2 * JR * K * (RU + C), bytes_accessed=n * 4_000_000, transcendentals=0
        ),
        name=name,
    )(*arrs, *accs)


def place(blk, e, shift):
    hs, rows = [], [(i, lo + r) for i, lo, n in blk[0] for r in range(0, n, K)]
    rows = [(i + shift, lo) for i, lo in rows]
    i, lo = blk[1][e]
    return rows[:C], rows[C], (i + shift, lo)


def received(i, col):
    two = []
    for b in range(2):
        lo = b * (BR + GC)
        two.append(([(i, lo + c * K) for c in range(C)], (i, lo + HR), (i, col + b * GC)))
    return two


def chol_kernel(a_ref, b_ref, d_ref, chol_ref, w_ref, yz_ref, m_ref, u_ref):
    row = lax.broadcasted_iota(jnp.int32, (K, K), 0)
    col = lax.broadcasted_iota(jnp.int32, (K, K), 1)
    eye = row == col
    gram = (a_ref[0:K, :] + b_ref[0:K, :]) * (1.0 / TOTAL)
    m_ref[:, :K] = gram + jnp.where(eye, d_ref[0:1, :], 0.0)
    m_ref[:, K:] = jnp.where(eye, 1.0, 0.0)
    sub = lax.broadcasted_iota(jnp.int32, (8, K), 0)
    pick = lambda v, r: jnp.broadcast_to(v[r : r + 1, :], (8, v.shape[1]))
    for b in range(K // 8):
        lo = 8 * b
        p = m_ref[lo : lo + 8, :]
        left, right = p[:, :K], p[:, K:]
        cols = [jnp.broadcast_to(p[:, lo + c : lo + c + 1], (8, K)) for c in range(8)]
        scale = jnp.ones((8, K), F32)
        for r in range(8):
            rs = lax.rsqrt(pick(cols[r], r))
            mult = jnp.where(sub > r, cols[r] * (rs * rs), 0.0)
            for c in range(r + 1, 8):
                cols[c] = cols[c] - mult * pick(cols[c], r)
            scale = jnp.where(sub == r, rs, scale)
            left = left - mult * pick(left, r)
            right = right - mult * pick(right, r)
        p = jnp.concatenate([left * scale, right * scale], axis=1)
        u_ref[lo : lo + 8, :] = p
        if b < K // 8 - 1:
            ut = p[:, :K].T
            rows = [pick(p, r) for r in range(8)]
            for t in range(b + 1, K // 8):
                at = slice(8 * t, 8 * t + 8)
                acc = m_ref[at, :]
                for r in range(8):
                    acc = acc - jnp.broadcast_to(ut[at, r : r + 1], (8, 2 * K)) * rows[r]
                m_ref[at, :] = acc
    chol_ref[...] = jnp.where(col >= row, u_ref[:, :K], 0.0).T
    w = u_ref[:, K:]
    w_ref[...] = w
    g = (a_ref[K : K + 8, :] + b_ref[K : K + 8, :]) * (1.0 / TOTAL)
    y = lax.dot_general(g, w, NT, precision=HI, preferred_element_type=F32)
    z = lax.dot_general(y, w, (((1,), (0,)), ((), ())), precision=HI, preferred_element_type=F32)
    yz_ref[0:8, :] = y
    yz_ref[8:16, :] = z


def cholesky(dk, dk2, damp):
    return pl.pallas_call(
        chol_kernel,
        out_shape=(
            jax.ShapeDtypeStruct((K, K), F32),
            jax.ShapeDtypeStruct((K, K), F32),
            jax.ShapeDtypeStruct((16, K), F32),
        ),
        in_specs=[VM] * 3,
        out_specs=(VM,) * 3,
        scratch_shapes=[pltpu.VMEM((K, 2 * K), F32), pltpu.VMEM((K, 2 * K), F32)],
        compiler_params=params(),
        name="panel_factor",
    )(dk, dk2, damp)


def halves(v):
    hi = v.astype(BF16)
    return hi, (v - hi.astype(F32)).astype(BF16)


def panel_kernel(k_ref, p_ref, pr_ref, po_ref, por_ref, w_ref, yz_ref, dir_ref, lpan_ref, la_ref, lb_ref):
    q, k = lax.axis_index("row"), k_ref[0]
    inv = 1.0 / TOTAL
    w_hi, w_lo = halves(w_ref[...])
    wb = jnp.concatenate([w_hi, w_lo, w_hi], axis=1)
    sub = lax.broadcasted_iota(jnp.int32, (8, 2 * K), 0)
    lane = lax.broadcasted_iota(jnp.int32, (8, 2 * K), 1)
    z = yz_ref[8:9, :]
    z2 = jnp.concatenate([z, jnp.zeros_like(z)], axis=1)
    lhs = jnp.where(lane == K, 1.0, jnp.where(sub == 0, -z2, 0.0))

    def solve(p):
        hi, lo = halves(p)
        return lax.dot_general(
            jnp.concatenate([hi, hi, lo], axis=1), wb, NT, preferred_element_type=F32
        )

    for lr in range(LR):
        rows = slice(lr * K, (lr + 1) * K)
        pe = (p_ref[rows, :] + pr_ref[rows, :]) * inv
        d = lax.dot_general(lhs, pe, NT, precision=HI, preferred_element_type=F32)
        i = lr * NZ + q
        dir_ref[lr : lr + 1, :] = jnp.where(
            i == k, yz_ref[0:1, :], jnp.where(i > k, d[0:1, :], d[1:2, :])
        )
        lpan = solve(pe[:, :K])
        lpan_ref[rows, :] = lpan
        hi, lo = halves(lpan)
        la_ref[rows, :] = jnp.concatenate([hi, hi, lo], axis=1)
    hi, lo = halves(solve((po_ref[...] + por_ref[...]) * inv))
    lb_ref[...] = jnp.concatenate([hi, lo, hi], axis=1)


def panel_solve(k, p, pr, po, por, w, yz):
    return pl.pallas_call(
        panel_kernel,
        out_shape=(
            jax.ShapeDtypeStruct((LR, K), F32),
            jax.ShapeDtypeStruct((RU, K), F32),
            jax.ShapeDtypeStruct((RU, 3 * K), BF16),
            jax.ShapeDtypeStruct((CU, 3 * K), BF16),
        ),
        in_specs=[SMEM] + [VM] * 6,
        out_specs=(VM,) * 4,
        compiler_params=params(),
        name="panel_solve",
    )(k, p, pr, po, por, w, yz)


def final_kernel(start, k_ref, g_ref, gr_ref, la_ref, lb_ref, lpan_ref, chol_ref, damp_ref, *refs):
    out_ref = refs[-1]
    q, k = lax.axis_index("row"), k_ref[0]
    s = (lax.axis_index("x") * NY + lax.axis_index("y")) * NC + lax.axis_index("core")
    lr = start + pl.program_id(0)
    i = lr * NZ + q
    upd = lax.dot_general(la_ref[...], lb_ref[...], NT, preferred_element_type=F32)
    gram = (g_ref[...] + gr_ref[...]) * (1.0 / TOTAL)
    row = lax.broadcasted_iota(jnp.int32, (K, K), 0)
    col = lax.broadcasted_iota(jnp.int32, (K, K), 1)
    damp = damp_ref[pl.ds(lr, 1), :]
    for lc in range(LC):
        j = lc * (NX * NY * NC) + s
        gt = gram[:, lc * K : (lc + 1) * K] + jnp.where((row == col) & (i == j), damp, 0.0)
        val = jnp.where(
            (i > k) & (j > k),
            gt - upd[:, lc * K : (lc + 1) * K],
            jnp.where(
                (i > k) & (j == k),
                lpan_ref[...],
                jnp.where((i == k) & (j == k), chol_ref[...], gt),
            ),
        )
        out_ref[pl.ds(lc, K, stride=LC), :] = val


def final(start, count, k, gown, grecv, la, lb, lpan, chol, damp, *prev):
    full = lambda shape: pl.BlockSpec(shape, lambda i: (0,) * len(shape))
    rows = lambda width: pl.BlockSpec((K, width), lambda i: (i + start, 0))
    return pl.pallas_call(
        lambda *r: final_kernel(start, *r),
        grid=(count,),
        out_shape=jax.ShapeDtypeStruct((RU * LC, K), F32),
        in_specs=[
            SMEM, rows(CU), rows(CU), rows(3 * K), full((CU, 3 * K)), rows(K), full((K, K)),
            full((LR, K)),
        ] + [pl.BlockSpec(memory_space=pl.ANY)] * len(prev),
        out_specs=pl.BlockSpec((K * LC, K), lambda i: (i + start, 0)),
        input_output_aliases={8: 0} if prev else {},
        compiler_params=params(),
        cost_estimate=pl.CostEstimate(
            flops=1, bytes_accessed=6000000, transcendentals=0
        ),
        name="trailing_update",
    )(k, gown, grecv, la, lb, lpan, chol, damp, *prev)


def device(x, y, c, z):
    return ((x * NY + y) * NC + c) * NZ + z


def hops(along_x_core, d):
    pairs = []
    for x in range(NX):
        for y in range(NY):
            for c in range(NC):
                for z in range(NZ):
                    to = ((x + d) % NX, y) if c == along_x_core else (x, (y + d) % NY)
                    pairs.append((device(x, y, c, z), device(*to, c, z)))
    return pairs


def body(g_jets, layer_input_jets, speed, resid, point_index, damping, panel):
    q = lax.axis_index("row")
    k = panel[0]
    one = lambda v, d: lax.ppermute(v, AXES, hops(0, d))
    two = lambda v, d: lax.ppermute(v, AXES, hops(1, d))
    swap = lambda v: lax.ppermute(v, "core", [(0, 1), (1, 0)])
    zbit = lambda v, bit: v + lax.ppermute(v, "row", [(i, i ^ bit) for i in range(NZ)])
    bar = lax.optimization_barrier

    plus, minus, low, high, own = pack(
        panel,
        point_index.reshape(1, M),
        layer_input_jets.reshape(HR, POOL),
        g_jets.transpose(1, 0, 2).reshape(C * A, POOL),
        speed.reshape(2, M),
        resid.reshape(2, M),
    )
    dsel = lax.dynamic_index_in_dim(damping[:, 0, :], k // NZ, 0, keepdims=True)
    dsel = jnp.broadcast_to(jnp.where(k % NZ == q, dsel, 0.0), (8, K))
    accs = chunk([place(BLOCK0, 0, 0)], (plus, own), (), "chunk_own")
    dsel = zbit(zbit(zbit(dsel, 1), 2), 4)
    ap, am, rp, rm = one(plus, 1), one(minus, -1), one(low, 2), one(high, 2)
    ap, am, rp, rm, accs, dsel = bar((ap, am, rp, rm, accs, dsel))
    m1 = assemble(BLOCK0, BLOCK1, plus, own, ap)
    m2 = assemble(BLOCK2, BLOCK3, am, rp, rm)
    m1p, m1m, m2p, m2m = two(m1[0], 1), two(m1[1], -1), two(m2[0], 1), two(m2[1], -1)
    line = [place(BLOCK1, 0, -2), place(BLOCK2, 0, 1), place(BLOCK3, 0, 1)]
    accs = chunk(line, (ap, am, rp, rm), accs, "chunk_line")
    m1p, m1m, accs = bar((m1p, m1m, accs))
    n1 = BR + GC
    r1p, r1m = two(m1p[:n1], 1), two(m1m[:n1], -1)
    e1 = 2 * BR + GC
    near = received(0, e1) + received(1, e1)
    accs = chunk(near, (m1p, m1m), accs, "chunk_near1")
    m2p, m2m, accs = bar((m2p, m2m, accs))
    r2p, r2m = two(m2p[:n1], 1), two(m2m[:n1], -1)
    far = [received(0, BR)[0], received(1, BR)[0]]
    accs = chunk(far + received(2, e1) + received(3, e1), (r1p, r1m, m2p, m2m), accs, "chunk_far1")
    accs = chunk(far, (r2p, r2m), accs, "chunk_far2")
    gown, gsib, p, po, ps, dk = accs

    dk2, p, ps, gsib = bar((swap(dk), p, ps, gsib))
    chol, w, yz = cholesky(dk, dk2, dsel)
    pr, por, gr, w = bar((swap(p), swap(ps), swap(gsib), w))
    mine, lpan, la, lb = panel_solve(panel, p, pr, po, por, w, yz)
    slot = lax.broadcasted_iota(jnp.int32, (1, NZ, 1), 1)
    full = jnp.where(slot == q, mine[:, None, :], 0.0)
    parts = [full]
    for bits in (1, 2, 3):
        parts.append(lax.ppermute(parts[0], "row", [(i, i ^ bits) for i in range(NZ)]))
    full = parts[0] + parts[1] + parts[2] + parts[3]
    rest = (panel, gown, gr, la, lb, lpan, chol, damping[:, 0, :])
    fac = final(0, 6, *rest)
    full, fac = bar((full, fac))
    fac = final(6, 6, *rest, fac)
    full = zbit(full, 4)
    return fac.reshape(LR, 1, K, LC, 1, K), full.reshape(-1)


def solution(mesh):
    grid = Mesh(mesh.devices.reshape(NX, NY, NC, NZ), AXES)
    pts = ("x", "y", "core")
    in_specs = (
        P(None, None, pts),
        P(None, None, pts),
        P(pts),
        P(pts),
        P(pts),
        P(None, "row", None),
        P(),
    )
    out_specs = (P(None, "row", None, None, pts, None), P())
    return jax.shard_map(body, mesh=grid, in_specs=in_specs, out_specs=out_specs, check_vma=False)
```

```python
import jax
import jax.numpy as jnp
from jax import lax
from jax.experimental import pallas as pl
from jax.experimental.pallas import tpu as pltpu
from jax.sharding import Mesh, PartitionSpec as P

NX, NY, NC, NZ = 4, 4, 2, 8
A, K, C, POOL, M = 96, 128, 9, 256, 128
LR, LC = 12, 3
TOTAL = 4096
HR = C * K
BR = 1280
ROWG, KG, VR, RR = HR, HR + 108, HR + 117, HR + 118
GC = 64
HB = BR // 2
PR = BR + 4 * GC
FR = HB + 2 * GC
MR = 2 * BR + 3 * GC
RU, CU = LR * K, LC * K
JR = RU + 2 * CU + 2 * K
J_K, J_R = RU + 2 * CU, RU + 2 * CU + K
F32, BF16 = jnp.float32, jnp.bfloat16
AXES = ("x", "y", "core", "row")
HI = lax.Precision.HIGHEST
NT = (((1,), (1,)), ((), ()))
TN = (((0,), (0,)), ((), ()))
VMEM_LIMIT = 20 * 1024 * 1024
SMEM = pl.BlockSpec(memory_space=pltpu.SMEM)
VM = pl.BlockSpec(memory_space=pltpu.VMEM)
HBM = pl.BlockSpec(memory_space=pltpu.HBM)


def params():
    return pltpu.CompilerParams(vmem_limit_bytes=VMEM_LIMIT)


def pack_kernel(
    k_ref, idx_hbm, h_hbm, g_hbm, v_hbm, r_hbm, plus_ref, minus_ref, low_ref, high_ref, own_ref,
    gs, tail, cbuf, idx_ref, h_ref, g_ref, v_ref, r_ref, sem,
):
    copies = [
        pltpu.make_async_copy(src, dst, sem.at[i])
        for i, (src, dst) in enumerate(
            (
                (idx_hbm, idx_ref), (v_hbm, v_ref), (r_hbm, r_ref), (g_hbm, g_ref), (h_hbm, h_ref),
            )
        )
    ]
    for cp in copies:
        cp.start()
    x, y = lax.axis_index("x"), lax.axis_index("y")
    core, q = lax.axis_index("core"), lax.axis_index("row")
    k = k_ref[0]
    pool = lax.broadcasted_iota(jnp.int32, (POOL, M), 0)
    copies[0].wait()
    sel = (pool == idx_ref[...]).astype(F32).astype(BF16)
    for cp in copies[1:4]:
        cp.wait()
    for c in range(C):
        gs[c * A : (c + 1) * A, :] = jnp.dot(
            g_ref[c * A : (c + 1) * A, :], sel, preferred_element_type=F32
        )
    tail[...] = jnp.zeros_like(tail)
    for c in range(C):
        tail[c * LR : (c + 1) * LR, :] = gs[pl.ds(c * A + q, LR, stride=NZ), :]
        tail[108 + c : 109 + c, :] = gs[pl.ds(c * A + k, 1), :]
    for i, ref in enumerate((v_ref, r_ref)):
        low = jnp.dot(ref[...], sel[:M], preferred_element_type=F32)
        high = jnp.dot(ref[...], sel[M:], preferred_element_type=F32)
        tail[117 + i : 118 + i, :] = low[0:1] + high[1:2]
    val = tail[...].astype(BF16)
    plus_ref[HR:BR, :] = val
    minus_ref[HR:BR, :] = val
    high_ref[HR - HB : HB, :] = val
    cbuf[...] = jnp.zeros_like(cbuf)
    for dp in range(4):
        for dt in range(4):
            px = lax.rem(jnp.where(core == 0, x + dp, x + dt), NX)
            py = lax.rem(jnp.where(core == 0, y + dt, y + dp), NY)
            d = px * NY + py
            for c in range(C):
                for o in range(2):
                    cc = core if o == 0 else 1 - core
                    for lc in range(LC):
                        row = c * 6 + o * LC + lc
                        cbuf[row : row + 1, :] = gs[pl.ds(c * A + lc * 32 + 2 * d + cc, 1), :]
            val = cbuf[...].astype(BF16)
            if dp == 0:
                own_ref[dt * GC : (dt + 1) * GC, :] = val
            elif dp == 1:
                plus_ref[BR + dt * GC : BR + (1 + dt) * GC, :] = val
            elif dp == 3:
                minus_ref[BR + dt * GC : BR + (1 + dt) * GC, :] = val
            elif dt < 2:
                low_ref[HB + dt * GC : HB + (dt + 1) * GC, :] = val
            else:
                high_ref[HB + (dt - 2) * GC : HB + (dt - 1) * GC, :] = val
    copies[4].wait()
    for c in range(C):
        val = jnp.dot(h_ref[c * K : (c + 1) * K, :], sel, preferred_element_type=F32).astype(BF16)
        plus_ref[c * K : (c + 1) * K, :] = val
        minus_ref[c * K : (c + 1) * K, :] = val
        if c < 5:
            low_ref[c * K : (c + 1) * K, :] = val
        else:
            high_ref[c * K - HB : (c + 1) * K - HB, :] = val


def pack(k, idx, h, g, v, r):
    return pl.pallas_call(
        pack_kernel,
        out_shape=(
            jax.ShapeDtypeStruct((PR, M), BF16),
            jax.ShapeDtypeStruct((PR, M), BF16),
            jax.ShapeDtypeStruct((FR, M), BF16),
            jax.ShapeDtypeStruct((FR, M), BF16),
            jax.ShapeDtypeStruct((4 * GC, M), BF16),
        ),
        in_specs=[SMEM] + [HBM] * 5,
        out_specs=(VM,) * 5,
        scratch_shapes=[
            pltpu.VMEM((C * A, M), F32),
            pltpu.VMEM((128, M), F32),
            pltpu.VMEM((GC, M), F32),
            pltpu.VMEM((1, M), jnp.int32),
            pltpu.VMEM((HR, POOL), BF16),
            pltpu.VMEM((C * A, POOL), BF16),
            pltpu.VMEM((2, M), BF16),
            pltpu.VMEM((2, M), BF16),
            pltpu.SemaphoreType.DMA((5,)),
        ],
        compiler_params=pltpu.CompilerParams(vmem_limit_bytes=60 * 1024 * 1024),
        name="pack",
    )(k, idx, h, g, v, r)


def block(i, cols):
    return ([(i, 0, HB), (i, HB, HB)], cols)


def after(i, lo):
    return [(i, lo + e * GC) for e in range(4)]


BLOCK0 = block(0, after(1, 0))
BLOCK1 = block(2, after(2, BR))
BLOCK2 = block(0, after(0, BR))
BLOCK3 = (
    [(1, 0, HB), (2, 0, HB)],
    [(1, HB), (1, HB + GC), (2, HB), (2, HB + GC)],
)


def message(first, second, e):
    out, at = [], 0
    for i, lo, n in first[0]:
        out.append((i, lo, n, at))
        at += n
    out.append((*first[1][2], GC, at))
    at += GC
    for i, lo, n in second[0]:
        out.append((i, lo, n, at))
        at += n
    for blk in (first, second):
        out.append((*blk[1][e], GC, at))
        at += GC
    return out


def assemble_kernel(plans, n_in, *refs):
    ins, outs = refs[:n_in], refs[n_in:]
    for plan, out in zip(plans, outs):
        for src, lo, n, at in plan:
            out[at : at + n, :] = ins[src][lo : lo + n, :]


def assemble(first, second, *ins):
    plans = (message(first, second, 1), message(second, first, 3))
    return pl.pallas_call(
        lambda *r: assemble_kernel(plans, len(ins), *r),
        out_shape=(jax.ShapeDtypeStruct((MR, M), BF16),) * 2,
        in_specs=[VM] * len(ins),
        out_specs=(VM,) * 2,
        compiler_params=params(),
        name="assemble",
    )(*ins)


def coefs(rows, per, v):
    row = lax.broadcasted_iota(jnp.int32, (rows, M), 0)
    c = jnp.zeros((rows, M), jnp.int32)
    for i in range(1, C):
        c = c + (row >= per * i).astype(jnp.int32)
    base = jnp.where((c == 1) | (c == 4) | (c == 7), 2.0, 1.0)
    return jnp.where(c < 3, base, -base * v)


ACCS = ((RU, CU), (RU, CU), (RU, 2 * K), (CU, K), (CU, K), (K + 16, K))


def chunk_kernel(blocks, n_in, n_acc, *refs):
    arrs, ins = refs[:n_in], refs[n_in : n_in + n_acc]
    outs, (jac, wg) = refs[n_in + n_acc : -2], refs[-2:]
    for blk, (hs, tl, cl) in enumerate(blocks):
        tail = arrs[tl[0]][tl[1] : tl[1] + 128, :].astype(F32)
        v = tail[117:118, :]
        lanes = slice(blk * M, (blk + 1) * M)
        wg[blk, 0:108, :] = tail[0:108, :] * coefs(108, LR, v)
        wg[blk, 176:185, :] = tail[108:117, :] * coefs(C, 1, v)
        gc = arrs[cl[0]][cl[1] : cl[1] + GC, :].astype(F32)
        wg[blk, 112:176, :] = gc * coefs(GC, 6, v)
        jac[J_R:JR, lanes] = jnp.zeros((JR - J_R, M), BF16)
        first_row = lax.broadcasted_iota(jnp.int32, (16, M), 0) == 0
        jac[J_R : J_R + 16, lanes] = jnp.where(first_row, tail[118:119, :], 0.0).astype(BF16)

    for blk, (hs, tl, cl) in enumerate(blocks):
        lanes = slice(blk * M, (blk + 1) * M)

        def slab(t, carry, hs=hs, lanes=lanes, blk=blk):
            base = pl.multiple_of(t * 16, 16)
            h = [arrs[i][pl.ds(lo + base, 16), :].astype(F32) for i, lo in hs]

            def unit(rows, dst):
                acc = wg[blk, rows[0] : rows[0] + 1, :] * h[0]
                for c in range(1, C):
                    acc = acc + wg[blk, rows[c] : rows[c] + 1, :] * h[c]
                jac[pl.ds(dst + base, 16), lanes] = acc.astype(BF16)

            for u in range(LR):
                unit([c * LR + u for c in range(C)], u * K)
            for u in range(6):
                unit([112 + c * 6 + u for c in range(C)], RU + u * K)
            unit([176 + c for c in range(C)], J_K)
            return carry

        lax.fori_loop(0, K // 16, slab, 0)

    def acc(i, rows, cols, val):
        if n_acc:
            val = val + ins[i][rows, cols]
        outs[i][rows, cols] = val

    al = slice(None)
    pd = lax.dot_general(jac[RU : J_R + 16, :], jac[J_K:J_R, :], NT, preferred_element_type=F32)
    acc(3, al, al, pd[0:CU])
    acc(4, al, al, pd[CU : 2 * CU])
    acc(5, al, al, pd[2 * CU :])
    tile = 512
    for n in (3, 0, 1, 2):
        for m in range(RU // tile):
            rows = slice(m * tile, (m + 1) * tile)
            val = lax.dot_general(
                jac[rows, :], jac[RU + n * 256 : RU + (n + 1) * 256, :], NT,
                preferred_element_type=F32,
            )
            if n == 0:
                acc(0, rows, slice(0, 256), val)
            elif n == 1:
                acc(0, rows, slice(256, 384), val[:, :128])
                acc(1, rows, slice(0, 128), val[:, 128:])
            elif n == 2:
                acc(1, rows, slice(128, 384), val)
            else:
                acc(2, rows, al, val)


def chunk(blocks, arrs, accs, name):
    n = len(blocks)
    return pl.pallas_call(
        lambda *r: chunk_kernel(blocks, len(arrs), len(accs), *r),
        out_shape=tuple(jax.ShapeDtypeStruct(s, F32) for s in ACCS),
        in_specs=[VM] * (len(arrs) + len(accs)),
        out_specs=(VM,) * len(ACCS),
        scratch_shapes=[pltpu.VMEM((JR, n * M), BF16), pltpu.VMEM((n, 192, M), F32)],
        compiler_params=params(),
        cost_estimate=pl.CostEstimate(
            flops=n * 2 * JR * K * (RU + C), bytes_accessed=n * 4_000_000, transcendentals=0
        ),
        name=name,
    )(*arrs, *accs)


def place(blk, e, shift):
    hs, rows = [], [(i, lo + r) for i, lo, n in blk[0] for r in range(0, n, K)]
    rows = [(i + shift, lo) for i, lo in rows]
    i, lo = blk[1][e]
    return rows[:C], rows[C], (i + shift, lo)


def received(i, col):
    two = []
    for b in range(2):
        lo = b * (BR + GC)
        two.append(([(i, lo + c * K) for c in range(C)], (i, lo + HR), (i, col + b * GC)))
    return two


def chol_kernel(a_ref, b_ref, d_ref, chol_ref, w_ref, yz_ref, m_ref, u_ref):
    row = lax.broadcasted_iota(jnp.int32, (K, K), 0)
    col = lax.broadcasted_iota(jnp.int32, (K, K), 1)
    eye = row == col
    gram = (a_ref[0:K, :] + b_ref[0:K, :]) * (1.0 / TOTAL)
    m_ref[:, :K] = gram + jnp.where(eye, d_ref[0:1, :], 0.0)
    m_ref[:, K:] = jnp.where(eye, 1.0, 0.0)
    sub = lax.broadcasted_iota(jnp.int32, (8, K), 0)
    pick = lambda v, r: jnp.broadcast_to(v[r : r + 1, :], (8, v.shape[1]))
    for b in range(K // 8):
        lo = 8 * b
        p = m_ref[lo : lo + 8, :]
        left, right = p[:, :K], p[:, K:]
        cols = [jnp.broadcast_to(p[:, lo + c : lo + c + 1], (8, K)) for c in range(8)]
        scale = jnp.ones((8, K), F32)
        for r in range(8):
            rs = lax.rsqrt(pick(cols[r], r))
            mult = jnp.where(sub > r, cols[r] * (rs * rs), 0.0)
            for c in range(r + 1, 8):
                cols[c] = cols[c] - mult * pick(cols[c], r)
            scale = jnp.where(sub == r, rs, scale)
            left = left - mult * pick(left, r)
            right = right - mult * pick(right, r)
        p = jnp.concatenate([left * scale, right * scale], axis=1)
        u_ref[lo : lo + 8, :] = p
        if b < K // 8 - 1:
            ut = p[:, :K].T
            rows = [pick(p, r) for r in range(8)]
            for t in range(b + 1, K // 8):
                at = slice(8 * t, 8 * t + 8)
                acc = m_ref[at, :]
                for r in range(8):
                    acc = acc - jnp.broadcast_to(ut[at, r : r + 1], (8, 2 * K)) * rows[r]
                m_ref[at, :] = acc
    chol_ref[...] = jnp.where(col >= row, u_ref[:, :K], 0.0).T
    w = u_ref[:, K:]
    w_ref[...] = w
    g = (a_ref[K : K + 8, :] + b_ref[K : K + 8, :]) * (1.0 / TOTAL)
    y = lax.dot_general(g, w, NT, precision=HI, preferred_element_type=F32)
    z = lax.dot_general(y, w, (((1,), (0,)), ((), ())), precision=HI, preferred_element_type=F32)
    yz_ref[0:8, :] = y
    yz_ref[8:16, :] = z


def cholesky(dk, dk2, damp):
    return pl.pallas_call(
        chol_kernel,
        out_shape=(
            jax.ShapeDtypeStruct((K, K), F32),
            jax.ShapeDtypeStruct((K, K), F32),
            jax.ShapeDtypeStruct((16, K), F32),
        ),
        in_specs=[VM] * 3,
        out_specs=(VM,) * 3,
        scratch_shapes=[pltpu.VMEM((K, 2 * K), F32), pltpu.VMEM((K, 2 * K), F32)],
        compiler_params=params(),
        name="panel_factor",
    )(dk, dk2, damp)


def halves(v):
    hi = v.astype(BF16)
    return hi, (v - hi.astype(F32)).astype(BF16)


def panel_kernel(k_ref, p_ref, pr_ref, po_ref, por_ref, w_ref, yz_ref, dir_ref, lpan_ref, la_ref, lb_ref):
    q, k = lax.axis_index("row"), k_ref[0]
    inv = 1.0 / TOTAL
    w_hi, w_lo = halves(w_ref[...])
    wb = jnp.concatenate([w_hi, w_lo, w_hi], axis=1)
    sub = lax.broadcasted_iota(jnp.int32, (8, 2 * K), 0)
    lane = lax.broadcasted_iota(jnp.int32, (8, 2 * K), 1)
    z = yz_ref[8:9, :]
    z2 = jnp.concatenate([z, jnp.zeros_like(z)], axis=1)
    lhs = jnp.where(lane == K, 1.0, jnp.where(sub == 0, -z2, 0.0))

    def solve(p):
        hi, lo = halves(p)
        return lax.dot_general(
            jnp.concatenate([hi, hi, lo], axis=1), wb, NT, preferred_element_type=F32
        )

    for lr in range(LR):
        rows = slice(lr * K, (lr + 1) * K)
        pe = (p_ref[rows, :] + pr_ref[rows, :]) * inv
        d = lax.dot_general(lhs, pe, NT, precision=HI, preferred_element_type=F32)
        i = lr * NZ + q
        dir_ref[lr : lr + 1, :] = jnp.where(
            i == k, yz_ref[0:1, :], jnp.where(i > k, d[0:1, :], d[1:2, :])
        )
        lpan = solve(pe[:, :K])
        lpan_ref[rows, :] = lpan
        hi, lo = halves(lpan)
        la_ref[rows, :] = jnp.concatenate([hi, hi, lo], axis=1)
    hi, lo = halves(solve((po_ref[...] + por_ref[...]) * inv))
    lb_ref[...] = jnp.concatenate([hi, lo, hi], axis=1)


def panel_solve(k, p, pr, po, por, w, yz):
    return pl.pallas_call(
        panel_kernel,
        out_shape=(
            jax.ShapeDtypeStruct((LR, K), F32),
            jax.ShapeDtypeStruct((RU, K), F32),
            jax.ShapeDtypeStruct((RU, 3 * K), BF16),
            jax.ShapeDtypeStruct((CU, 3 * K), BF16),
        ),
        in_specs=[SMEM] + [VM] * 6,
        out_specs=(VM,) * 4,
        compiler_params=params(),
        name="panel_solve",
    )(k, p, pr, po, por, w, yz)


def final_kernel(start, k_ref, g_ref, gr_ref, la_ref, lb_ref, lpan_ref, chol_ref, damp_ref, *refs):
    out_ref = refs[-1]
    q, k = lax.axis_index("row"), k_ref[0]
    s = (lax.axis_index("x") * NY + lax.axis_index("y")) * NC + lax.axis_index("core")
    lr = start + pl.program_id(0)
    i = lr * NZ + q
    upd = lax.dot_general(la_ref[...], lb_ref[...], NT, preferred_element_type=F32)
    gram = (g_ref[...] + gr_ref[...]) * (1.0 / TOTAL)
    row = lax.broadcasted_iota(jnp.int32, (K, K), 0)
    col = lax.broadcasted_iota(jnp.int32, (K, K), 1)
    damp = damp_ref[pl.ds(lr, 1), :]
    for lc in range(LC):
        j = lc * (NX * NY * NC) + s
        gt = gram[:, lc * K : (lc + 1) * K] + jnp.where((row == col) & (i == j), damp, 0.0)
        val = jnp.where(
            (i > k) & (j > k),
            gt - upd[:, lc * K : (lc + 1) * K],
            jnp.where(
                (i > k) & (j == k),
                lpan_ref[...],
                jnp.where((i == k) & (j == k), chol_ref[...], gt),
            ),
        )
        out_ref[pl.ds(lc, K, stride=LC), :] = val


def final(start, count, k, gown, grecv, la, lb, lpan, chol, damp, *prev):
    full = lambda shape: pl.BlockSpec(shape, lambda i: (0,) * len(shape))
    rows = lambda width: pl.BlockSpec((K, width), lambda i: (i + start, 0))
    return pl.pallas_call(
        lambda *r: final_kernel(start, *r),
        grid=(count,),
        out_shape=jax.ShapeDtypeStruct((RU * LC, K), F32),
        in_specs=[
            SMEM, rows(CU), rows(CU), rows(3 * K), full((CU, 3 * K)), rows(K), full((K, K)),
            full((LR, K)),
        ] + [pl.BlockSpec(memory_space=pl.ANY)] * len(prev),
        out_specs=pl.BlockSpec((K * LC, K), lambda i: (i + start, 0)),
        input_output_aliases={8: 0} if prev else {},
        compiler_params=params(),
        cost_estimate=pl.CostEstimate(
            flops=1, bytes_accessed=6000000, transcendentals=0
        ),
        name="trailing_update",
    )(k, gown, grecv, la, lb, lpan, chol, damp, *prev)


def device(x, y, c, z):
    return ((x * NY + y) * NC + c) * NZ + z


def hops(along_x_core, d):
    pairs = []
    for x in range(NX):
        for y in range(NY):
            for c in range(NC):
                for z in range(NZ):
                    to = ((x + d) % NX, y) if c == along_x_core else (x, (y + d) % NY)
                    pairs.append((device(x, y, c, z), device(*to, c, z)))
    return pairs


def body(g_jets, layer_input_jets, speed, resid, point_index, damping, panel):
    q = lax.axis_index("row")
    k = panel[0]
    one = lambda v, d: lax.ppermute(v, AXES, hops(0, d))
    two = lambda v, d: lax.ppermute(v, AXES, hops(1, d))
    swap = lambda v: lax.ppermute(v, "core", [(0, 1), (1, 0)])
    zbit = lambda v, bit: v + lax.ppermute(v, "row", [(i, i ^ bit) for i in range(NZ)])
    bar = lax.optimization_barrier

    plus, minus, low, high, own = pack(
        panel,
        point_index.reshape(1, M),
        layer_input_jets.reshape(HR, POOL),
        g_jets.transpose(1, 0, 2).reshape(C * A, POOL),
        speed.reshape(2, M),
        resid.reshape(2, M),
    )
    dsel = lax.dynamic_index_in_dim(damping[:, 0, :], k // NZ, 0, keepdims=True)
    dsel = jnp.broadcast_to(jnp.where(k % NZ == q, dsel, 0.0), (8, K))
    accs = chunk([place(BLOCK0, 0, 0)], (plus, own), (), "chunk_own")
    ap, am, rp, rm = one(plus, 1), one(minus, -1), one(low, 2), one(high, 2)
    ap, am, rp, rm, accs, dsel = bar((ap, am, rp, rm, accs, zbit(zbit(dsel, 1), 2)))
    m1 = assemble(BLOCK0, BLOCK1, plus, own, ap)
    m2 = assemble(BLOCK2, BLOCK3, am, rp, rm)
    m1p, m1m, m2p, m2m = two(m1[0], 1), two(m1[1], -1), two(m2[0], 1), two(m2[1], -1)
    line = [place(BLOCK1, 0, -2), place(BLOCK2, 0, 1), place(BLOCK3, 0, 1)]
    accs = chunk(line, (ap, am, rp, rm), accs, "chunk_line")
    m1p, m1m, accs, dsel = bar((m1p, m1m, accs, zbit(dsel, 6)))
    n1 = BR + GC
    r1p, r1m = two(m1p[:n1], 1), two(m1m[:n1], -1)
    e1 = 2 * BR + GC
    near = received(0, e1) + received(1, e1)
    accs = chunk(near, (m1p, m1m), accs, "chunk_near1")
    m2p, m2m, accs = bar((m2p, m2m, accs))
    r2p, r2m = two(m2p[:n1], 1), two(m2m[:n1], -1)
    far = [received(0, BR)[0], received(1, BR)[0]]
    accs = chunk(far + received(2, e1) + received(3, e1), (r1p, r1m, m2p, m2m), accs, "chunk_far1")
    accs = chunk(far, (r2p, r2m), accs, "chunk_far2")
    gown, gsib, p, po, ps, dk = accs

    dk2, p, ps, gsib = bar((swap(dk), p, ps, gsib))
    chol, w, yz = cholesky(dk, dk2, dsel)
    pr, por, gr, w = bar((swap(p), swap(ps), swap(gsib), w))
    mine, lpan, la, lb = panel_solve(panel, p, pr, po, por, w, yz)
    slot = lax.broadcasted_iota(jnp.int32, (1, NZ, 1), 1)
    full = jnp.where(slot == q, mine[:, None, :], 0.0)
    parts = [full]
    for bits in (1, 2, 3):
        parts.append(lax.ppermute(parts[0], "row", [(i, i ^ bits) for i in range(NZ)]))
    full = parts[0] + parts[1] + parts[2] + parts[3]
    rest = (panel, gown, gr, la, lb, lpan, chol, damping[:, 0, :])
    fac = final(0, 7, *rest)
    full, fac = bar((full, fac))
    fac = final(7, 5, *rest, fac)
    full = zbit(full, 6)
    return fac.reshape(LR, 1, K, LC, 1, K), full.reshape(-1)


def solution(mesh):
    grid = Mesh(mesh.devices.reshape(NX, NY, NC, NZ), AXES)
    pts = ("x", "y", "core")
    in_specs = (
        P(None, None, pts),
        P(None, None, pts),
        P(pts),
        P(pts),
        P(pts),
        P(None, "row", None),
        P(),
    )
    out_specs = (P(None, "row", None, None, pts, None), P())
    return jax.shard_map(body, mesh=grid, in_specs=in_specs, out_specs=out_specs, check_vma=False)
```

```python
import jax
import jax.numpy as jnp
from jax import lax
from jax.experimental import pallas as pl
from jax.experimental.pallas import tpu as pltpu
from jax.sharding import Mesh, PartitionSpec as P

NX, NY, NC, NZ = 4, 4, 2, 8
A, K, C, POOL, M = 96, 128, 9, 256, 128
LR, LC = 12, 3
TOTAL = 4096
HR = C * K
BR = 1280
ROWG, KG, VR, RR = HR, HR + 108, HR + 117, HR + 118
GC = 64
HB = BR // 2
PR = BR + 4 * GC
FR = HB + 2 * GC
MR = 2 * BR + 3 * GC
RU, CU = LR * K, LC * K
JR = RU + 2 * CU + 2 * K
J_K, J_R = RU + 2 * CU, RU + 2 * CU + K
F32, BF16 = jnp.float32, jnp.bfloat16
AXES = ("x", "y", "core", "row")
HI = lax.Precision.HIGHEST
NT = (((1,), (1,)), ((), ()))
TN = (((0,), (0,)), ((), ()))
VMEM_LIMIT = 20 * 1024 * 1024
SMEM = pl.BlockSpec(memory_space=pltpu.SMEM)
VM = pl.BlockSpec(memory_space=pltpu.VMEM)
HBM = pl.BlockSpec(memory_space=pltpu.HBM)


def params():
    return pltpu.CompilerParams(vmem_limit_bytes=VMEM_LIMIT)


def pack_kernel(
    k_ref, idx_hbm, h_hbm, g_hbm, v_hbm, r_hbm, plus_ref, minus_ref, low_ref, high_ref, own_ref,
    gs, tail, cbuf, idx_ref, h_ref, g_ref, v_ref, r_ref, sem,
):
    copies = [
        pltpu.make_async_copy(src, dst, sem.at[i])
        for i, (src, dst) in enumerate(
            (
                (idx_hbm, idx_ref), (v_hbm, v_ref), (r_hbm, r_ref), (g_hbm, g_ref), (h_hbm, h_ref),
            )
        )
    ]
    for cp in copies:
        cp.start()
    x, y = lax.axis_index("x"), lax.axis_index("y")
    core, q = lax.axis_index("core"), lax.axis_index("row")
    k = k_ref[0]
    pool = lax.broadcasted_iota(jnp.int32, (POOL, M), 0)
    copies[0].wait()
    sel = (pool == idx_ref[...]).astype(F32).astype(BF16)
    for cp in copies[1:4]:
        cp.wait()
    for c in range(C):
        gs[c * A : (c + 1) * A, :] = jnp.dot(
            g_ref[c * A : (c + 1) * A, :], sel, preferred_element_type=F32
        )
    tail[...] = jnp.zeros_like(tail)
    for c in range(C):
        tail[c * LR : (c + 1) * LR, :] = gs[pl.ds(c * A + q, LR, stride=NZ), :]
        tail[108 + c : 109 + c, :] = gs[pl.ds(c * A + k, 1), :]
    for i, ref in enumerate((v_ref, r_ref)):
        low = jnp.dot(ref[...], sel[:M], preferred_element_type=F32)
        high = jnp.dot(ref[...], sel[M:], preferred_element_type=F32)
        tail[117 + i : 118 + i, :] = low[0:1] + high[1:2]
    val = tail[...].astype(BF16)
    plus_ref[HR:BR, :] = val
    minus_ref[HR:BR, :] = val
    high_ref[HR - HB : HB, :] = val
    cbuf[...] = jnp.zeros_like(cbuf)
    for dp in range(4):
        for dt in range(4):
            px = lax.rem(jnp.where(core == 0, x + dp, x + dt), NX)
            py = lax.rem(jnp.where(core == 0, y + dt, y + dp), NY)
            d = px * NY + py
            for c in range(C):
                for o in range(2):
                    cc = core if o == 0 else 1 - core
                    for lc in range(LC):
                        row = c * 6 + o * LC + lc
                        cbuf[row : row + 1, :] = gs[pl.ds(c * A + lc * 32 + 2 * d + cc, 1), :]
            val = cbuf[...].astype(BF16)
            if dp == 0:
                own_ref[dt * GC : (dt + 1) * GC, :] = val
            elif dp == 1:
                plus_ref[BR + dt * GC : BR + (1 + dt) * GC, :] = val
            elif dp == 3:
                minus_ref[BR + dt * GC : BR + (1 + dt) * GC, :] = val
            elif dt < 2:
                low_ref[HB + dt * GC : HB + (dt + 1) * GC, :] = val
            else:
                high_ref[HB + (dt - 2) * GC : HB + (dt - 1) * GC, :] = val
    copies[4].wait()
    for c in range(C):
        val = jnp.dot(h_ref[c * K : (c + 1) * K, :], sel, preferred_element_type=F32).astype(BF16)
        plus_ref[c * K : (c + 1) * K, :] = val
        minus_ref[c * K : (c + 1) * K, :] = val
        if c < 5:
            low_ref[c * K : (c + 1) * K, :] = val
        else:
            high_ref[c * K - HB : (c + 1) * K - HB, :] = val


def pack(k, idx, h, g, v, r):
    return pl.pallas_call(
        pack_kernel,
        out_shape=(
            jax.ShapeDtypeStruct((PR, M), BF16),
            jax.ShapeDtypeStruct((PR, M), BF16),
            jax.ShapeDtypeStruct((FR, M), BF16),
            jax.ShapeDtypeStruct((FR, M), BF16),
            jax.ShapeDtypeStruct((4 * GC, M), BF16),
        ),
        in_specs=[SMEM] + [HBM] * 5,
        out_specs=(VM,) * 5,
        scratch_shapes=[
            pltpu.VMEM((C * A, M), F32),
            pltpu.VMEM((128, M), F32),
            pltpu.VMEM((GC, M), F32),
            pltpu.VMEM((1, M), jnp.int32),
            pltpu.VMEM((HR, POOL), BF16),
            pltpu.VMEM((C * A, POOL), BF16),
            pltpu.VMEM((2, M), BF16),
            pltpu.VMEM((2, M), BF16),
            pltpu.SemaphoreType.DMA((5,)),
        ],
        compiler_params=pltpu.CompilerParams(vmem_limit_bytes=60 * 1024 * 1024),
        name="pack",
    )(k, idx, h, g, v, r)


def block(i, cols):
    return ([(i, 0, HB), (i, HB, HB)], cols)


def after(i, lo):
    return [(i, lo + e * GC) for e in range(4)]


BLOCK0 = block(0, after(1, 0))
BLOCK1 = block(2, after(2, BR))
BLOCK2 = block(0, after(0, BR))
BLOCK3 = (
    [(1, 0, HB), (2, 0, HB)],
    [(1, HB), (1, HB + GC), (2, HB), (2, HB + GC)],
)


def message(first, second, e):
    out, at = [], 0
    for i, lo, n in first[0]:
        out.append((i, lo, n, at))
        at += n
    out.append((*first[1][2], GC, at))
    at += GC
    for i, lo, n in second[0]:
        out.append((i, lo, n, at))
        at += n
    for blk in (first, second):
        out.append((*blk[1][e], GC, at))
        at += GC
    return out


def assemble_kernel(plans, n_in, *refs):
    ins, outs = refs[:n_in], refs[n_in:]
    for plan, out in zip(plans, outs):
        for src, lo, n, at in plan:
            out[at : at + n, :] = ins[src][lo : lo + n, :]


def assemble(first, second, *ins):
    plans = (message(first, second, 1), message(second, first, 3))
    return pl.pallas_call(
        lambda *r: assemble_kernel(plans, len(ins), *r),
        out_shape=(jax.ShapeDtypeStruct((MR, M), BF16),) * 2,
        in_specs=[VM] * len(ins),
        out_specs=(VM,) * 2,
        compiler_params=params(),
        name="assemble",
    )(*ins)


def coefs(rows, per, v):
    row = lax.broadcasted_iota(jnp.int32, (rows, M), 0)
    c = jnp.zeros((rows, M), jnp.int32)
    for i in range(1, C):
        c = c + (row >= per * i).astype(jnp.int32)
    base = jnp.where((c == 1) | (c == 4) | (c == 7), 2.0, 1.0)
    return jnp.where(c < 3, base, -base * v)


ACCS = ((RU, CU), (RU, CU), (RU, 2 * K), (CU, K), (CU, K), (K + 16, K))


def chunk_kernel(blocks, n_in, n_acc, *refs):
    arrs, ins = refs[:n_in], refs[n_in : n_in + n_acc]
    outs, (jac, wg) = refs[n_in + n_acc : -2], refs[-2:]
    for blk, (hs, tl, cl) in enumerate(blocks):
        tail = arrs[tl[0]][tl[1] : tl[1] + 128, :].astype(F32)
        v = tail[117:118, :]
        lanes = slice(blk * M, (blk + 1) * M)
        wg[blk, 0:108, :] = tail[0:108, :] * coefs(108, LR, v)
        wg[blk, 176:185, :] = tail[108:117, :] * coefs(C, 1, v)
        gc = arrs[cl[0]][cl[1] : cl[1] + GC, :].astype(F32)
        wg[blk, 112:176, :] = gc * coefs(GC, 6, v)
        jac[J_R:JR, lanes] = jnp.zeros((JR - J_R, M), BF16)
        first_row = lax.broadcasted_iota(jnp.int32, (16, M), 0) == 0
        jac[J_R : J_R + 16, lanes] = jnp.where(first_row, tail[118:119, :], 0.0).astype(BF16)

    for blk, (hs, tl, cl) in enumerate(blocks):
        lanes = slice(blk * M, (blk + 1) * M)

        def slab(t, carry, hs=hs, lanes=lanes, blk=blk):
            base = pl.multiple_of(t * 16, 16)
            h = [arrs[i][pl.ds(lo + base, 16), :].astype(F32) for i, lo in hs]

            def unit(rows, dst):
                acc = wg[blk, rows[0] : rows[0] + 1, :] * h[0]
                for c in range(1, C):
                    acc = acc + wg[blk, rows[c] : rows[c] + 1, :] * h[c]
                jac[pl.ds(dst + base, 16), lanes] = acc.astype(BF16)

            for u in range(LR):
                unit([c * LR + u for c in range(C)], u * K)
            for u in range(6):
                unit([112 + c * 6 + u for c in range(C)], RU + u * K)
            unit([176 + c for c in range(C)], J_K)
            return carry

        lax.fori_loop(0, K // 16, slab, 0)

    def acc(i, rows, cols, val):
        if n_acc:
            val = val + ins[i][rows, cols]
        outs[i][rows, cols] = val

    al = slice(None)
    pd = lax.dot_general(jac[RU : J_R + 16, :], jac[J_K:J_R, :], NT, preferred_element_type=F32)
    acc(3, al, al, pd[0:CU])
    acc(4, al, al, pd[CU : 2 * CU])
    acc(5, al, al, pd[2 * CU :])
    tile = 512
    for n in (3, 0, 1, 2):
        for m in range(RU // tile):
            rows = slice(m * tile, (m + 1) * tile)
            val = lax.dot_general(
                jac[rows, :], jac[RU + n * 256 : RU + (n + 1) * 256, :], NT,
                preferred_element_type=F32,
            )
            if n == 0:
                acc(0, rows, slice(0, 256), val)
            elif n == 1:
                acc(0, rows, slice(256, 384), val[:, :128])
                acc(1, rows, slice(0, 128), val[:, 128:])
            elif n == 2:
                acc(1, rows, slice(128, 384), val)
            else:
                acc(2, rows, al, val)


def chunk(blocks, arrs, accs, name):
    n = len(blocks)
    return pl.pallas_call(
        lambda *r: chunk_kernel(blocks, len(arrs), len(accs), *r),
        out_shape=tuple(jax.ShapeDtypeStruct(s, F32) for s in ACCS),
        in_specs=[VM] * (len(arrs) + len(accs)),
        out_specs=(VM,) * len(ACCS),
        scratch_shapes=[pltpu.VMEM((JR, n * M), BF16), pltpu.VMEM((n, 192, M), F32)],
        compiler_params=params(),
        cost_estimate=pl.CostEstimate(
            flops=n * 2 * JR * K * (RU + C), bytes_accessed=n * 4_000_000, transcendentals=0
        ),
        name=name,
    )(*arrs, *accs)


def place(blk, e, shift):
    hs, rows = [], [(i, lo + r) for i, lo, n in blk[0] for r in range(0, n, K)]
    rows = [(i + shift, lo) for i, lo in rows]
    i, lo = blk[1][e]
    return rows[:C], rows[C], (i + shift, lo)


def received(i, col):
    two = []
    for b in range(2):
        lo = b * (BR + GC)
        two.append(([(i, lo + c * K) for c in range(C)], (i, lo + HR), (i, col + b * GC)))
    return two


def chol_kernel(a_ref, b_ref, d_ref, chol_ref, w_ref, yz_ref, m_ref, u_ref):
    row = lax.broadcasted_iota(jnp.int32, (K, K), 0)
    col = lax.broadcasted_iota(jnp.int32, (K, K), 1)
    eye = row == col
    gram = (a_ref[0:K, :] + b_ref[0:K, :]) * (1.0 / TOTAL)
    m_ref[:, :K] = gram + jnp.where(eye, d_ref[0:1, :], 0.0)
    m_ref[:, K:] = jnp.where(eye, 1.0, 0.0)
    sub = lax.broadcasted_iota(jnp.int32, (8, K), 0)
    pick = lambda v, r: jnp.broadcast_to(v[r : r + 1, :], (8, v.shape[1]))
    for b in range(K // 8):
        lo = 8 * b
        p = m_ref[lo : lo + 8, :]
        left, right = p[:, :K], p[:, K:]
        cols = [jnp.broadcast_to(p[:, lo + c : lo + c + 1], (8, K)) for c in range(8)]
        scale = jnp.ones((8, K), F32)
        for r in range(8):
            rs = lax.rsqrt(pick(cols[r], r))
            mult = jnp.where(sub > r, cols[r] * (rs * rs), 0.0)
            for c in range(r + 1, 8):
                cols[c] = cols[c] - mult * pick(cols[c], r)
            scale = jnp.where(sub == r, rs, scale)
            left = left - mult * pick(left, r)
            right = right - mult * pick(right, r)
        p = jnp.concatenate([left * scale, right * scale], axis=1)
        u_ref[lo : lo + 8, :] = p
        if b < K // 8 - 1:
            ut = p[:, :K].T
            rows = [pick(p, r) for r in range(8)]
            for t in range(b + 1, K // 8):
                at = slice(8 * t, 8 * t + 8)
                acc = m_ref[at, :]
                for r in range(8):
                    acc = acc - jnp.broadcast_to(ut[at, r : r + 1], (8, 2 * K)) * rows[r]
                m_ref[at, :] = acc
    chol_ref[...] = jnp.where(col >= row, u_ref[:, :K], 0.0).T
    w = u_ref[:, K:]
    w_ref[...] = w
    g = (a_ref[K : K + 8, :] + b_ref[K : K + 8, :]) * (1.0 / TOTAL)
    y = lax.dot_general(g, w, NT, precision=HI, preferred_element_type=F32)
    z = lax.dot_general(y, w, (((1,), (0,)), ((), ())), precision=HI, preferred_element_type=F32)
    yz_ref[0:8, :] = y
    yz_ref[8:16, :] = z


def cholesky(dk, dk2, damp):
    return pl.pallas_call(
        chol_kernel,
        out_shape=(
            jax.ShapeDtypeStruct((K, K), F32),
            jax.ShapeDtypeStruct((K, K), F32),
            jax.ShapeDtypeStruct((16, K), F32),
        ),
        in_specs=[VM] * 3,
        out_specs=(VM,) * 3,
        scratch_shapes=[pltpu.VMEM((K, 2 * K), F32), pltpu.VMEM((K, 2 * K), F32)],
        compiler_params=params(),
        name="panel_factor",
    )(dk, dk2, damp)


def halves(v):
    hi = v.astype(BF16)
    return hi, (v - hi.astype(F32)).astype(BF16)


def panel_kernel(k_ref, p_ref, pr_ref, po_ref, por_ref, w_ref, yz_ref, dir_ref, lpan_ref, la_ref, lb_ref):
    q, k = lax.axis_index("row"), k_ref[0]
    inv = 1.0 / TOTAL
    w_hi, w_lo = halves(w_ref[...])
    wb = jnp.concatenate([w_hi, w_lo, w_hi], axis=1)
    sub = lax.broadcasted_iota(jnp.int32, (8, 2 * K), 0)
    lane = lax.broadcasted_iota(jnp.int32, (8, 2 * K), 1)
    z = yz_ref[8:9, :]
    z2 = jnp.concatenate([z, jnp.zeros_like(z)], axis=1)
    lhs = jnp.where(lane == K, 1.0, jnp.where(sub == 0, -z2, 0.0))

    def solve(p):
        hi, lo = halves(p)
        return lax.dot_general(
            jnp.concatenate([hi, hi, lo], axis=1), wb, NT, preferred_element_type=F32
        )

    for lr in range(LR):
        rows = slice(lr * K, (lr + 1) * K)
        pe = (p_ref[rows, :] + pr_ref[rows, :]) * inv
        d = lax.dot_general(lhs, pe, NT, precision=HI, preferred_element_type=F32)
        i = lr * NZ + q
        dir_ref[lr : lr + 1, :] = jnp.where(
            i == k, yz_ref[0:1, :], jnp.where(i > k, d[0:1, :], d[1:2, :])
        )
        lpan = solve(pe[:, :K])
        lpan_ref[rows, :] = lpan
        hi, lo = halves(lpan)
        la_ref[rows, :] = jnp.concatenate([hi, hi, lo], axis=1)
    hi, lo = halves(solve((po_ref[...] + por_ref[...]) * inv))
    lb_ref[...] = jnp.concatenate([hi, lo, hi], axis=1)


def panel_solve(k, p, pr, po, por, w, yz):
    return pl.pallas_call(
        panel_kernel,
        out_shape=(
            jax.ShapeDtypeStruct((LR, K), F32),
            jax.ShapeDtypeStruct((RU, K), F32),
            jax.ShapeDtypeStruct((RU, 3 * K), BF16),
            jax.ShapeDtypeStruct((CU, 3 * K), BF16),
        ),
        in_specs=[SMEM] + [VM] * 6,
        out_specs=(VM,) * 4,
        compiler_params=params(),
        name="panel_solve",
    )(k, p, pr, po, por, w, yz)


def final_kernel(start, k_ref, g_ref, gr_ref, la_ref, lb_ref, lpan_ref, chol_ref, damp_ref, *refs):
    out_ref = refs[-1]
    q, k = lax.axis_index("row"), k_ref[0]
    s = (lax.axis_index("x") * NY + lax.axis_index("y")) * NC + lax.axis_index("core")
    lr = start + pl.program_id(0)
    i = lr * NZ + q
    upd = lax.dot_general(la_ref[...], lb_ref[...], NT, preferred_element_type=F32)
    gram = (g_ref[...] + gr_ref[...]) * (1.0 / TOTAL)
    row = lax.broadcasted_iota(jnp.int32, (K, K), 0)
    col = lax.broadcasted_iota(jnp.int32, (K, K), 1)
    damp = damp_ref[pl.ds(lr, 1), :]
    for lc in range(LC):
        j = lc * (NX * NY * NC) + s
        gt = gram[:, lc * K : (lc + 1) * K] + jnp.where((row == col) & (i == j), damp, 0.0)
        val = jnp.where(
            (i > k) & (j > k),
            gt - upd[:, lc * K : (lc + 1) * K],
            jnp.where(
                (i > k) & (j == k),
                lpan_ref[...],
                jnp.where((i == k) & (j == k), chol_ref[...], gt),
            ),
        )
        out_ref[pl.ds(lc, K, stride=LC), :] = val


def final(start, count, k, gown, grecv, la, lb, lpan, chol, damp, *prev):
    full = lambda shape: pl.BlockSpec(shape, lambda i: (0,) * len(shape))
    rows = lambda width: pl.BlockSpec((K, width), lambda i: (i + start, 0))
    return pl.pallas_call(
        lambda *r: final_kernel(start, *r),
        grid=(count,),
        out_shape=jax.ShapeDtypeStruct((RU * LC, K), F32),
        in_specs=[
            SMEM, rows(CU), rows(CU), rows(3 * K), full((CU, 3 * K)), rows(K), full((K, K)),
            full((LR, K)),
        ] + [pl.BlockSpec(memory_space=pl.ANY)] * len(prev),
        out_specs=pl.BlockSpec((K * LC, K), lambda i: (i + start, 0)),
        input_output_aliases={8: 0} if prev else {},
        compiler_params=params(),
        cost_estimate=pl.CostEstimate(
            flops=1, bytes_accessed=6000000, transcendentals=0
        ),
        name="trailing_update",
    )(k, gown, grecv, la, lb, lpan, chol, damp, *prev)


def device(x, y, c, z):
    return ((x * NY + y) * NC + c) * NZ + z


def hops(along_x_core, d):
    pairs = []
    for x in range(NX):
        for y in range(NY):
            for c in range(NC):
                for z in range(NZ):
                    to = ((x + d) % NX, y) if c == along_x_core else (x, (y + d) % NY)
                    pairs.append((device(x, y, c, z), device(*to, c, z)))
    return pairs


def body(g_jets, layer_input_jets, speed, resid, point_index, damping, panel):
    q = lax.axis_index("row")
    k = panel[0]
    one = lambda v, d: lax.ppermute(v, AXES, hops(0, d))
    two = lambda v, d: lax.ppermute(v, AXES, hops(1, d))
    swap = lambda v: lax.ppermute(v, "core", [(0, 1), (1, 0)])
    zbit = lambda v, bit: v + lax.ppermute(v, "row", [(i, i ^ bit) for i in range(NZ)])
    bar = lax.optimization_barrier

    plus, minus, low, high, own = pack(
        panel,
        point_index.reshape(1, M),
        layer_input_jets.reshape(HR, POOL),
        g_jets.transpose(1, 0, 2).reshape(C * A, POOL),
        speed.reshape(2, M),
        resid.reshape(2, M),
    )
    dsel = lax.dynamic_index_in_dim(damping[:, 0, :], k // NZ, 0, keepdims=True)
    dsel = jnp.broadcast_to(jnp.where(k % NZ == q, dsel, 0.0), (8, K))
    accs = chunk([place(BLOCK0, 0, 0)], (plus, own), (), "chunk_own")
    ap, am, rp, rm = one(plus, 1), one(minus, -1), one(low, 2), one(high, 2)
    ap, am, rp, rm, accs, dsel = bar((ap, am, rp, rm, accs, zbit(zbit(dsel, 1), 2)))
    m1 = assemble(BLOCK0, BLOCK1, plus, own, ap)
    m2 = assemble(BLOCK2, BLOCK3, am, rp, rm)
    m1p, m1m, m2p, m2m = two(m1[0], 1), two(m1[1], -1), two(m2[0], 1), two(m2[1], -1)
    line = [place(BLOCK1, 0, -2), place(BLOCK2, 0, 1), place(BLOCK3, 0, 1)]
    accs = chunk(line, (ap, am, rp, rm), accs, "chunk_line")
    m1p, m1m, accs, dsel = bar((m1p, m1m, accs, dsel))
    n1 = BR + GC
    r1p, r1m = two(m1p[:n1], 1), two(m1m[:n1], -1)
    e1 = 2 * BR + GC
    near = received(0, e1) + received(1, e1)
    accs = chunk(near, (m1p, m1m), accs, "chunk_near1")
    m2p, m2m, accs, dsel = bar((m2p, m2m, accs, zbit(dsel, 6)))
    r2p, r2m = two(m2p[:n1], 1), two(m2m[:n1], -1)
    far = [received(0, BR)[0], received(1, BR)[0]]
    accs = chunk(far + received(2, e1) + received(3, e1), (r1p, r1m, m2p, m2m), accs, "chunk_far1")
    accs = chunk(far, (r2p, r2m), accs, "chunk_far2")
    gown, gsib, p, po, ps, dk = accs

    dk2, p, ps, gsib = bar((swap(dk), p, ps, gsib))
    chol, w, yz = cholesky(dk, dk2, dsel)
    pr, por, gr, w = bar((swap(p), swap(ps), swap(gsib), w))
    mine, lpan, la, lb = panel_solve(panel, p, pr, po, por, w, yz)
    slot = lax.broadcasted_iota(jnp.int32, (1, NZ, 1), 1)
    full = jnp.where(slot == q, mine[:, None, :], 0.0)
    parts = [full]
    for bits in (1, 2, 3):
        parts.append(lax.ppermute(parts[0], "row", [(i, i ^ bits) for i in range(NZ)]))
    full = parts[0] + parts[1] + parts[2] + parts[3]
    rest = (panel, gown, gr, la, lb, lpan, chol, damping[:, 0, :])
    fac = final(0, 7, *rest)
    full, fac = bar((full, fac))
    fac = final(7, 5, *rest, fac)
    full = zbit(full, 6)
    return fac.reshape(LR, 1, K, LC, 1, K), full.reshape(-1)


def solution(mesh):
    grid = Mesh(mesh.devices.reshape(NX, NY, NC, NZ), AXES)
    pts = ("x", "y", "core")
    in_specs = (
        P(None, None, pts),
        P(None, None, pts),
        P(pts),
        P(pts),
        P(pts),
        P(None, "row", None),
        P(),
    )
    out_specs = (P(None, "row", None, None, pts, None), P())
    return jax.shard_map(body, mesh=grid, in_specs=in_specs, out_specs=out_specs, check_vma=False)
```
